32 devices in a mesh: dp: 16 (over z, x, core), seq: 2 (over y).
Axes of the slice: x: 2, y: 2, z: 4, core: 2. Of those that a mesh axis runs over, the one named last changes fastest.
Arguments:
- tokens: bfloat16 [2, 16, 1024, 1024], P(None, 'dp', 'seq'), may hold values from -6 to 6
- lengths: int32 [2, 16], P(None, 'dp'), may hold values from 256 to 1024, as said below
- w_query: bfloat16 [1024, 1024], P(('dp', 'seq')), may hold values from -0.1875 to 0.1875
- w_key: bfloat16 [1024, 1024], P(('dp', 'seq')), may hold values from -0.1875 to 0.1875
- w_value: bfloat16 [1024, 1024], P(('dp', 'seq')), may hold values from -0.1875 to 0.1875
- w_out: bfloat16 [1024, 1024], P(('dp', 'seq')), may hold values from -3 to 3
- w_up: bfloat16 [1024, 4096], P(('dp', 'seq')), may hold values from -0.1875 to 0.1875
- w_down: bfloat16 [4096, 1024], P(('dp', 'seq')), may hold values from -0.09375 to 0.09375
- vectors: bfloat16 [8, 1024], P(None, ('dp', 'seq')), as said below
- up_bias: bfloat16 [4096], P(('dp', 'seq')), may hold values from -3 to 3
- cotangent: bfloat16 [2, 16, 1024, 1024], P(None, 'dp', 'seq'), may hold values from -6 to 6
Outputs:
- activations: bfloat16 [2, 16, 1024, 1024], P(None, 'dp', 'seq')
- grad_tokens: float32 [2, 16, 1024, 1024], P(None, 'dp', 'seq')
- grad_w_query: float32 [1024, 1024], P(('dp', 'seq'))
- grad_w_key: float32 [1024, 1024], P(('dp', 'seq'))
- grad_w_value: float32 [1024, 1024], P(('dp', 'seq'))
- grad_w_out: float32 [1024, 1024], P(('dp', 'seq'))
- grad_w_up: float32 [1024, 4096], P(('dp', 'seq'))
- grad_w_down: float32 [4096, 1024], P(('dp', 'seq'))
- grad_vectors: float32 [8, 1024], P(None, ('dp', 'seq'))
- grad_up_bias: float32 [4096], P(('dp', 'seq'))
The draws below stay inside these ranges and needn't reach their ends.
Inputs may be any that keep to these rules, and one draw needn't show every extreme that they name: `lengths`: in every sequence column one of the 2 micro-batches, which one drawn from the seed, has length 1024; the others are drawn evenly. `vectors`: rows 3 and 6 lie near 1, the others near 0.
All inputs are finite; a program needn't handle non-finite values.
Results may differ from the reference program's by a relative error of at most 0.014.
Values may be sent and summed in bfloat16 or wider, within the bound.
A program may use at most 320 MiB of HBM per device.

```python
import math
import jax
import jax.numpy as jnp
from jax import lax

D = 1024
H = 16
FF = 4096
HD = 64
MICRO = 2
LENGTH = 1024
SEQS_MB = 16


def draw_lengths(key, part):
    key = jax.random.fold_in(key, 7)
    first_key, second_key = jax.random.split(key)
    drawn = jax.random.randint(first_key, (MICRO, SEQS_MB), LENGTH // 4, LENGTH + 1)
    chosen = jax.random.randint(second_key, (1, SEQS_MB), 0, MICRO)
    rows_idx = jnp.arange(MICRO, dtype=jnp.int32)[:, None]
    return jnp.where(rows_idx == chosen, LENGTH, drawn).astype(jnp.int32)


def draw_vectors(key, part):
    key = jax.random.fold_in(key, 11)
    noise = jax.random.normal(key, (8, D), jnp.float32)
    rows_idx = jnp.arange(8)[:, None]
    gain_rows = (rows_idx == 3) | (rows_idx == 6)
    drawn = jnp.where(gain_rows, 1.0 + 0.1 * jnp.clip(noise, -3.0, 3.0), 0.3 * jnp.clip(noise, -4.0, 4.0))
    return drawn.astype(jnp.bfloat16)


def shard_levels(stream_key, extent, cuts, low, high):
    def one(axis_at, shards_of):
        steps = jax.random.uniform(jax.random.fold_in(jax.random.fold_in(stream_key, 6), axis_at), (shards_of,), jnp.float32, low / len(cuts), high / len(cuts))
        return jnp.repeat(jnp.exp(steps), extent[axis_at] // shards_of).reshape((-1,) + (1,) * (len(extent) - axis_at - 1))

    loudness = one(*cuts[0])
    for cut in cuts[1:]:
        loudness = loudness * one(*cut)
    return loudness


def normal_values(own_key, dims, width, most, cuts=(), kind=jnp.bfloat16):
    values = jax.random.normal(own_key, dims, jnp.float32) * width
    if len(cuts) > 0:
        values = shard_levels(own_key, dims, cuts, -0.22, 0.18) * values
    return jnp.clip(values, min=-most, max=most).astype(kind)


def setup_inputs(seed: int = 0) -> dict:
    key_of = jax.random.split(jax.random.key(seed), 12)
    tokens = normal_values(key_of[0], (MICRO, SEQS_MB, LENGTH, D), 1.0, 6.0, ((1, 16), (2, 2)))
    lengths = draw_lengths(jax.random.fold_in(key_of[11], 71), 0)
    w_query = normal_values(key_of[2], (D, D), D ** -0.5, 0.1875, ((0, 32),))
    w_key = normal_values(key_of[3], (D, D), D ** -0.5, 0.1875, ((0, 32),))
    w_value = normal_values(key_of[4], (D, D), D ** -0.5, 0.1875, ((0, 32),))
    w_out = normal_values(key_of[5], (D, D), 4 ** -0.5, 3.0, ((0, 32),))
    w_up = normal_values(key_of[6], (D, FF), D ** -0.5, 0.1875, ((0, 32),))
    w_down = normal_values(key_of[7], (FF, D), FF ** -0.5, 0.09375, ((0, 32),))
    vectors = draw_vectors(jax.random.fold_in(key_of[11], 71), 0)
    up_bias = normal_values(key_of[9], (FF,), 0.5, 3.0, ((0, 32),))
    cotangent = normal_values(key_of[10], (MICRO, SEQS_MB, LENGTH, D), 1.0, 6.0, ((1, 16), (2, 2)))
    return dict(tokens=tokens, lengths=lengths, w_query=w_query, w_key=w_key, w_value=w_value, w_out=w_out, w_up=w_up, w_down=w_down, vectors=vectors, up_bias=up_bias, cotangent=cotangent)


@jax.custom_vjp
def low(v):
    return lax.optimization_barrier(v.astype(jnp.bfloat16)).astype(jnp.float32)

@jax.custom_vjp
def low_back(v):
    return v

def low_keep(v):
    return (low(v), None)

def low_pass(kept, grad):
    return (grad,)

def back_keep(v):
    return (v, None)

def back_low(kept, grad):
    return (low(grad),)
low.defvjp(low_keep, low_pass)
low_back.defvjp(back_keep, back_low)
HIGHEST = lax.Precision.HIGHEST
EPSILON = 1e-05

def layer_norm(inputs, gain, shift):
    center = inputs - lax.optimization_barrier(jnp.mean(inputs, axis=-1, keepdims=True))
    return center * lax.rsqrt(lax.optimization_barrier(jnp.mean(center * center, axis=-1, keepdims=True)) + EPSILON) * gain + shift

def forward(inputs, params, length):
    w_query, w_key, w_value, w_out, w_up, w_down, vectors, up_bias = params
    positions = inputs.shape[0]
    valid = jnp.arange(positions, dtype=jnp.int32) < length
    query = low(low_back(jnp.dot(inputs, w_query, precision=HIGHEST) + vectors[0]))
    keys = low(low_back(jnp.dot(inputs, w_key, precision=HIGHEST)))
    vals = low(low_back(jnp.dot(inputs, w_value, precision=HIGHEST) + vectors[1]))
    head_keys = keys.reshape(positions, H, HD)
    head_vals = vals.reshape(positions, H, HD)
    block = min(512, positions)
    factor = 1.0 / math.sqrt(HD)

    def attend(query_block):
        scores = jnp.einsum('qhd,khd->hqk', query_block, head_keys, precision=HIGHEST) * factor
        scores = low_back(jnp.where(valid[None, None, :], scores, -1000000000.0))
        top = lax.optimization_barrier(jnp.max(scores, axis=-1, keepdims=True))
        total = top + jnp.log(lax.optimization_barrier(jnp.sum(jnp.exp(scores - top), axis=-1, keepdims=True)))
        probs = low(jnp.exp(scores - total))
        return jnp.einsum('hqk,khd->qhd', probs, head_vals, precision=HIGHEST)
    context = lax.map(jax.checkpoint(attend), query.reshape(positions // block, block, H, HD))
    context = low(low_back(context.reshape(positions, D)))
    attention = low_back(jnp.dot(context, w_out, precision=HIGHEST) + vectors[2])
    hidden = layer_norm(inputs + attention, vectors[3], vectors[4])
    upper = low_back(jnp.dot(low(hidden), w_up, precision=HIGHEST) + up_bias)
    active = low(jax.nn.gelu(upper))
    lowered = low_back(jnp.dot(active, w_down, precision=HIGHEST) + vectors[5])
    result = layer_norm(hidden + lowered, vectors[6], vectors[7])
    return result * valid[:, None].astype(jnp.float32)

def reference(tokens, lengths, w_query, w_key, w_value, w_out, w_up, w_down, vectors, up_bias, cotangent):
    params = tuple((weight.astype(jnp.float32) for weight in (w_query, w_key, w_value, w_out, w_up, w_down, vectors, up_bias)))
    inputs = tokens.reshape(MICRO * SEQS_MB, LENGTH, D).astype(jnp.float32)
    grads_in = cotangent.reshape(MICRO * SEQS_MB, LENGTH, D).astype(jnp.float32)
    limits = lengths.reshape(MICRO * SEQS_MB).astype(jnp.int32)

    def one_sequence(totals, item):
        rows_in, rows_grad, length = item

        def layer_fn(values_in, weights_in):
            return forward(values_in, weights_in, length)
        result, pull = jax.vjp(layer_fn, rows_in, params)
        grad_rows, grad_params = pull(rows_grad)
        totals = jax.tree.map(jnp.add, totals, grad_params)
        return (totals, (result.astype(jnp.bfloat16), grad_rows))
    start = jax.tree.map(jnp.zeros_like, params)
    totals, (outputs, grad_rows) = lax.scan(one_sequence, start, (inputs, grads_in, limits))
    out_shape = (MICRO, SEQS_MB, LENGTH, D)
    return (outputs.reshape(out_shape), grad_rows.reshape(out_shape), totals[0], totals[1], totals[2], totals[3], totals[4], totals[5], totals[6], totals[7])
```

```python
import functools
import math

import jax
import jax.numpy as jnp
from jax import lax
from jax.experimental import pallas as pl
from jax.experimental.pallas import tpu as pltpu
from jax.sharding import PartitionSpec as P

H = 16


EPSILON = 1e-05


def fetch_forward(w_query, w_key, w_value, w_out, w_up, w_down, vectors, up_bias):
    return (
        lax.all_gather(w_query, ("dp", "seq"), axis=0, tiled=True),
        lax.all_gather(w_key, ("dp", "seq"), axis=0, tiled=True),
        lax.all_gather(w_value, ("dp", "seq"), axis=0, tiled=True),
        lax.all_gather(w_out, ("dp", "seq"), axis=0, tiled=True),
        lax.all_gather(w_up, ("dp", "seq"), axis=0, tiled=True),
        lax.all_gather(w_down, ("dp", "seq"), axis=0, tiled=True),
        lax.all_gather(vectors, ("dp", "seq"), axis=1, tiled=True),
        lax.all_gather(up_bias, ("dp", "seq"), axis=0, tiled=True),
    )


def fetch_backward(w_query, w_key, w_value, w_out, w_up, w_down, vectors, up_bias):
    return (
        lax.all_gather(w_query, ("dp", "seq"), axis=0, tiled=True),
        lax.all_gather(w_key, ("dp", "seq"), axis=0, tiled=True),
        lax.all_gather(w_value, ("dp", "seq"), axis=0, tiled=True),
        lax.all_gather(w_out, ("dp", "seq"), axis=0, tiled=True),
        lax.all_gather(w_up, ("dp", "seq"), axis=0, tiled=True),
        lax.all_gather(w_down, ("dp", "seq"), axis=0, tiled=True),
        lax.all_gather(vectors, ("dp", "seq"), axis=1, tiled=True),
        lax.all_gather(up_bias, ("dp", "seq"), axis=0, tiled=True),
    )


def norm_forward(inputs, gain, shift):
    center = inputs - jnp.mean(inputs, axis=-1, keepdims=True)
    inverse = lax.rsqrt(jnp.mean(center * center, axis=-1, keepdims=True) + EPSILON)
    normed = center * inverse
    return (normed * gain + shift, normed, inverse)


def norm_backward(grad_out, normed, inverse, gain):
    grad_norm = grad_out * gain
    inner = (
        grad_norm
        - jnp.mean(grad_norm, axis=-1, keepdims=True)
        - normed * jnp.mean(grad_norm * normed, axis=-1, keepdims=True)
    )
    return (inner * inverse, jnp.sum(grad_out * normed, axis=0), jnp.sum(grad_out, axis=0))


def score_heads(query_heads, key_heads, key_valid, factor):
    scores = (
        jnp.einsum("qhd,khd->hqk", query_heads, key_heads, preferred_element_type=jnp.float32)
        * factor
    )
    return jnp.where(key_valid[None, None, :], scores, -1000000000.0)


def per_device(
    tokens, lengths, w_query, w_key, w_value, w_out, w_up, w_down, vectors, up_bias, cotangent
):
    micro = tokens.shape[0]
    slot = tokens.shape[2]
    width = tokens.shape[3]
    hidden_units = w_up.shape[1]
    heads = H
    head_dim = width // heads
    factor = 1.0 / math.sqrt(head_dim)
    positions = lax.axis_index("seq") * slot + jnp.arange(slot, dtype=jnp.int32)
    f32 = jnp.float32
    sums = [
        jnp.zeros((width, width), f32),
        jnp.zeros((width, width), f32),
        jnp.zeros((width, width), f32),
        jnp.zeros((width, width), f32),
        jnp.zeros((width, hidden_units), f32),
        jnp.zeros((hidden_units, width), f32),
        jnp.zeros((8, width), f32),
        jnp.zeros((hidden_units,), f32),
    ]
    outputs = []
    grad_list = []
    for micro_index in range(micro):
        full_query, full_key, full_value, full_out, full_up, full_down, full_vectors, full_bias = (
            fetch_forward(w_query, w_key, w_value, w_out, w_up, w_down, vectors, up_bias)
        )
        vec_f = full_vectors.astype(f32)
        bias_f = full_bias.astype(f32)
        rows_in = tokens[micro_index, 0]
        length = lengths[micro_index, 0]
        valid = (positions < length)[:, None].astype(f32)
        query = (jnp.dot(rows_in, full_query, preferred_element_type=f32) + vec_f[0]).astype(
            jnp.bfloat16
        )
        keys_own = jnp.dot(rows_in, full_key, preferred_element_type=f32).astype(jnp.bfloat16)
        vals_own = (jnp.dot(rows_in, full_value, preferred_element_type=f32) + vec_f[1]).astype(
            jnp.bfloat16
        )
        keys_all, vals_all = (
            lax.all_gather(keys_own, "seq", axis=0, tiled=True),
            lax.all_gather(vals_own, "seq", axis=0, tiled=True),
        )
        total_len = keys_all.shape[0]
        key_valid = jnp.arange(total_len, dtype=jnp.int32) < length
        query_heads = query.reshape(slot, heads, head_dim)
        key_heads = keys_all.reshape(total_len, heads, head_dim)
        val_heads = vals_all.reshape(total_len, heads, head_dim)
        scores = score_heads(query_heads, key_heads, key_valid, factor)
        top = jnp.max(scores, axis=-1, keepdims=True)
        log_total = top + jnp.log(jnp.sum(jnp.exp(scores - top), axis=-1, keepdims=True))
        probs = jnp.exp(scores - log_total).astype(jnp.bfloat16)
        context = (
            jnp.einsum("hqk,khd->qhd", probs, val_heads, preferred_element_type=f32)
            .reshape(slot, width)
            .astype(jnp.bfloat16)
        )
        attention = jnp.dot(context, full_out, preferred_element_type=f32) + vec_f[2]
        hidden, normed_one, inverse_one = norm_forward(
            rows_in.astype(f32) + attention, vec_f[3], vec_f[4]
        )
        hidden_low = hidden.astype(jnp.bfloat16)
        upper = jnp.dot(hidden_low, full_up, preferred_element_type=f32) + bias_f
        active = jax.nn.gelu(upper).astype(jnp.bfloat16)
        lowered = jnp.dot(active, full_down, preferred_element_type=f32) + vec_f[5]
        result, normed_two, inverse_two = norm_forward(hidden + lowered, vec_f[6], vec_f[7])
        outputs.append((result * valid).astype(jnp.bfloat16))
        full_query, full_key, full_value, full_out, full_up, full_down, full_vectors, full_bias = (
            fetch_backward(w_query, w_key, w_value, w_out, w_up, w_down, vectors, up_bias)
        )
        vec_f = full_vectors.astype(f32)
        grad_out = cotangent[micro_index, 0].astype(f32) * valid
        grad_res2, grad_gain2, grad_shift2 = norm_backward(
            grad_out, normed_two, inverse_two, vec_f[6]
        )
        grad_down = grad_res2.astype(jnp.bfloat16)
        grad_bias2 = jnp.sum(grad_down.astype(f32), axis=0)
        sums[5] = sums[5] + jnp.einsum("sf,sd->fd", active, grad_down, preferred_element_type=f32)
        grad_active = jnp.einsum("sd,fd->sf", grad_down, full_down, preferred_element_type=f32)
        gelu_pull = jax.vjp(jax.nn.gelu, upper)[1]
        grad_upper = gelu_pull(grad_active)[0].astype(jnp.bfloat16)
        sums[7] = sums[7] + jnp.sum(grad_upper.astype(f32), axis=0)
        sums[4] = sums[4] + jnp.einsum(
            "sd,sf->df", hidden_low, grad_upper, preferred_element_type=f32
        )
        grad_hidden = grad_res2 + jnp.einsum(
            "sf,df->sd", grad_upper, full_up, preferred_element_type=f32
        )
        grad_res1, grad_gain1, grad_shift1 = norm_backward(
            grad_hidden, normed_one, inverse_one, vec_f[3]
        )
        grad_att = grad_res1.astype(jnp.bfloat16)
        grad_bias_out = jnp.sum(grad_att.astype(f32), axis=0)
        sums[3] = sums[3] + jnp.einsum("sd,se->de", context, grad_att, preferred_element_type=f32)
        grad_context = jnp.einsum(
            "se,de->sd", grad_att, full_out, preferred_element_type=f32
        ).astype(jnp.bfloat16)
        grad_ctx_heads = grad_context.reshape(slot, heads, head_dim)
        scores_again = score_heads(query_heads, key_heads, key_valid, factor)
        full_probs = jnp.exp(scores_again - log_total)
        probs_low = full_probs.astype(jnp.bfloat16)
        grad_probs = jnp.einsum(
            "qhd,khd->hqk", grad_ctx_heads, val_heads, preferred_element_type=f32
        )
        grad_val_term = jnp.einsum(
            "hqk,qhd->khd", probs_low, grad_ctx_heads, preferred_element_type=f32
        )
        row_inner = jnp.sum(full_probs * grad_probs, axis=-1, keepdims=True)
        grad_scores = (full_probs * (grad_probs - row_inner)).astype(jnp.bfloat16)
        grad_query = (
            (
                jnp.einsum("hqk,khd->qhd", grad_scores, key_heads, preferred_element_type=f32)
                * factor
            )
            .reshape(slot, width)
            .astype(jnp.bfloat16)
        )
        grad_key_term = (
            jnp.einsum("hqk,qhd->khd", grad_scores, query_heads, preferred_element_type=f32)
            * factor
        )
        grad_keys, grad_vals = (
            lax.psum_scatter(
                grad_key_term.reshape(total_len, width).astype(jnp.bfloat16),
                "seq",
                scatter_dimension=0,
                tiled=True,
            ).astype(jnp.float32),
            lax.psum_scatter(
                grad_val_term.reshape(total_len, width).astype(jnp.bfloat16),
                "seq",
                scatter_dimension=0,
                tiled=True,
            ).astype(jnp.float32),
        )
        grad_keys = grad_keys.astype(jnp.bfloat16)
        grad_vals = grad_vals.astype(jnp.bfloat16)
        grad_bias_query = jnp.sum(grad_query.astype(f32), axis=0)
        grad_bias_vals = jnp.sum(grad_vals.astype(f32), axis=0)
        sums[0] = sums[0] + jnp.einsum("sd,se->de", rows_in, grad_query, preferred_element_type=f32)
        sums[1] = sums[1] + jnp.einsum("sd,se->de", rows_in, grad_keys, preferred_element_type=f32)
        sums[2] = sums[2] + jnp.einsum("sd,se->de", rows_in, grad_vals, preferred_element_type=f32)
        sums[6] = sums[6] + jnp.stack(
            [
                grad_bias_query,
                grad_bias_vals,
                grad_bias_out,
                grad_gain1,
                grad_shift1,
                grad_bias2,
                grad_gain2,
                grad_shift2,
            ]
        )
        grad_rows = grad_res1 + jnp.einsum(
            "se,de->sd", grad_query, full_query, preferred_element_type=f32
        )
        grad_rows = grad_rows + jnp.einsum(
            "se,de->sd", grad_keys, full_key, preferred_element_type=f32
        )
        grad_rows = grad_rows + jnp.einsum(
            "se,de->sd", grad_vals, full_value, preferred_element_type=f32
        )
        grad_list.append(grad_rows)
    shares = (
        lax.psum_scatter(sums[0], ("dp", "seq"), scatter_dimension=0, tiled=True),
        lax.psum_scatter(sums[1], ("dp", "seq"), scatter_dimension=0, tiled=True),
        lax.psum_scatter(sums[2], ("dp", "seq"), scatter_dimension=0, tiled=True),
        lax.psum_scatter(sums[3], ("dp", "seq"), scatter_dimension=0, tiled=True),
        lax.psum_scatter(sums[4], ("dp", "seq"), scatter_dimension=0, tiled=True),
        lax.psum_scatter(sums[5], ("dp", "seq"), scatter_dimension=0, tiled=True),
        lax.psum_scatter(sums[6], ("dp", "seq"), scatter_dimension=1, tiled=True),
        lax.psum_scatter(sums[7], ("dp", "seq"), scatter_dimension=0, tiled=True),
    )
    activations = jnp.stack(outputs)[:, None]
    grad_tokens = jnp.stack(grad_list)[:, None]
    return (
        activations,
        grad_tokens,
        shares[0],
        shares[1],
        shares[2],
        shares[3],
        shares[4],
        shares[5],
        shares[6],
        shares[7],
    )


MESH = pl.DeviceIdType.MESH
F32 = jnp.float32
BF16 = jnp.bfloat16
ANY = pl.ANY
VMEM = pltpu.VMEM
LOG2E = math.log2(math.e)
LIMIT = 58 * 1024 * 1024
GELU_C = math.sqrt(2.0 / math.pi)
GELU_A = 0.044715


def nt(a, b):
    return lax.dot_general(a, b, (((1,), (1,)), ((), ())), preferred_element_type=F32)


def nn(a, b):
    return lax.dot_general(a, b, (((1,), (0,)), ((), ())), preferred_element_type=F32)


def tn(a, b):
    return lax.dot_general(a, b, (((0,), (0,)), ((), ())), preferred_element_type=F32)


def place():
    dp = lax.axis_index("dp")
    return dp // 4, (dp // 2) % 2, dp % 2, lax.axis_index("seq")


def device(z, x, c, y):
    return (z * 4 + x * 2 + c, y)


def greet(z, x, c, y):
    barrier = pltpu.get_barrier_semaphore()
    partners = [device(z, x, 1 - c, y), device(z, 1 - x, c, y), device(z, x, c, 1 - y)]
    partners += [device((z + d) % 4, x, c, y) for d in (1, 2, 3)]
    for partner in partners:
        pl.semaphore_signal(barrier, inc=1, device_id=partner, device_id_type=MESH)
    pl.semaphore_wait(barrier, len(partners))


def gather_copies(ref, send, recv, order, phase, pos):
    z, x, c, y = pos
    every = slice(None)

    def copy(region, slot, target):
        return pltpu.make_async_remote_copy(
            src_ref=ref.at[region],
            dst_ref=ref.at[region],
            send_sem=send.at[slot],
            recv_sem=recv.at[slot],
            device_id=device(*target),
            device_id_type=MESH,
        )

    done = order[:phase]
    have = (
        every if "z" in done else z,
        every if "x" in done else x,
        every if "c" in done else c,
        every if "y" in done else y,
    )
    axis = order[phase]
    if axis == "z":
        return [copy(have, 2 + d, ((z + d) % 4, x, c, y)) for d in (1, 2, 3)]
    if axis == "x":
        return [copy(have, 0, (z, 1 - x, c, y))]
    if axis == "y":
        return [copy(have, 1, (z, x, c, 1 - y))]
    return [copy(have, 2, (z, x, 1 - c, y))]


ORDERS = ("yzxc", "zxyc")
PHASES = 4
SLOTS = 6


def gather_phase(ref, send, recv, phase, pos):
    for core, order in enumerate(ORDERS):

        @pl.when(pos[2] == core)
        def _():
            if phase > 0:
                for copy in gather_copies(ref, send, recv, order, phase - 1, pos):
                    copy.wait_recv()
            if phase < PHASES:
                for copy in gather_copies(ref, send, recv, order, phase, pos):
                    copy.start()


def gather_sent(ref, send, recv, pos):
    for core, order in enumerate(ORDERS):

        @pl.when(pos[2] == core)
        def _():
            for phase in range(PHASES):
                for copy in gather_copies(ref, send, recv, order, phase, pos):
                    copy.wait_send()


def gather_kernel(ws, sm, tok, cot, wf, sf, xs, ct, send, recv, own, tsend, trecv):
    pos = place()
    z, x, c, y = pos
    chunks = ws.shape[0]
    copies = [
        pltpu.make_async_copy(ws, wf.at[:, z, x, c, y], own.at[0]),
        pltpu.make_async_copy(sm, sf.at[z, x, c, y], own.at[1]),
        pltpu.make_async_copy(tok.at[y, 0], xs.at[0], own.at[2]),
        pltpu.make_async_copy(cot.at[y, 0], ct.at[0], own.at[3]),
    ]
    for copy in copies:
        copy.start()
    greet(*pos)
    swaps = []
    for index, (src, dst) in enumerate(((tok, xs), (cot, ct))):
        swaps.append(
            pltpu.make_async_remote_copy(
                src_ref=src.at[1 - y, 0],
                dst_ref=dst.at[1],
                send_sem=tsend.at[index],
                recv_sem=trecv.at[index],
                device_id=device(z, x, c, 1 - y),
                device_id_type=MESH,
            )
        )
    swaps[0].start()
    copies[0].wait()
    copies[1].wait()

    def chunk(index):
        return (wf.at[index], send.at[index], recv.at[index])

    small = (sf, send.at[chunks], recv.at[chunks])

    def step(t, carry):
        for phase in range(PHASES + 1):
            index = t - phase

            @pl.when((index >= 0) & (index < chunks))
            def _():
                gather_phase(*chunk(index), phase, pos)

            @pl.when(index == 0)
            def _():
                gather_phase(*small, phase, pos)

        return carry

    lax.fori_loop(0, chunks + PHASES, step, 0)
    swaps[1].start()
    for copy in copies[2:]:
        copy.wait()
    gather_sent(*small, pos)

    def finish(index, carry):
        gather_sent(*chunk(index), pos)
        return carry

    lax.fori_loop(0, chunks, finish, 0)
    for swap in swaps:
        swap.wait()


def gather(ws, sm, tok, cot):
    chunks, rows, width = ws.shape
    half = tok.shape[2]
    return pl.pallas_call(
        gather_kernel,
        out_shape=(
            jax.ShapeDtypeStruct((chunks, 4, 2, 2, 2, rows, width), BF16),
            jax.ShapeDtypeStruct((4, 2, 2, 2) + sm.shape, BF16),
            jax.ShapeDtypeStruct((2, half, width), BF16),
            jax.ShapeDtypeStruct((2, half, width), BF16),
        ),
        in_specs=[pl.BlockSpec(memory_space=ANY)] * 4,
        out_specs=[pl.BlockSpec(memory_space=ANY)] * 4,
        scratch_shapes=[
            pltpu.SemaphoreType.DMA((chunks + 1, SLOTS)),
            pltpu.SemaphoreType.DMA((chunks + 1, SLOTS)),
            pltpu.SemaphoreType.DMA((4,)),
            pltpu.SemaphoreType.DMA((2,)),
            pltpu.SemaphoreType.DMA((2,)),
        ],
        compiler_params=pltpu.CompilerParams(collective_id=0, has_side_effects=True),
        name="gather",
    )(ws, sm, tok, cot)


def scatter_copies(core, phase, grad, bufs, send, recv, pos):
    z, x, c, y = pos
    b0, b1, b2, b3 = bufs

    def remote(src, dst, slot, target):
        return pltpu.make_async_remote_copy(
            src_ref=src,
            dst_ref=dst,
            send_sem=send.at[slot],
            recv_sem=recv.at[slot],
            device_id=device(*target),
            device_id_type=MESH,
        )

    if phase == 0:
        return [remote(grad.at[:, :, 1 - c], b0, 2, (z, x, 1 - c, y))]
    if core == 0:
        if phase == 1:
            return [remote(b0.at[:, 1 - x], b1, 0, (z, 1 - x, c, y))]
        if phase == 2:
            return [
                remote(b1.at[(z + d) % 4], b2.at[pl.ds(2 * (d - 1), 2)], 2 + d, ((z + d) % 4, x, c, y))
                for d in (1, 2, 3)
            ]
        return [remote(b1.at[z, 1 - y], b3.at[0], 1, (z, x, c, 1 - y))]
    if phase == 1:
        return [remote(b0.at[:, :, 1 - y], b1, 1, (z, x, c, 1 - y))]
    if phase == 2:
        return [remote(b1.at[:, 1 - x], b2.at[pl.ds(0, 4)], 0, (z, 1 - x, c, y))]
    return [remote(b2.at[(z + d) % 4], b3.at[d - 1], 2 + d, ((z + d) % 4, x, c, y)) for d in (1, 2, 3)]


def scatter_add(core, phase, own, bufs, out, pos):
    z, x, c, y = pos
    b0, b1, b2, b3 = bufs

    def plus(dst, a, b):
        dst[...] = (a.astype(F32) + b.astype(F32)).astype(dst.dtype)

    if phase == 0:
        for zz in range(4):
            for xx in range(2):
                plus(b0.at[zz, xx], own[zz, xx], b0[zz, xx])
    elif phase == 1:
        for zz in range(4):
            plus(b1.at[zz], b0[zz, x] if core == 0 else b0[zz, :, y], b1[zz])
    elif core == 0:
        if phase == 2:
            total = b1[z].astype(F32)
            for d in range(3):
                total = total + b2[pl.ds(2 * d, 2)].astype(F32)
            b1[z] = total.astype(BF16)
        else:
            out[...] = b1[z, y].astype(F32) + b3[0].astype(F32)
    elif phase == 2:
        for zz in range(4):
            plus(b2.at[zz], b1[zz, x], b2[zz])
    else:
        total = b2[z].astype(F32)
        for d in range(3):
            total = total + b3[d].astype(F32)
        out[...] = total


def scatter_phase(phase, grad, own, own_sem, bufs, out, send, recv, pos):
    c = pos[2]
    mine = pltpu.make_async_copy(grad.at[:, :, c], own, own_sem)
    if phase == 0:
        mine.start()
    if phase == 1:
        mine.wait()
    for core in (0, 1):

        @pl.when(c == core)
        def _():
            if phase > 0:
                for copy in scatter_copies(core, phase - 1, grad, bufs, send, recv, pos):
                    copy.wait_recv()
                scatter_add(core, phase - 1, own, bufs, out, pos)
            if phase < PHASES:
                for copy in scatter_copies(core, phase, grad, bufs, send, recv, pos):
                    copy.start()


def scatter_sent(grad, bufs, send, recv, pos):
    for core in (0, 1):

        @pl.when(pos[2] == core)
        def _():
            for phase in range(PHASES):
                for copy in scatter_copies(core, phase, grad, bufs, send, recv, pos):
                    copy.wait_send()


def scatter_kernel(parts, *refs):
    count = len(parts) + 1
    grads, rows_ref = refs[:count], refs[count]
    outs, small_out, rows_out = refs[count + 1 : 2 * count], refs[2 * count], refs[2 * count + 1]
    bufs, small_bufs = refs[2 * count + 2 : 2 * count + 6], refs[2 * count + 6 : 2 * count + 10]
    own, small_own, send, recv, own_sem, swap_sem = refs[2 * count + 10 :]
    pos = place()
    z, x, c, y = pos
    greet(*pos)
    swap = pltpu.make_async_remote_copy(
        src_ref=rows_ref,
        dst_ref=rows_out,
        send_sem=swap_sem.at[0],
        recv_sem=swap_sem.at[1],
        device_id=device(z, x, c, 1 - y),
        device_id_type=MESH,
    )
    swap.start()
    total = sum(parts)
    small = total
    starts = [sum(parts[:k]) for k in range(len(parts))]

    def view(index):
        return [buf.at[index] for buf in bufs]

    def step(t, carry):
        for phase in range(PHASES + 1):
            index = t - phase
            for k, start in enumerate(starts):

                @pl.when((index >= start) & (index < start + parts[k]))
                def _():
                    scatter_phase(
                        phase,
                        grads[k].at[index - start],
                        own.at[index % 2],
                        own_sem.at[index % 2],
                        view(index),
                        outs[k].at[index - start],
                        send.at[index],
                        recv.at[index],
                        pos,
                    )

            @pl.when(index == total)
            def _():
                scatter_phase(
                    phase,
                    grads[-1],
                    small_own,
                    own_sem.at[2],
                    small_bufs,
                    small_out,
                    send.at[small],
                    recv.at[small],
                    pos,
                )

        return carry

    lax.fori_loop(0, total + 1 + PHASES, step, 0)
    scatter_sent(grads[-1], small_bufs, send.at[small], recv.at[small], pos)

    def finish(index, carry):
        scatter_sent(grads[0].at[0], view(index), send.at[index], recv.at[index], pos)
        return carry

    lax.fori_loop(0, total, finish, 0)
    swap.wait()


def scatter(grads, small, rows_back, cid):
    parts = [grad.shape[0] for grad in grads]
    rows, width = grads[0].shape[-2:]
    total = sum(parts)

    def buffers(lead, rows, width):
        return [
            VMEM(lead + (4, 2, 2, rows, width), BF16),
            VMEM(lead + (4, 2, rows, width), BF16),
            VMEM(lead + (6, rows, width), BF16),
            VMEM(lead + (3, rows, width), BF16),
        ]

    srows, swidth = small.shape[-2:]
    return pl.pallas_call(
        functools.partial(scatter_kernel, parts),
        out_shape=[jax.ShapeDtypeStruct((n, rows, width), F32) for n in parts]
        + [jax.ShapeDtypeStruct((srows, swidth), F32), jax.ShapeDtypeStruct(rows_back.shape, rows_back.dtype)],
        in_specs=[pl.BlockSpec(memory_space=ANY)] * (len(parts) + 2),
        out_specs=[pl.BlockSpec(memory_space=VMEM)] * (len(parts) + 1) + [pl.BlockSpec(memory_space=ANY)],
        scratch_shapes=buffers((total,), rows, width)
        + buffers((), srows, swidth)
        + [
            VMEM((2, 4, 2, 2, rows, width), BF16),
            VMEM((4, 2, 2, srows, swidth), BF16),
            pltpu.SemaphoreType.DMA((total + 1, SLOTS)),
            pltpu.SemaphoreType.DMA((total + 1, SLOTS)),
            pltpu.SemaphoreType.DMA((3,)),
            pltpu.SemaphoreType.DMA((2,)),
        ],
        compiler_params=pltpu.CompilerParams(collective_id=cid, has_side_effects=True, vmem_limit_bytes=LIMIT),
        name="scatter",
    )(*grads, small, rows_back)


def lanes(shape):
    return lax.broadcasted_iota(jnp.int32, shape, len(shape) - 1)


def attend_kernel(xs, wf, sf, kaug, qs, ks, vs, ctx, aug, res, vec, wbuf, wsem):
    rows, width = xs.shape
    block = 256
    loads = [pltpu.make_async_copy(wf.at[i], wbuf.at[i % 2], wsem.at[i % 2]) for i in range(4)]
    loads[0].start()
    for g in range(8):
        tile = sf[4 * g].astype(F32)
        for s in range(1, 4):
            tile = tile + sf[4 * g + s].astype(F32)
        vec[0:8, 128 * g : 128 * g + 128] = tile[0:8]
    for r in range(4):
        for g in range(8):
            vec[8 + r : 9 + r, 128 * g : 128 * g + 128] = sf[8 * r + g].astype(F32)[8:9]
    for i, dst in enumerate((qs, ks, vs)):
        loads[i].wait()
        loads[i + 1].start()

        def project(b, carry):
            sl = pl.ds(pl.multiple_of(b * block, block), block)
            out = nn(xs[sl, :], wbuf[i % 2])
            if i == 0:
                out = (out + vec[0:1, :]) * (LOG2E / 8.0)
            elif i == 2:
                out = out + vec[1:2, :]
            dst[sl, :] = out.astype(BF16)
            return carry

        lax.fori_loop(0, rows // block, project, 0)

    low1 = (lanes((1, 128)) < 64).astype(F32).astype(BF16)
    high1 = (lanes((1, 128)) >= 64).astype(F32).astype(BF16)
    ones1 = (lanes((1, 128)) % 64 == 0).astype(F32).astype(BF16)
    qlane = lanes((block, 128))
    sixty = qlane % 64

    def pair(hp, carry):
        cols = pl.ds(pl.multiple_of(hp * 128, 128), 128)
        k2 = ks[:, cols]
        v2 = vs[:, cols]
        ka = k2 * low1 + kaug[...] * high1
        kb = k2 * high1 + kaug[...] * low1

        def query_block(b, carry):
            sl = pl.ds(pl.multiple_of(b * block, block), block)
            q2 = qs[sl, cols]
            parts = []
            for mine, other, kk in ((low1, high1, ka), (high1, low1, kb)):
                s = nt(q2 * mine + ones1 * other, kk)
                top = jnp.max(s, axis=1, keepdims=True)
                e = jnp.exp2(s - top)
                total = jnp.sum(e, axis=1, keepdims=True)
                o = nn(e.astype(BF16), v2)
                parts.append((o / total, -(top + jnp.log2(total))))
            low = qlane < 64
            ctx[sl, cols] = jnp.where(low, parts[0][0], parts[1][0]).astype(BF16)
            neg = jnp.where(low, parts[1][1], parts[0][1])
            hi = neg.astype(BF16).astype(F32)
            mid = (neg - hi).astype(BF16).astype(F32)
            lo = neg - hi - mid
            aug[hp, sl, :] = jnp.where(
                sixty == 0,
                1.0,
                jnp.where(sixty == 1, hi, jnp.where(sixty == 2, mid, jnp.where(sixty == 3, lo, 0.0))),
            ).astype(BF16)
            return carry

        lax.fori_loop(0, rows // block, query_block, 0)
        return carry

    lax.fori_loop(0, width // 128, pair, 0)
    loads[3].wait()

    def project_out(b, carry):
        sl = pl.ds(pl.multiple_of(b * block, block), block)
        out = nn(ctx[sl, :], wbuf[1])
        res[sl, :] = xs[sl, :].astype(F32) + (out + vec[2:3, :])
        return carry

    lax.fori_loop(0, rows // block, project_out, 0)


def attend(xs, wf, sf, kaug):
    rows, width = xs.shape
    low = jax.ShapeDtypeStruct((rows, width), BF16)
    return pl.pallas_call(
        attend_kernel,
        out_shape=(
            low,
            low,
            low,
            low,
            jax.ShapeDtypeStruct((width // 128, rows, 128), BF16),
            jax.ShapeDtypeStruct((rows, width), F32),
            jax.ShapeDtypeStruct((16, width), F32),
        ),
        in_specs=[
            pl.BlockSpec(memory_space=VMEM),
            pl.BlockSpec(memory_space=ANY),
            pl.BlockSpec(memory_space=VMEM),
            pl.BlockSpec(memory_space=VMEM),
        ],
        out_specs=[pl.BlockSpec(memory_space=VMEM)] * 7,
        scratch_shapes=[VMEM((2, width, width), BF16), pltpu.SemaphoreType.DMA((2,))],
        compiler_params=pltpu.CompilerParams(vmem_limit_bytes=LIMIT),
        cost_estimate=pl.CostEstimate(flops=2 * 6 * rows * width * width, bytes_accessed=30 << 20, transcendentals=1 << 24),
        name="attend",
    )(xs, wf, sf, kaug)


def feed_kernel(res, ct, valid, vec, wu, wd, act, gres1, gwu, gwd, rows_out, bias_out, hid, acc, low, gdn, actv, slope):
    step = pl.program_id(0)
    chunks = pl.num_programs(0) // 2
    rows, width = res.shape
    block = 256
    nb = rows // block
    wide = wu.shape[1]
    last = step == 2 * chunks - 1
    down = jnp.concatenate([wd[jj, s] for s in range(4) for jj in range(4)], axis=0)

    def blocks(body):
        def run(b, carry):
            body(b, pl.ds(pl.multiple_of(b * block, block), block))
            return carry

        lax.fori_loop(0, nb, run, 0)

    def norm(v):
        center = v - jnp.mean(v, axis=-1, keepdims=True)
        inverse = lax.rsqrt(jnp.mean(center * center, axis=-1, keepdims=True) + 1e-05)
        return center * inverse, inverse

    def norm_back(g, normed, inverse, gain):
        gn = g * gain
        inner = gn - jnp.mean(gn, axis=-1, keepdims=True) - normed * jnp.mean(gn * normed, axis=-1, keepdims=True)
        return inner * inverse

    def rowsum(v):
        return jnp.sum(v, axis=0, keepdims=True)

    @pl.when(step == 0)
    def _():
        rows_out[...] = jnp.zeros_like(rows_out)

        def body(b, sl):
            normed, _ = norm(res[sl, :])
            hidden = normed * vec[3:4, :] + vec[4:5, :]
            hid[sl, :] = hidden
            low[sl, :] = hidden.astype(BF16)

        blocks(body)

    @pl.when(step < chunks)
    def _():
        bias = vec[pl.ds(8 + step // 2, 1), pl.ds(pl.multiple_of((step % 2) * wide, wide), wide)]

        def body(b, sl):
            up = nn(low[sl, :], wu[...]) + bias
            square = up * up
            t = jnp.tanh(up * (GELU_C + (GELU_C * GELU_A) * square))
            half = 0.5 * up
            a = (half + half * t).astype(BF16)
            d = 0.5 + 0.5 * t + half * (1.0 - t * t) * (GELU_C + (3.0 * GELU_C * GELU_A) * square)
            actv[step, sl, :] = a
            slope[step, sl, :] = d.astype(BF16)
            part = nn(a, down)

            @pl.when(step == 0)
            def _():
                acc[sl, :] = part

            @pl.when(step > 0)
            def _():
                acc[sl, :] += part

        blocks(body)

    @pl.when(step == chunks - 1)
    def _():
        def body(b, sl):
            normed, inverse = norm(hid[sl, :] + (acc[sl, :] + vec[5:6, :]))
            ok = valid[sl, 0:1]
            act[sl, :] = ((normed * vec[6:7, :] + vec[7:8, :]) * ok).astype(BF16)
            g = ct[sl, :].astype(F32) * ok
            back = norm_back(g, normed, inverse, vec[6:7, :])
            acc[sl, :] = back
            gd = back.astype(BF16)
            gdn[sl, :] = gd
            rows_out[6:7, :] += rowsum(g * normed)
            rows_out[7:8, :] += rowsum(g)
            rows_out[5:6, :] += rowsum(gd.astype(F32))

        blocks(body)

    @pl.when(step >= chunks)
    def _():
        i = step - chunks
        bias_out[...] = jnp.zeros_like(bias_out)

        def body(b, sl):
            ga = nt(gdn[sl, :], down)
            gu = (slope[i, sl, :].astype(F32) * ga).astype(BF16)
            slope[i, sl, :] = gu
            bias_out[0:1, :] += rowsum(gu.astype(F32))
            acc[sl, :] += nt(gu, wu[...])

        blocks(body)
        for q in range(wide // 128):
            part = tn(actv[i, :, 128 * q : 128 * q + 128], gdn[...]).astype(BF16)
            for jj in range(4):
                gwd[jj, q] = part[32 * jj : 32 * jj + 32]
        for q in range(width // 256):
            gwu[0, 256 * q : 256 * q + 256, :] = tn(low[:, 256 * q : 256 * q + 256], slope[i]).astype(BF16)

    @pl.when(last)
    def _():
        def body(b, sl):
            normed, inverse = norm(res[sl, :])
            g = acc[sl, :]
            back = norm_back(g, normed, inverse, vec[3:4, :])
            gres1[sl, :] = back
            rows_out[3:4, :] += rowsum(g * normed)
            rows_out[4:5, :] += rowsum(g)
            rows_out[2:3, :] += rowsum(back.astype(BF16).astype(F32))

        blocks(body)


def feed(res, ct, valid, vec, wf):
    rows, width = res.shape
    wide = 512
    chunks = 4 * width // wide
    up_w = wf.reshape(12, width, width)
    down_w = wf.reshape(12, 32, 32, width)

    def whole(shape):
        return pl.BlockSpec(shape, lambda i: (0,) * len(shape), pipeline_mode=pl.Buffered(1))

    def second(i):
        return jnp.maximum(i - chunks, 0)

    return pl.pallas_call(
        feed_kernel,
        grid=(2 * chunks,),
        out_shape=(
            jax.ShapeDtypeStruct((rows, width), BF16),
            jax.ShapeDtypeStruct((rows, width), F32),
            jax.ShapeDtypeStruct((4, width, width), BF16),
            jax.ShapeDtypeStruct((4, 32, 32, width), BF16),
            jax.ShapeDtypeStruct((8, width), F32),
            jax.ShapeDtypeStruct((chunks, 8, wide), F32),
        ),
        in_specs=[
            whole((rows, width)),
            whole((rows, width)),
            whole((rows, 128)),
            whole((16, width)),
            pl.BlockSpec((None, width, wide), lambda i: (4 + (i % chunks) // 2, 0, i % 2)),
            pl.BlockSpec((4, 4, 32, width), lambda i: (2, i % chunks, 0, 0)),
        ],
        out_specs=[
            whole((rows, width)),
            whole((rows, width)),
            pl.BlockSpec((1, width, wide), lambda i: (second(i) // 2, 0, second(i) % 2)),
            pl.BlockSpec((4, 4, 32, width), lambda i: (0, second(i), 0, 0)),
            whole((8, width)),
            pl.BlockSpec((None, 8, wide), lambda i: (second(i), 0, 0)),
        ],
        scratch_shapes=[
            VMEM((rows, width), F32),
            VMEM((rows, width), F32),
            VMEM((rows, width), BF16),
            VMEM((rows, width), BF16),
            VMEM((chunks, rows, wide), BF16),
            VMEM((chunks, rows, wide), BF16),
        ],
        compiler_params=pltpu.CompilerParams(vmem_limit_bytes=LIMIT, dimension_semantics=("arbitrary",)),
        cost_estimate=pl.CostEstimate(flops=2 * 24 * rows * width * width, bytes_accessed=80 << 20, transcendentals=1 << 22),
        name="feed",
    )(res, ct, valid, vec, up_w, down_w)


def retreat_kernel(gres1, xs, wf, qs, ks, vs, ctx, aug, kaug, gtok, dw, rows_out, gat, gcx, gqs, gks, gvs, wbuf, dbuf, wsem, dsem):
    rows, width = xs.shape
    block = 256
    nb = rows // block
    order = (3, 0, 1, 2)
    loads = [pltpu.make_async_copy(wf.at[order[i]], wbuf.at[i % 2], wsem.at[i % 2]) for i in range(4)]
    stores = [pltpu.make_async_copy(dbuf.at[i % 2], dw.at[order[i]], dsem.at[i % 2]) for i in range(4)]
    loads[0].start()
    rows_out[...] = jnp.zeros_like(rows_out)

    def blocks(body):
        def run(b, carry):
            body(pl.ds(pl.multiple_of(b * block, block), block))
            return carry

        lax.fori_loop(0, nb, run, 0)

    def weight_grad(slot, left, right):
        def run(b, carry):
            sl = pl.ds(pl.multiple_of(b * block, block), block)
            dbuf[slot, sl, :] = tn(left[:, sl], right[...]).astype(BF16)
            return carry

        lax.fori_loop(0, width // block, run, 0)

    def low_rows(sl):
        gat[sl, :] = gres1[sl, :].astype(BF16)

    blocks(low_rows)
    loads[0].wait()
    loads[1].start()

    def context_rows(sl):
        gcx[sl, :] = nt(gat[sl, :], wbuf[0]).astype(BF16)

    blocks(context_rows)
    weight_grad(0, ctx, gat)
    stores[0].start()

    low1 = (lanes((1, 128)) < 64).astype(F32).astype(BF16)
    high1 = (lanes((1, 128)) >= 64).astype(F32).astype(BF16)
    ones1 = (lanes((1, 128)) % 64 < 2).astype(F32).astype(BF16)
    alane = lanes((rows, 128))
    low = alane < 64
    sixty = alane % 64

    def pair(hp, carry):
        cols = pl.ds(pl.multiple_of(hp * 128, 128), 128)
        q2 = qs[:, cols]
        g2 = gcx[:, cols]
        au = aug[hp]
        prod = g2.astype(F32) * ctx[:, cols].astype(F32)
        da = -jnp.sum(jnp.where(low, prod, 0.0), axis=1, keepdims=True)
        db = -jnp.sum(jnp.where(low, 0.0, prod), axis=1, keepdims=True)
        neg = jnp.where(low, db, da)
        hi = neg.astype(BF16).astype(F32)
        daug = jnp.where(sixty == 0, hi, jnp.where(sixty == 1, neg - hi, 0.0)).astype(BF16)
        qa = (q2 * low1 + au * high1, q2 * high1 + au * low1)
        ga = (g2 * low1 + daug * high1, g2 * high1 + daug * low1)
        gq = []
        for head in range(2):
            mine, other = (low1, high1) if head == 0 else (high1, low1)
            total = jnp.zeros((128, rows), F32)
            for b in range(nb):
                sl = slice(b * block, (b + 1) * block)
                k2 = ks[sl, cols]
                v2 = vs[sl, cols]
                s = nt(k2 * mine + kaug[sl, :] * other, qa[head])
                p = jnp.exp2(s)
                gp = nt(v2 * mine + ones1 * other, ga[head])
                ds = (p * gp).astype(BF16)
                gv = nn(p.astype(BF16), g2).astype(BF16)
                gk = (nn(ds, q2) * (1.0 / LOG2E)).astype(BF16)
                total = total + tn(k2, ds)
                if head == 0:
                    gvs[sl, cols] = gv
                    gks[sl, cols] = gk
                else:
                    gvs[sl, cols] = gvs[sl, cols] * low1 + gv * high1
                    gks[sl, cols] = gks[sl, cols] * low1 + gk * high1
            gq.append(total)
        both = jnp.concatenate([gq[0][0:64], gq[1][64:128]], axis=0) * 0.125
        gqs[:, cols] = both.T.astype(BF16)
        return carry

    lax.fori_loop(0, width // 128, pair, 0)

    for i, (left, base) in enumerate(((gqs, gres1), (gks, gtok), (gvs, gtok)), start=1):
        loads[i].wait()
        if i < 3:
            loads[i + 1].start()

        def token_rows(sl):
            gtok[sl, :] = base[sl, :] + nt(left[sl, :], wbuf[i % 2])
            if i != 2:
                row = 0 if i == 1 else 1
                rows_out[row : row + 1, :] += jnp.sum(left[sl, :].astype(F32), axis=0, keepdims=True)

        blocks(token_rows)
        if i >= 2:
            stores[i - 2].wait()
        weight_grad(i % 2, xs, left)
        stores[i].start()
    stores[2].wait()
    stores[3].wait()


def retreat(gres1, xs, wf, qs, ks, vs, ctx, aug, kaug):
    rows, width = xs.shape
    vmem = pl.BlockSpec(memory_space=VMEM)
    hbm = pl.BlockSpec(memory_space=ANY)
    return pl.pallas_call(
        retreat_kernel,
        out_shape=(
            jax.ShapeDtypeStruct((rows, width), F32),
            jax.ShapeDtypeStruct((4, width, width), BF16),
            jax.ShapeDtypeStruct((8, width), F32),
        ),
        in_specs=[vmem, vmem, hbm] + [vmem] * 6,
        out_specs=[vmem, hbm, vmem],
        scratch_shapes=[VMEM((rows, width), BF16)] * 5
        + [
            VMEM((2, width, width), BF16),
            VMEM((2, width, width), BF16),
            pltpu.SemaphoreType.DMA((2,)),
            pltpu.SemaphoreType.DMA((2,)),
        ],
        compiler_params=pltpu.CompilerParams(vmem_limit_bytes=LIMIT),
        cost_estimate=pl.CostEstimate(flops=2 * 14 * rows * width * width, bytes_accessed=40 << 20, transcendentals=1 << 24),
        name="retreat",
    )(gres1, xs, wf, qs, ks, vs, ctx, aug, kaug)


def paired(
    tokens, lengths, w_query, w_key, w_value, w_out, w_up, w_down, vectors, up_bias, cotangent
):
    half, width = tokens.shape[2:]
    rows = 2 * half
    rank = lax.axis_index("dp") * 2 + lax.axis_index("seq")
    y = lax.axis_index("seq")
    shard = w_query.shape[0]
    ws = jnp.concatenate(
        [
            jnp.stack([w_query, w_key, w_value, w_out]),
            w_up.reshape(shard, 4, width).transpose(1, 0, 2),
            w_down.reshape(4, shard, width),
        ]
    )
    spot = jnp.tile(vectors, (1, 4)) * (jnp.arange(128) // 32 == rank % 4).astype(BF16)
    sm = jnp.concatenate([spot, up_bias[None, :], jnp.zeros((7, 128), BF16)])
    wf, sf, xs, ct = gather(ws, sm, tokens, cotangent)
    xs = xs.reshape(rows, width)
    ct = ct.reshape(rows, width)
    wsquare = wf.reshape(12, width, width)
    length = lax.dynamic_index_in_dim(lengths[:, 0], y, keepdims=False)
    near = jnp.arange(half, dtype=jnp.int32)
    position = jnp.concatenate([y * half + near, (1 - y) * half + near])
    ok = position < length
    valid = jnp.broadcast_to(ok[:, None], (rows, 128)).astype(F32)
    sixty = jnp.arange(128) % 64
    bias = jnp.where(ok, 0.0, -1e9)[:, None]
    kaug = jnp.where(sixty == 0, bias, ((sixty > 0) & (sixty < 4)).astype(F32)).astype(BF16)
    qs, ks, vs, ctx, aug, res, vec = attend(xs, wsquare, sf.reshape(32, 16, 128), kaug)
    act, gres1, gwu, gwd, frows, fbias = feed(res, ct, valid, vec, wf)
    gtok, dw, arows = retreat(gres1, xs, wsquare, qs, ks, vs, ctx, aug, kaug)
    all_rows = jnp.concatenate([arows[0:2], frows[2:8]])
    small = jnp.concatenate(
        [
            jnp.repeat(all_rows.reshape(8, 8, 128).transpose(1, 0, 2), 4, axis=0),
            fbias[:, 0, :].reshape(32, 1, 128),
            jnp.zeros((32, 7, 128), F32),
        ],
        axis=1,
    ).astype(BF16)
    six = (4, 2, 2, 2)
    back = jnp.concatenate([act[half:], gtok[half:].astype(BF16)])
    gu, gd, ga, gs, home = scatter(
        [
            gwu.reshape((4,) + six + (shard, width)),
            gwd.reshape((4,) + six + (shard, width)),
            dw.reshape((4,) + six + (shard, width)),
        ],
        small.reshape(six + (16, 128)),
        back,
        1,
    )

    def in_place(own, other):
        mine = y == 0
        first = jnp.where(mine, own, other)
        second = jnp.where(mine, other, own)
        return jnp.stack([first, second])[:, None]

    activations = in_place(act[:half], home[:half])
    grad_tokens = in_place(gtok[:half], home[half:].astype(F32))
    grad_vectors = lax.dynamic_slice_in_dim(gs[0:8], (rank % 4) * 32, 32, axis=1)
    return (
        activations,
        grad_tokens,
        ga[0],
        ga[1],
        ga[2],
        ga[3],
        gu.transpose(1, 0, 2).reshape(shard, 4 * width),
        gd.reshape(4 * shard, width),
        grad_vectors,
        gs[8],
    )


def solution(mesh):
    placed = (
        P(None, "dp", "seq", None),
        P(None, "dp"),
        P(("dp", "seq"), None),
        P(("dp", "seq"), None),
        P(("dp", "seq"), None),
        P(("dp", "seq"), None),
        P(("dp", "seq"), None),
        P(("dp", "seq"), None),
        P(None, ("dp", "seq")),
        P(("dp", "seq")),
        P(None, "dp", "seq", None),
    )
    own = mesh.shape["dp"] == 16 and mesh.shape["seq"] == 2
    return jax.shard_map(
        paired if own else per_device,
        mesh=mesh,
        in_specs=placed,
        out_specs=(
            P(None, "dp", "seq", None),
            P(None, "dp", "seq", None),
            P(("dp", "seq"), None),
            P(("dp", "seq"), None),
            P(("dp", "seq"), None),
            P(("dp", "seq"), None),
            P(("dp", "seq"), None),
            P(("dp", "seq"), None),
            P(None, ("dp", "seq")),
            P(("dp", "seq")),
        ),
        check_vma=False,
    )
```

```python
import functools
import math

import jax
import jax.numpy as jnp
from jax import lax
from jax.experimental import pallas as pl
from jax.experimental.pallas import tpu as pltpu
from jax.sharding import PartitionSpec as P

H = 16


EPSILON = 1e-05


def fetch_forward(w_query, w_key, w_value, w_out, w_up, w_down, vectors, up_bias):
    return (
        lax.all_gather(w_query, ("dp", "seq"), axis=0, tiled=True),
        lax.all_gather(w_key, ("dp", "seq"), axis=0, tiled=True),
        lax.all_gather(w_value, ("dp", "seq"), axis=0, tiled=True),
        lax.all_gather(w_out, ("dp", "seq"), axis=0, tiled=True),
        lax.all_gather(w_up, ("dp", "seq"), axis=0, tiled=True),
        lax.all_gather(w_down, ("dp", "seq"), axis=0, tiled=True),
        lax.all_gather(vectors, ("dp", "seq"), axis=1, tiled=True),
        lax.all_gather(up_bias, ("dp", "seq"), axis=0, tiled=True),
    )


def fetch_backward(w_query, w_key, w_value, w_out, w_up, w_down, vectors, up_bias):
    return (
        lax.all_gather(w_query, ("dp", "seq"), axis=0, tiled=True),
        lax.all_gather(w_key, ("dp", "seq"), axis=0, tiled=True),
        lax.all_gather(w_value, ("dp", "seq"), axis=0, tiled=True),
        lax.all_gather(w_out, ("dp", "seq"), axis=0, tiled=True),
        lax.all_gather(w_up, ("dp", "seq"), axis=0, tiled=True),
        lax.all_gather(w_down, ("dp", "seq"), axis=0, tiled=True),
        lax.all_gather(vectors, ("dp", "seq"), axis=1, tiled=True),
        lax.all_gather(up_bias, ("dp", "seq"), axis=0, tiled=True),
    )


def norm_forward(inputs, gain, shift):
    center = inputs - jnp.mean(inputs, axis=-1, keepdims=True)
    inverse = lax.rsqrt(jnp.mean(center * center, axis=-1, keepdims=True) + EPSILON)
    normed = center * inverse
    return (normed * gain + shift, normed, inverse)


def norm_backward(grad_out, normed, inverse, gain):
    grad_norm = grad_out * gain
    inner = (
        grad_norm
        - jnp.mean(grad_norm, axis=-1, keepdims=True)
        - normed * jnp.mean(grad_norm * normed, axis=-1, keepdims=True)
    )
    return (inner * inverse, jnp.sum(grad_out * normed, axis=0), jnp.sum(grad_out, axis=0))


def score_heads(query_heads, key_heads, key_valid, factor):
    scores = (
        jnp.einsum("qhd,khd->hqk", query_heads, key_heads, preferred_element_type=jnp.float32)
        * factor
    )
    return jnp.where(key_valid[None, None, :], scores, -1000000000.0)


def per_device(
    tokens, lengths, w_query, w_key, w_value, w_out, w_up, w_down, vectors, up_bias, cotangent
):
    micro = tokens.shape[0]
    slot = tokens.shape[2]
    width = tokens.shape[3]
    hidden_units = w_up.shape[1]
    heads = H
    head_dim = width // heads
    factor = 1.0 / math.sqrt(head_dim)
    positions = lax.axis_index("seq") * slot + jnp.arange(slot, dtype=jnp.int32)
    f32 = jnp.float32
    sums = [
        jnp.zeros((width, width), f32),
        jnp.zeros((width, width), f32),
        jnp.zeros((width, width), f32),
        jnp.zeros((width, width), f32),
        jnp.zeros((width, hidden_units), f32),
        jnp.zeros((hidden_units, width), f32),
        jnp.zeros((8, width), f32),
        jnp.zeros((hidden_units,), f32),
    ]
    outputs = []
    grad_list = []
    for micro_index in range(micro):
        full_query, full_key, full_value, full_out, full_up, full_down, full_vectors, full_bias = (
            fetch_forward(w_query, w_key, w_value, w_out, w_up, w_down, vectors, up_bias)
        )
        vec_f = full_vectors.astype(f32)
        bias_f = full_bias.astype(f32)
        rows_in = tokens[micro_index, 0]
        length = lengths[micro_index, 0]
        valid = (positions < length)[:, None].astype(f32)
        query = (jnp.dot(rows_in, full_query, preferred_element_type=f32) + vec_f[0]).astype(
            jnp.bfloat16
        )
        keys_own = jnp.dot(rows_in, full_key, preferred_element_type=f32).astype(jnp.bfloat16)
        vals_own = (jnp.dot(rows_in, full_value, preferred_element_type=f32) + vec_f[1]).astype(
            jnp.bfloat16
        )
        keys_all, vals_all = (
            lax.all_gather(keys_own, "seq", axis=0, tiled=True),
            lax.all_gather(vals_own, "seq", axis=0, tiled=True),
        )
        total_len = keys_all.shape[0]
        key_valid = jnp.arange(total_len, dtype=jnp.int32) < length
        query_heads = query.reshape(slot, heads, head_dim)
        key_heads = keys_all.reshape(total_len, heads, head_dim)
        val_heads = vals_all.reshape(total_len, heads, head_dim)
        scores = score_heads(query_heads, key_heads, key_valid, factor)
        top = jnp.max(scores, axis=-1, keepdims=True)
        log_total = top + jnp.log(jnp.sum(jnp.exp(scores - top), axis=-1, keepdims=True))
        probs = jnp.exp(scores - log_total).astype(jnp.bfloat16)
        context = (
            jnp.einsum("hqk,khd->qhd", probs, val_heads, preferred_element_type=f32)
            .reshape(slot, width)
            .astype(jnp.bfloat16)
        )
        attention = jnp.dot(context, full_out, preferred_element_type=f32) + vec_f[2]
        hidden, normed_one, inverse_one = norm_forward(
            rows_in.astype(f32) + attention, vec_f[3], vec_f[4]
        )
        hidden_low = hidden.astype(jnp.bfloat16)
        upper = jnp.dot(hidden_low, full_up, preferred_element_type=f32) + bias_f
        active = jax.nn.gelu(upper).astype(jnp.bfloat16)
        lowered = jnp.dot(active, full_down, preferred_element_type=f32) + vec_f[5]
        result, normed_two, inverse_two = norm_forward(hidden + lowered, vec_f[6], vec_f[7])
        outputs.append((result * valid).astype(jnp.bfloat16))
        full_query, full_key, full_value, full_out, full_up, full_down, full_vectors, full_bias = (
            fetch_backward(w_query, w_key, w_value, w_out, w_up, w_down, vectors, up_bias)
        )
        vec_f = full_vectors.astype(f32)
        grad_out = cotangent[micro_index, 0].astype(f32) * valid
        grad_res2, grad_gain2, grad_shift2 = norm_backward(
            grad_out, normed_two, inverse_two, vec_f[6]
        )
        grad_down = grad_res2.astype(jnp.bfloat16)
        grad_bias2 = jnp.sum(grad_down.astype(f32), axis=0)
        sums[5] = sums[5] + jnp.einsum("sf,sd->fd", active, grad_down, preferred_element_type=f32)
        grad_active = jnp.einsum("sd,fd->sf", grad_down, full_down, preferred_element_type=f32)
        gelu_pull = jax.vjp(jax.nn.gelu, upper)[1]
        grad_upper = gelu_pull(grad_active)[0].astype(jnp.bfloat16)
        sums[7] = sums[7] + jnp.sum(grad_upper.astype(f32), axis=0)
        sums[4] = sums[4] + jnp.einsum(
            "sd,sf->df", hidden_low, grad_upper, preferred_element_type=f32
        )
        grad_hidden = grad_res2 + jnp.einsum(
            "sf,df->sd", grad_upper, full_up, preferred_element_type=f32
        )
        grad_res1, grad_gain1, grad_shift1 = norm_backward(
            grad_hidden, normed_one, inverse_one, vec_f[3]
        )
        grad_att = grad_res1.astype(jnp.bfloat16)
        grad_bias_out = jnp.sum(grad_att.astype(f32), axis=0)
        sums[3] = sums[3] + jnp.einsum("sd,se->de", context, grad_att, preferred_element_type=f32)
        grad_context = jnp.einsum(
            "se,de->sd", grad_att, full_out, preferred_element_type=f32
        ).astype(jnp.bfloat16)
        grad_ctx_heads = grad_context.reshape(slot, heads, head_dim)
        scores_again = score_heads(query_heads, key_heads, key_valid, factor)
        full_probs = jnp.exp(scores_again - log_total)
        probs_low = full_probs.astype(jnp.bfloat16)
        grad_probs = jnp.einsum(
            "qhd,khd->hqk", grad_ctx_heads, val_heads, preferred_element_type=f32
        )
        grad_val_term = jnp.einsum(
            "hqk,qhd->khd", probs_low, grad_ctx_heads, preferred_element_type=f32
        )
        row_inner = jnp.sum(full_probs * grad_probs, axis=-1, keepdims=True)
        grad_scores = (full_probs * (grad_probs - row_inner)).astype(jnp.bfloat16)
        grad_query = (
            (
                jnp.einsum("hqk,khd->qhd", grad_scores, key_heads, preferred_element_type=f32)
                * factor
            )
            .reshape(slot, width)
            .astype(jnp.bfloat16)
        )
        grad_key_term = (
            jnp.einsum("hqk,qhd->khd", grad_scores, query_heads, preferred_element_type=f32)
            * factor
        )
        grad_keys, grad_vals = (
            lax.psum_scatter(
                grad_key_term.reshape(total_len, width).astype(jnp.bfloat16),
                "seq",
                scatter_dimension=0,
                tiled=True,
            ).astype(jnp.float32),
            lax.psum_scatter(
                grad_val_term.reshape(total_len, width).astype(jnp.bfloat16),
                "seq",
                scatter_dimension=0,
                tiled=True,
            ).astype(jnp.float32),
        )
        grad_keys = grad_keys.astype(jnp.bfloat16)
        grad_vals = grad_vals.astype(jnp.bfloat16)
        grad_bias_query = jnp.sum(grad_query.astype(f32), axis=0)
        grad_bias_vals = jnp.sum(grad_vals.astype(f32), axis=0)
        sums[0] = sums[0] + jnp.einsum("sd,se->de", rows_in, grad_query, preferred_element_type=f32)
        sums[1] = sums[1] + jnp.einsum("sd,se->de", rows_in, grad_keys, preferred_element_type=f32)
        sums[2] = sums[2] + jnp.einsum("sd,se->de", rows_in, grad_vals, preferred_element_type=f32)
        sums[6] = sums[6] + jnp.stack(
            [
                grad_bias_query,
                grad_bias_vals,
                grad_bias_out,
                grad_gain1,
                grad_shift1,
                grad_bias2,
                grad_gain2,
                grad_shift2,
            ]
        )
        grad_rows = grad_res1 + jnp.einsum(
            "se,de->sd", grad_query, full_query, preferred_element_type=f32
        )
        grad_rows = grad_rows + jnp.einsum(
            "se,de->sd", grad_keys, full_key, preferred_element_type=f32
        )
        grad_rows = grad_rows + jnp.einsum(
            "se,de->sd", grad_vals, full_value, preferred_element_type=f32
        )
        grad_list.append(grad_rows)
    shares = (
        lax.psum_scatter(sums[0], ("dp", "seq"), scatter_dimension=0, tiled=True),
        lax.psum_scatter(sums[1], ("dp", "seq"), scatter_dimension=0, tiled=True),
        lax.psum_scatter(sums[2], ("dp", "seq"), scatter_dimension=0, tiled=True),
        lax.psum_scatter(sums[3], ("dp", "seq"), scatter_dimension=0, tiled=True),
        lax.psum_scatter(sums[4], ("dp", "seq"), scatter_dimension=0, tiled=True),
        lax.psum_scatter(sums[5], ("dp", "seq"), scatter_dimension=0, tiled=True),
        lax.psum_scatter(sums[6], ("dp", "seq"), scatter_dimension=1, tiled=True),
        lax.psum_scatter(sums[7], ("dp", "seq"), scatter_dimension=0, tiled=True),
    )
    activations = jnp.stack(outputs)[:, None]
    grad_tokens = jnp.stack(grad_list)[:, None]
    return (
        activations,
        grad_tokens,
        shares[0],
        shares[1],
        shares[2],
        shares[3],
        shares[4],
        shares[5],
        shares[6],
        shares[7],
    )


MESH = pl.DeviceIdType.MESH
F32 = jnp.float32
BF16 = jnp.bfloat16
ANY = pl.ANY
VMEM = pltpu.VMEM
LOG2E = math.log2(math.e)
LIMIT = 58 * 1024 * 1024
GELU_C = math.sqrt(2.0 / math.pi)
GELU_A = 0.044715


def nt(a, b):
    return lax.dot_general(a, b, (((1,), (1,)), ((), ())), preferred_element_type=F32)


def nn(a, b):
    return lax.dot_general(a, b, (((1,), (0,)), ((), ())), preferred_element_type=F32)


def tn(a, b):
    return lax.dot_general(a, b, (((0,), (0,)), ((), ())), preferred_element_type=F32)


def place():
    dp = lax.axis_index("dp")
    return dp // 4, (dp // 2) % 2, dp % 2, lax.axis_index("seq")


def device(z, x, c, y):
    return (z * 4 + x * 2 + c, y)


def greet(z, x, c, y):
    barrier = pltpu.get_barrier_semaphore()
    partners = [device(z, x, 1 - c, y), device(z, 1 - x, c, y), device(z, x, c, 1 - y)]
    partners += [device((z + d) % 4, x, c, y) for d in (1, 2, 3)]
    for partner in partners:
        pl.semaphore_signal(barrier, inc=1, device_id=partner, device_id_type=MESH)
    pl.semaphore_wait(barrier, len(partners))


PHASES = 4
SLOTS = 6


def orders(half):
    return ("yzxc", "zyxc" if half == 0 else "zxyc")


def gather_copies(ref, rows, send, recv, order, phase, pos):
    z, x, c, y = pos
    every = slice(None)
    done = order[:phase]
    have = (
        every if "z" in done else z,
        every if "x" in done else x,
        every if "c" in done else c,
        every if "y" in done else y,
        rows,
    )

    def copy(slot, target):
        return pltpu.make_async_remote_copy(
            src_ref=ref.at[have],
            dst_ref=ref.at[have],
            send_sem=send.at[slot],
            recv_sem=recv.at[slot],
            device_id=device(*target),
            device_id_type=MESH,
        )

    axis = order[phase]
    if axis == "z":
        return [copy(2 + d, ((z + d) % 4, x, c, y)) for d in (1, 2, 3)]
    if axis == "x":
        return [copy(0, (z, 1 - x, c, y))]
    if axis == "y":
        return [copy(1, (z, x, c, 1 - y))]
    return [copy(2, (z, x, 1 - c, y))]


def gather_phase(ref, rows, send, recv, phase, pos, half):
    for core in (0, 1):
        for odd in (0, 1):
            if core == 0 and odd == 1:
                continue
            order = orders(odd)[core]
            here = pos[2] == core
            if core == 1:
                here = here & (half == odd)

            @pl.when(here)
            def _():
                if phase > 0:
                    for copy in gather_copies(ref, rows, send, recv, order, phase - 1, pos):
                        copy.wait_recv()
                if phase < PHASES:
                    for copy in gather_copies(ref, rows, send, recv, order, phase, pos):
                        copy.start()


def gather_sent(ref, rows, send, recv, pos, half):
    for core in (0, 1):
        for odd in (0, 1):
            if core == 0 and odd == 1:
                continue
            order = orders(odd)[core]
            here = pos[2] == core
            if core == 1:
                here = here & (half == odd)

            @pl.when(here)
            def _():
                for phase in range(PHASES):
                    for copy in gather_copies(ref, rows, send, recv, order, phase, pos):
                        copy.wait_send()


def lanes(shape):
    return lax.broadcasted_iota(jnp.int32, shape, len(shape) - 1)


def norm(v):
    center = v - jnp.mean(v, axis=-1, keepdims=True)
    inverse = lax.rsqrt(jnp.mean(center * center, axis=-1, keepdims=True) + EPSILON)
    return center * inverse, inverse


def norm_back(g, normed, inverse, gain):
    gn = g * gain
    inner = gn - jnp.mean(gn, axis=-1, keepdims=True) - normed * jnp.mean(gn * normed, axis=-1, keepdims=True)
    return inner * inverse


def rowsum(v):
    return jnp.sum(v, axis=0, keepdims=True)


def blocks(rows, block, body):
    def run(b, carry):
        body(pl.ds(pl.multiple_of(b * block, block), block))
        return carry

    lax.fori_loop(0, rows // block, run, 0)


def tiles(width, tile, body):
    def run(b, carry):
        body(b, pl.ds(pl.multiple_of(b * tile, tile), tile))
        return carry

    lax.fori_loop(0, width // tile, run, 0)


def forward_kernel(
    wq, wk, wv, wo, wup, wdown, sm, tok, cot, kaug, valid,
    wfa, wfd, sf, xs_o, q_o, k_o, v_o, ctx_o, aug_o, res_o, low_o, act_o, slope_o, back_o, gdn_o, out_o, vec, rows_out,
    xs, ct, qs, ks, vs, ctx, aug, res, acc, low, actv, slope, wbuf, dbuf, small,
    send, recv, place_sem, own_sem, swap_send, swap_recv, wsem, dsem, out_sem,
):
    pos = place()
    z, x, c, y = pos
    rows, width = xs.shape
    half = rows // 2
    chunks = 24
    high = 16

    first = [pltpu.make_async_copy(w, wfa.at[i, z, x, c, y], place_sem.at[i]) for i, w in enumerate((wq, wk, wv, wo))]
    for j in range(4):
        first.append(
            pltpu.make_async_copy(
                wup.at[:, width * j : width * (j + 1)], wfa.at[4 + j, z, x, c, y], place_sem.at[4 + j]
            )
        )
    for j in range(4):
        first.append(
            pltpu.make_async_copy(wdown.at[:, 256 * j : 256 * (j + 1)], wfd.at[j, z, x, c, y], place_sem.at[8 + j])
        )
    first.append(pltpu.make_async_copy(sm, sf.at[z, x, c, y], place_sem.at[12]))
    for copy in first:
        copy.start()
    mine = [
        pltpu.make_async_copy(tok.at[y, 0], xs.at[pl.ds(0, half)], own_sem.at[0]),
        pltpu.make_async_copy(cot.at[y, 0], ct.at[pl.ds(0, half)], own_sem.at[1]),
    ]
    for copy in mine:
        copy.start()
    greet(*pos)
    for copy in first:
        copy.wait()

    piece = half // 8

    def swap(src, dst, slot, index):
        at = pl.multiple_of(index * piece, piece)
        return pltpu.make_async_remote_copy(
            src_ref=src.at[1 - y, 0, pl.ds(at, piece)],
            dst_ref=dst.at[pl.ds(half + at, piece)],
            send_sem=swap_send.at[slot, index],
            recv_sem=swap_recv.at[slot, index],
            device_id=device(z, x, c, 1 - y),
            device_id_type=MESH,
        )

    def chunk(index, kind):
        odd = index % 2
        if kind == 0:
            return (wfa.at[index // 2], pl.ds(pl.multiple_of(odd * 16, 16), 16), send.at[index], recv.at[index])
        return (wfd.at[index // 2 - 8], pl.ds(pl.multiple_of(odd * 64, 64), 64), send.at[index], recv.at[index])

    tiny = (sf, slice(None), send.at[chunks], recv.at[chunks])

    def step(t, carry):
        for phase in range(PHASES + 1):
            index = t - phase

            @pl.when((index >= 0) & (index < high))
            def _():
                gather_phase(*chunk(index, 0), phase, pos, index % 2)

            @pl.when((index >= high) & (index < chunks))
            def _():
                gather_phase(*chunk(index, 1), phase, pos, index % 2)

            @pl.when(index == 0)
            def _():
                gather_phase(*tiny, phase, pos, 0)

        @pl.when(t < 4)
        def _():
            swap(tok, xs, 0, 2 * t).start()
            swap(tok, xs, 0, 2 * t + 1).start()

        @pl.when((t >= 12) & (t < 20))
        def _():
            swap(cot, ct, 1, t - 12).start()

        return carry

    def advance(start, stop):
        lax.fori_loop(start, stop, step, 0)

    def weight(index, slot):
        return pltpu.make_async_copy(wfa.at[index], wbuf.at[slot], wsem.at[slot])

    def square(slot, cols):
        return wbuf[slot, :, :, :, :, :, cols].reshape(width, cols.size)

    def save(src, dst, slot):
        copy = pltpu.make_async_copy(src, dst, out_sem.at[slot])
        copy.start()
        return copy

    advance(0, 6)
    weight(0, 0).start()
    for index in range(8):
        swap(tok, xs, 0, index).wait_recv()
    for copy in mine:
        copy.wait()
    saves = [save(xs, xs_o, 0)]
    gathered = pltpu.make_async_copy(sf, small, own_sem.at[2])
    gathered.start()
    gathered.wait()
    tiles32 = [small[a, b, d, e].astype(F32) for a in range(4) for b in range(2) for d in range(2) for e in range(2)]
    for g in range(8):
        vec[0:8, 128 * g : 128 * g + 128] = sum(tiles32[4 * g + s] for s in range(4))[0:8]
    for r in range(4):
        for g in range(8):
            vec[8 + r : 9 + r, 128 * g : 128 * g + 128] = tiles32[8 * r + g][8:9]
    vec[12:16, :] = jnp.zeros((4, width), F32)

    for i, dst in enumerate((qs, ks, vs)):
        if i > 0:
            advance(4 + 2 * i, 6 + 2 * i)
            weight(i, i % 2).start()
        weight(i, i % 2).wait()

        def project(n, cols):
            out = nn(xs[...], square(i % 2, cols))
            if i == 0:
                out = (out + vec[0:1, cols]) * (LOG2E / 8.0)
            elif i == 2:
                out = out + vec[1:2, cols]
            dst[:, cols] = out.astype(BF16)

        tiles(width, 256, project)
        saves.append(save(dst, (q_o, k_o, v_o)[i], 1 + i))
    advance(10, 12)
    weight(3, 1).start()

    block = 256
    low1 = (lanes((1, 128)) < 64).astype(F32).astype(BF16)
    high1 = (lanes((1, 128)) >= 64).astype(F32).astype(BF16)
    ones1 = (lanes((1, 128)) % 64 == 0).astype(F32).astype(BF16)
    qlane = lanes((block, 128))
    sixty = qlane % 64

    def pair(hp, carry):
        cols = pl.ds(pl.multiple_of(hp * 128, 128), 128)
        k2 = ks[:, cols]
        v2 = vs[:, cols]
        ka = k2 * low1 + kaug[...] * high1
        kb = k2 * high1 + kaug[...] * low1

        def query_block(sl):
            q2 = qs[sl, cols]
            parts = []
            for own, other, kk in ((low1, high1, ka), (high1, low1, kb)):
                s = nt(q2 * own + ones1 * other, kk)
                top = jnp.max(s, axis=1, keepdims=True)
                e = jnp.exp2(s - top)
                total = jnp.sum(e, axis=1, keepdims=True)
                o = nn(e.astype(BF16), v2)
                parts.append((o / total, -(top + jnp.log2(total))))
            lower = qlane < 64
            ctx[sl, cols] = jnp.where(lower, parts[0][0], parts[1][0]).astype(BF16)
            neg = jnp.where(lower, parts[1][1], parts[0][1])
            hi = neg.astype(BF16).astype(F32)
            mid = (neg - hi).astype(BF16).astype(F32)
            lo = neg - hi - mid
            aug[sl, cols] = jnp.where(
                sixty == 0,
                1.0,
                jnp.where(sixty == 1, hi, jnp.where(sixty == 2, mid, jnp.where(sixty == 3, lo, 0.0))),
            ).astype(BF16)

        blocks(rows, block, query_block)
        advance(12 + (hp * 3) // 2, 12 + ((hp + 1) * 3) // 2)
        return carry

    lax.fori_loop(0, width // 128, pair, 0)
    saves.append(save(ctx, ctx_o, 4))
    saves.append(save(aug, aug_o, 5))
    weight(3, 1).wait()
    weight(4, 0).start()

    def project_out(n, cols):
        out = nn(ctx[...], square(1, cols))
        res[:, cols] = xs[:, cols].astype(F32) + (out + vec[2:3, cols])

    tiles(width, 256, project_out)
    weight(5, 1).start()
    saves.append(save(res, res_o, 6))

    def normalize(sl):
        normed, _ = norm(res[sl, :])
        low[sl, :] = (normed * vec[3:4, :] + vec[4:5, :]).astype(BF16)

    blocks(rows, block, normalize)
    saves.append(save(low, low_o, 7))

    for j in range(4):
        weight(4 + j, j % 2).wait()

        def climb(n, cols):
            up = nn(low[...], square(j % 2, cols)) + vec[8 + j : 9 + j, cols]
            sq = up * up
            t = jnp.tanh(up * (GELU_C + (GELU_C * GELU_A) * sq))
            hf = 0.5 * up
            actv[j, :, cols] = (hf + hf * t).astype(BF16)
            slope[j, :, cols] = (
                0.5 + 0.5 * t + hf * (1.0 - t * t) * (GELU_C + (3.0 * GELU_C * GELU_A) * sq)
            ).astype(BF16)

        tiles(width, 256, climb)
        if j < 2:
            weight(6 + j, j).start()
        saves.append(save(actv.at[j], act_o.at[j], 8 + j))
        saves.append(save(slope.at[j], slope_o.at[j], 12 + j))
        advance(24 + j, 25 + j)

    def shaft(j, slot):
        return pltpu.make_async_copy(wfd.at[j], dbuf.at[slot], dsem.at[slot])

    shaft(0, 0).start()
    shaft(1, 1).start()
    for j in range(4):
        shaft(j, j % 2).wait()
        cols = slice(256 * j, 256 * (j + 1))
        total = vec[5:6, cols]
        for k in range(4):
            total = total + nn(actv[k], dbuf[j % 2, k].reshape(width, 256))
        acc[:, cols] = total
        if j < 2:
            shaft(2 + j, j).start()

    for index in range(8):
        swap(cot, ct, 1, index).wait_recv()
    saves[1].wait()
    rows_out[...] = jnp.zeros_like(rows_out)

    def middle(sl):
        normed, _ = norm(res[sl, :])
        hidden = normed * vec[3:4, :] + vec[4:5, :]
        normed, inverse = norm(hidden + acc[sl, :])
        ok = valid[sl, 0:1]
        qs[sl, :] = ((normed * vec[6:7, :] + vec[7:8, :]) * ok).astype(BF16)
        g = ct[sl, :].astype(F32) * ok
        back = norm_back(g, normed, inverse, vec[6:7, :])
        acc[sl, :] = back
        gd = back.astype(BF16)
        ct[sl, :] = gd
        rows_out[6:7, :] += rowsum(g * normed)
        rows_out[7:8, :] += rowsum(g)
        rows_out[5:6, :] += rowsum(gd.astype(F32))

    blocks(rows, block, middle)
    saves.append(save(qs, out_o, 16))
    saves.append(save(acc, back_o, 17))
    saves.append(save(ct, gdn_o, 18))

    def finish(index, carry):
        @pl.when(index < high)
        def _():
            gather_sent(*chunk(index, 0), pos, index % 2)

        @pl.when(index >= high)
        def _():
            gather_sent(*chunk(index, 1), pos, index % 2)

        return carry

    lax.fori_loop(0, chunks, finish, 0)
    gather_sent(*tiny, pos, 0)
    for slot, (src, dst) in enumerate(((tok, xs), (cot, ct))):
        for index in range(8):
            swap(src, dst, slot, index).wait_send()
    for k, copy in enumerate(saves):
        if k != 1:
            copy.wait()


def forward_pass(weights, sm, tok, cot, kaug, valid):
    width = tok.shape[3]
    rows = 2 * tok.shape[2]
    low = jax.ShapeDtypeStruct((rows, width), BF16)
    full = jax.ShapeDtypeStruct((rows, width), F32)
    wide = jax.ShapeDtypeStruct((4, rows, width), BF16)
    six = (4, 2, 2, 2)
    vmem = pl.BlockSpec(memory_space=VMEM)
    hbm = pl.BlockSpec(memory_space=ANY)
    dma = pltpu.SemaphoreType.DMA
    return pl.pallas_call(
        forward_kernel,
        out_shape=(
            jax.ShapeDtypeStruct((8,) + six + (32, width), BF16),
            jax.ShapeDtypeStruct((4,) + six + (128, 256), BF16),
            jax.ShapeDtypeStruct(six + (16, 128), BF16),
            low, low, low, low, low, low, full, low, wide, wide, full, low, low,
            jax.ShapeDtypeStruct((16, width), F32),
            jax.ShapeDtypeStruct((8, width), F32),
        ),
        in_specs=[vmem] * 7 + [hbm] * 2 + [vmem] * 2,
        out_specs=[hbm] * 16 + [vmem] * 2,
        scratch_shapes=[VMEM((rows, width), BF16)] * 7
        + [
            VMEM((rows, width), F32),
            VMEM((rows, width), F32),
            VMEM((rows, width), BF16),
            VMEM((4, rows, width), BF16),
            VMEM((4, rows, width), BF16),
            VMEM((2,) + six + (32, width), BF16),
            VMEM((2,) + six + (128, 256), BF16),
            VMEM(six + (16, 128), BF16),
            dma((25, SLOTS)),
            dma((25, SLOTS)),
            dma((13,)),
            dma((3,)),
            dma((2, 8)),
            dma((2, 8)),
            dma((2,)),
            dma((2,)),
            dma((19,)),
        ],
        compiler_params=pltpu.CompilerParams(collective_id=0, has_side_effects=True, vmem_limit_bytes=LIMIT),
        cost_estimate=pl.CostEstimate(flops=2 * 14 * rows * width * width, bytes_accessed=90 << 20, transcendentals=1 << 24),
        name="forward_pass",
    )(*weights, sm, tok, cot, kaug, valid)


CHUNKS = 12
DEPTH = 4
STARTS = (0, 1, 2, 3, 4, 5, 6, 7, 8, 12, 16, 17)
TICKS = STARTS[-1] + PHASES + 1


def chunk_at(tick):
    index = jnp.where(tick <= 8, tick, jnp.where(tick <= 12, 9, tick - 6))
    return index, (tick >= 0) & ((tick <= 8) | (tick == 12) | ((tick >= 16) & (tick <= 17)))


MODES = 3


def mode_of(core, index):
    return jnp.where(core == 0, 0, jnp.where(index < 9, 1, 2))


def scatter_copies(mode, phase, grad, bufs, send, recv, pos):
    z, x, c, y = pos
    b0, b1, b2, b3 = bufs

    def remote(src, dst, slot, target):
        return pltpu.make_async_remote_copy(
            src_ref=src,
            dst_ref=dst,
            send_sem=send.at[slot],
            recv_sem=recv.at[slot],
            device_id=device(*target),
            device_id_type=MESH,
        )

    across = (z, 1 - x, c, y)
    beside = (z, x, c, 1 - y)
    if phase == 0:
        return [remote(grad.at[:, :, 1 - c], b0, 2, (z, x, 1 - c, y))]
    if phase == 1:
        if mode == 1:
            return [remote(b0.at[:, :, 1 - y], b1, 1, beside)]
        return [remote(b0.at[:, 1 - x], b1, 0, across)]
    if phase == 2:
        if mode == 0:
            return [
                remote(b1.at[(z + d) % 4], b2.at[pl.ds(2 * (d - 1), 2)], 2 + d, ((z + d) % 4, x, c, y))
                for d in (1, 2, 3)
            ]
        if mode == 1:
            return [remote(b1.at[:, 1 - x], b2.at[pl.ds(0, 4)], 0, across)]
        return [remote(b1.at[:, 1 - y], b2.at[pl.ds(0, 4)], 1, beside)]
    if mode == 0:
        return [remote(b1.at[z, 1 - y], b3.at[0], 1, beside)]
    return [remote(b2.at[(z + d) % 4], b3.at[d - 1], 2 + d, ((z + d) % 4, x, c, y)) for d in (1, 2, 3)]


def scatter_add(mode, phase, own, bufs, out, pos):
    z, x, c, y = pos
    b0, b1, b2, b3 = bufs

    def plus(dst, a, b):
        dst[...] = (a.astype(F32) + b.astype(F32)).astype(dst.dtype)

    def each(body):
        def run(zz, carry):
            body(zz)
            return carry

        lax.fori_loop(0, 4, run, 0)

    if phase == 0:

        def body(zz):
            plus(b0.at[zz], own[zz], b0[zz])

        each(body)
    elif phase == 1:

        def body(zz):
            plus(b1.at[zz], b0[zz, :, y] if mode == 1 else b0[zz, x], b1[zz])

        each(body)
    elif mode == 0:
        if phase == 2:
            total = b1[z].astype(F32)
            for d in range(3):
                total = total + b2[pl.ds(2 * d, 2)].astype(F32)
            b1[z] = total.astype(BF16)
        else:
            out[...] = b1[z, y].astype(F32) + b3[0].astype(F32)
    elif phase == 2:

        def body(zz):
            plus(b2.at[zz], b1[zz, x] if mode == 1 else b1[zz, y], b2[zz])

        each(body)
    else:
        total = b2[z].astype(F32)
        for d in range(3):
            total = total + b3[d].astype(F32)
        out[...] = total


def scatter_phase(phase, mode, grad, own, own_sem, bufs, out, send, recv, credit, index, pos):
    z, x, c, y = pos

    def mine():
        return pltpu.make_async_copy(grad.at[:, :, c], own, own_sem)

    if phase == 0:
        mine().start()
        if credit is not None:

            @pl.when(index >= DEPTH)
            def _():
                pl.semaphore_wait(credit, 1)

    if phase == 1:
        mine().wait()
    for which in range(MODES):

        @pl.when(mode == which)
        def _():
            if phase > 0:
                for copy in scatter_copies(which, phase - 1, grad, bufs, send, recv, pos):
                    copy.wait_recv()
                if phase == 2:
                    for copy in scatter_copies(which, 1, grad, bufs, send, recv, pos):
                        copy.wait_send()
                scatter_add(which, phase - 1, own, bufs, out, pos)
            if phase < PHASES:
                for copy in scatter_copies(which, phase, grad, bufs, send, recv, pos):
                    copy.start()

    if phase == 2 and credit is not None:

        @pl.when(index < CHUNKS - DEPTH)
        def _():
            pl.semaphore_signal(credit, inc=1, device_id=device(z, x, 1 - c, y), device_id_type=MESH)


def scatter_sent(mode, grad, bufs, send, recv, pos):
    for which in range(MODES):

        @pl.when(mode == which)
        def _():
            for phase in (0, 2, 3):
                for copy in scatter_copies(which, phase, grad, bufs, send, recv, pos):
                    copy.wait_send()


def backward_kernel(
    wfa, wfd, xs_i, q_i, k_i, v_i, ctx_i, aug_i, res_i, low_i, act_i, slope_i, back_i, gdn_i, out_i, vec, rows_in, kaug,
    gw, act_o, gtok_o, outs, small_out,
    acc, rbuf, gdn, low, quad, duo, wbuf, dbuf, stage, own, b0, b1, b2, b3, home, rows_sum, bias_sum,
    small_g, small_own, s0, s1, s2, s3,
    send, recv, own_sem, credit, swap_send, swap_recv, load_sem, rsem, wsem, dsem, stage_sem, out_sem,
):
    pos = place()
    z, x, c, y = pos
    rows, width = acc.shape
    half = rows // 2
    block = 256

    def load(src, dst, slot):
        return pltpu.make_async_copy(src, dst, load_sem.at[slot])

    loads = [load(act_i.at[k], quad.at[k], k) for k in range(4)]
    loads += [load(gdn_i, gdn, 4), load(low_i, low, 5), load(back_i, acc, 6)]
    loads += [load(out_i.at[pl.ds(0, half)], duo.at[1, pl.ds(0, half)], 7), load(slope_i.at[0], duo.at[0], 8)]
    for k in (4, 0, 1, 2, 3, 5, 6, 7, 8):
        loads[k].start()
    greet(*pos)

    away = pltpu.make_async_remote_copy(
        src_ref=out_i.at[pl.ds(half, half)],
        dst_ref=act_o.at[y, 0],
        send_sem=swap_send.at[0],
        recv_sem=swap_recv.at[0],
        device_id=device(z, x, c, 1 - y),
        device_id_type=MESH,
    )
    away.start()

    def views(index):
        slot = index % DEPTH
        return (b0.at[slot], b1.at[index], b2.at[index], b3.at[index])

    small_bufs = (s0, s1, s2, s3)

    def step(t, carry):
        for phase in range(PHASES + 1):
            index, there = chunk_at(t - phase)

            @pl.when(there)
            def _():
                scatter_phase(
                    phase, mode_of(c, index), gw.at[index], own.at[index % 2], own_sem.at[index % 2], views(index),
                    outs.at[index], send.at[index], recv.at[index], credit, index, pos,
                )

            @pl.when(t - phase == STARTS[-1])
            def _():
                scatter_phase(
                    phase, mode_of(c, 0), small_g, small_own, own_sem.at[2], small_bufs, small_out,
                    send.at[CHUNKS], recv.at[CHUNKS], None, 0, pos,
                )

        return carry

    def advance(start, stop):
        lax.fori_loop(start, stop, step, 0)

    def weight(index, slot):
        return pltpu.make_async_copy(wfa.at[index], wbuf.at[slot], wsem.at[slot])

    def shaft(j, slot):
        return pltpu.make_async_copy(wfd.at[:, j], dbuf.at[slot], dsem.at[slot])

    def store(index, slot):
        return pltpu.make_async_copy(stage.at[slot], gw.at[index], stage_sem.at[slot])

    weight(4, 0).start()
    shaft(0, 0).start()
    rows_sum[...] = rows_in[...]
    bias_sum[...] = jnp.zeros_like(bias_sum)

    for k in (4, 0, 1, 2, 3):
        loads[k].wait()
    for jj in range(4):
        slot = jj % 2
        if jj >= 2:
            store(jj - 2, slot).wait()

        def quarter(k, carry):
            part = tn(quad[k], gdn[:, 256 * jj : 256 * (jj + 1)]).astype(BF16).reshape(2, 2, 2, 4, 32, 256)
            for q in range(4):
                stage[slot, k, :, :, :, :, 256 * q : 256 * (q + 1)] = part[:, :, :, q]
            return carry

        lax.fori_loop(0, 4, quarter, 0)
        store(jj, slot).start()
        if jj >= 2:
            advance(jj - 2, jj - 1)
    loads[5].wait()
    loads[6].wait()
    loads[7].wait()
    keep = pltpu.make_async_copy(duo.at[1, pl.ds(0, half)], act_o.at[y, 0], out_sem.at[0])
    keep.start()
    for k, src in enumerate((q_i, k_i, v_i, ctx_i)):
        load(src, quad.at[k], k).start()
    small_block = 128
    load(res_i.at[pl.ds(0, small_block)], rbuf.at[0], 9).start()

    def slope_load(j):
        return load(slope_i.at[j], duo.at[j % 2], 8 - j % 2)

    def square_rows(slot, n):
        return wbuf[slot, n].reshape(256, width)

    for j in range(4):
        slot = j % 2
        slope_load(j).wait()
        shaft(j, slot).wait()
        if j == 0:
            keep.wait()
        if j < 3:
            slope_load(j + 1).start()
            weight(5 + j, 1 - slot).start()
            shaft(j + 1, 1 - slot).start()
        for n in range(4):
            cols = slice(256 * n, 256 * (n + 1))
            total = nt(gdn[:, 0:256], dbuf[slot, 0, n // 2, n % 2].reshape(256, 256))
            for jj in range(1, 4):
                total = total + nt(
                    gdn[:, 256 * jj : 256 * (jj + 1)], dbuf[slot, jj, n // 2, n % 2].reshape(256, 256)
                )
            gu = (duo[slot, :, cols].astype(F32) * total).astype(BF16)
            duo[slot, :, cols] = gu
            bias_sum[8 * j : 8 * j + 1, cols] = rowsum(gu.astype(F32))
        store(2 + j, slot).wait()
        advance(2 + j, 3 + j)

        def up_grad(n, cols):
            part = tn(low[...], duo[slot, :, cols]).astype(BF16)
            stage[slot, :, :, :, :, :, cols] = part.reshape(4, 2, 2, 2, 32, 256)

        tiles(width, 256, up_grad)
        store(4 + j, slot).start()
        weight(4 + j, slot).wait()
        for n in range(4):
            cols = slice(256 * n, 256 * (n + 1))
            acc[:, cols] += nt(duo[slot], square_rows(slot, n))
    weight(3, 0).start()
    load(xs_i, duo.at[0], 8).start()
    load(aug_i, duo.at[1], 7).start()

    for b in range(rows // small_block):
        sl = slice(b * small_block, (b + 1) * small_block)
        load(res_i.at[pl.ds(b * small_block, small_block)], rbuf.at[b % 2], 9 + b % 2).wait()
        if b + 1 < rows // small_block:
            load(res_i.at[pl.ds((b + 1) * small_block, small_block)], rbuf.at[(b + 1) % 2], 9 + (b + 1) % 2).start()
        normed, inverse = norm(rbuf[b % 2])
        g = acc[sl, :]
        back = norm_back(g, normed, inverse, vec[3:4, :])
        acc[sl, :] = back
        gat = back.astype(BF16)
        gdn[sl, :] = gat
        rows_sum[3:4, :] += rowsum(g * normed)
        rows_sum[4:5, :] += rowsum(g)
        rows_sum[2:3, :] += rowsum(gat.astype(F32))

    store(6, 0).wait()
    advance(6, 7)
    for k in range(4):
        load((q_i, k_i, v_i, ctx_i)[k], quad.at[k], k).wait()

    def out_grad(n, cols):
        part = tn(quad[3], gdn[:, cols]).astype(BF16)
        stage[0, :, :, :, :, :, cols] = part.reshape(4, 2, 2, 2, 32, 256)

    tiles(width, 256, out_grad)
    store(8, 0).start()
    weight(3, 0).wait()
    for n in range(4):
        low[:, 256 * n : 256 * (n + 1)] = nt(gdn[...], square_rows(0, n)).astype(BF16)
    store(7, 1).wait()
    advance(7, 8)
    weight(0, 0).start()
    load(xs_i, duo.at[0], 8).wait()
    load(aug_i, duo.at[1], 7).wait()
    store(8, 0).wait()

    qs, ks, vs, ctx = (quad.at[k] for k in range(4))
    xs, aug = duo.at[0], duo.at[1]
    low1 = (lanes((1, 128)) < 64).astype(F32).astype(BF16)
    high1 = (lanes((1, 128)) >= 64).astype(F32).astype(BF16)
    ones1 = (lanes((1, 128)) % 64 < 2).astype(F32).astype(BF16)
    alane = lanes((rows, 128))
    lower = alane < 64
    sixty = alane % 64

    def token_grad(k, first, slot, target):
        def run(n, carry):
            src = pl.ds(pl.multiple_of(first + n * 256, 256), 256)
            dst = pl.ds(pl.multiple_of(target + n * 256, 256), 256)
            part = tn(xs[...], quad[k, :, src]).astype(BF16)
            stage[slot, :, :, :, :, :, dst] = part.reshape(4, 2, 2, 2, 32, 256)
            return carry

        lax.fori_loop(0, 2, run, 0)

    def pair(hp, carry):
        @pl.when(hp == 4)
        def _():
            token_grad(0, 0, 0, 0)
            token_grad(1, 0, 0, 512)
            store(9, 0).start()
            token_grad(2, 0, 1, 0)
            store(9, 0).wait()

        advance(8 + hp, 9 + hp)
        cols = pl.ds(pl.multiple_of(hp * 128, 128), 128)
        q2 = qs[:, cols]
        g2 = low[:, cols]
        au = aug[:, cols]
        prod = g2.astype(F32) * ctx[:, cols].astype(F32)
        da = -jnp.sum(jnp.where(lower, prod, 0.0), axis=1, keepdims=True)
        db = -jnp.sum(jnp.where(lower, 0.0, prod), axis=1, keepdims=True)
        neg = jnp.where(lower, db, da)
        hi = neg.astype(BF16).astype(F32)
        daug = jnp.where(sixty == 0, hi, jnp.where(sixty == 1, neg - hi, 0.0)).astype(BF16)
        qa = (q2 * low1 + au * high1, q2 * high1 + au * low1)
        ga = (g2 * low1 + daug * high1, g2 * high1 + daug * low1)
        gq = []
        gk_all = []
        gv_all = []
        for head in range(2):
            mine, other = (low1, high1) if head == 0 else (high1, low1)
            total = jnp.zeros((128, rows), F32)
            gks = []
            gvs = []
            for b in range(rows // block):
                sl = slice(b * block, (b + 1) * block)
                k2 = ks[sl, cols]
                v2 = vs[sl, cols]
                s = nt(k2 * mine + kaug[sl, :] * other, qa[head])
                p = jnp.exp2(s)
                gp = nt(v2 * mine + ones1 * other, ga[head])
                ds = (p * gp).astype(BF16)
                gvs.append(nn(p.astype(BF16), g2).astype(BF16) * mine)
                gks.append((nn(ds, q2) * (1.0 / LOG2E)).astype(BF16) * mine)
                total = total + tn(k2, ds)
            gq.append(total)
            gk_all.append(gks)
            gv_all.append(gvs)
        for b in range(rows // block):
            sl = slice(b * block, (b + 1) * block)
            ks[sl, cols] = gk_all[0][b] + gk_all[1][b]
            vs[sl, cols] = gv_all[0][b] + gv_all[1][b]
        both = jnp.concatenate([gq[0][0:64], gq[1][64:128]], axis=0) * 0.125
        qs[:, cols] = both.T.astype(BF16)
        return carry

    weight(1, 1).start()
    lax.fori_loop(0, 8, pair, 0)
    token_grad(0, 512, 1, 512)
    store(10, 1).start()
    token_grad(1, 512, 0, 0)
    token_grad(2, 512, 0, 512)
    store(11, 0).start()

    def bias_rows(n, cols):
        rows_sum[0:1, cols] = rowsum(quad[0, :, cols].astype(F32))
        rows_sum[1:2, cols] = rowsum(quad[2, :, cols].astype(F32))

    tiles(width, 256, bias_rows)
    for zz in range(4):
        for s in range(8):
            g = 2 * zz + s // 4
            tile = jnp.concatenate(
                [
                    rows_sum[:, 128 * g : 128 * (g + 1)],
                    bias_sum[8 * zz : 8 * zz + 8, 128 * s : 128 * (s + 1)],
                ],
                axis=0,
            )
            small_g[zz, s // 4, (s // 2) % 2, s % 2] = tile.astype(BF16)
    store(10, 1).wait()
    advance(16, 17)
    store(11, 0).wait()
    advance(17, 18)

    def token_rows(k, slot, sl):
        for n in range(4):
            cols = slice(256 * n, 256 * (n + 1))
            acc[sl, cols] += nt(quad[k, sl], square_rows(slot, n))

    weight(0, 0).wait()
    token_rows(0, 0, slice(0, rows))
    weight(2, 0).start()
    weight(1, 1).wait()
    token_rows(1, 1, slice(0, rows))
    weight(2, 0).wait()
    token_rows(2, 0, slice(half, rows))
    low[0:half, :] = acc[half:rows, :].astype(BF16)
    turn = pltpu.make_async_remote_copy(
        src_ref=low.at[pl.ds(0, half)],
        dst_ref=home,
        send_sem=swap_send.at[1],
        recv_sem=swap_recv.at[1],
        device_id=device(z, x, c, 1 - y),
        device_id_type=MESH,
    )
    turn.start()
    token_rows(2, 0, slice(0, half))
    kept = pltpu.make_async_copy(acc.at[pl.ds(0, half)], gtok_o.at[y, 0], out_sem.at[0])
    kept.start()
    advance(18, TICKS)
    turn.wait()
    acc[half:rows, :] = home[...].astype(F32)
    came = pltpu.make_async_copy(acc.at[pl.ds(half, half)], gtok_o.at[1 - y, 0], out_sem.at[1])
    came.start()
    away.wait()

    def finish(index, carry):
        scatter_sent(mode_of(c, index), gw.at[index], views(index), send.at[index], recv.at[index], pos)
        return carry

    lax.fori_loop(0, CHUNKS, finish, 0)
    scatter_sent(mode_of(c, 0), small_g, small_bufs, send.at[CHUNKS], recv.at[CHUNKS], pos)
    kept.wait()
    came.wait()


def backward_pass(wfa, wfd, saved, vec, rows_in, kaug):
    rows, width = saved[0].shape
    six = (4, 2, 2, 2)
    vmem = pl.BlockSpec(memory_space=VMEM)
    hbm = pl.BlockSpec(memory_space=ANY)
    dma = pltpu.SemaphoreType.DMA

    def buffers(rows, width, depth, count):
        return [
            VMEM(depth + (4, 2, 2, rows, width), BF16),
            VMEM(count + (4, 2, rows, width), BF16),
            VMEM(count + (6, rows, width), BF16),
            VMEM(count + (3, rows, width), BF16),
        ]

    return pl.pallas_call(
        backward_kernel,
        out_shape=(
            jax.ShapeDtypeStruct((CHUNKS,) + six + (32, width), BF16),
            jax.ShapeDtypeStruct((2, 1, rows // 2, width), BF16),
            jax.ShapeDtypeStruct((2, 1, rows // 2, width), F32),
            jax.ShapeDtypeStruct((CHUNKS, 32, width), F32),
            jax.ShapeDtypeStruct((16, 128), F32),
        ),
        in_specs=[hbm] * 15 + [vmem] * 3,
        out_specs=[hbm] * 3 + [vmem] * 2,
        scratch_shapes=[
            VMEM((rows, width), F32),
            VMEM((2, 128, width), F32),
            VMEM((rows, width), BF16),
            VMEM((rows, width), BF16),
            VMEM((4, rows, width), BF16),
            VMEM((2, rows, width), BF16),
            VMEM((2,) + six + (32, width), BF16),
            VMEM((2, 4, 2, 2, 2, 128, 256), BF16),
            VMEM((2,) + six + (32, width), BF16),
            VMEM((2, 4, 2, 2, 32, width), BF16),
        ]
        + buffers(32, width, (DEPTH,), (CHUNKS,))
        + [
            VMEM((rows // 2, width), BF16),
            VMEM((8, width), F32),
            VMEM((32, width), F32),
            VMEM(six + (16, 128), BF16),
            VMEM((4, 2, 2, 16, 128), BF16),
        ]
        + buffers(16, 128, (), ())
        + [
            dma((CHUNKS + 1, SLOTS)),
            dma((CHUNKS + 1, SLOTS)),
            dma((3,)),
            pltpu.SemaphoreType.REGULAR,
            dma((2,)),
            dma((2,)),
            dma((11,)),
            dma((2,)),
            dma((2,)),
            dma((2,)),
            dma((2,)),
            dma((2,)),
        ],
        compiler_params=pltpu.CompilerParams(collective_id=1, has_side_effects=True, vmem_limit_bytes=62 * 1024 * 1024),
        cost_estimate=pl.CostEstimate(flops=2 * 32 * rows * width * width, bytes_accessed=90 << 20, transcendentals=1 << 24),
        name="backward_pass",
    )(wfa, wfd, *saved, vec, rows_in, kaug)


def paired(
    tokens, lengths, w_query, w_key, w_value, w_out, w_up, w_down, vectors, up_bias, cotangent
):
    half, width = tokens.shape[2:]
    rows = 2 * half
    y = lax.axis_index("seq")
    rank = lax.axis_index("dp") * 2 + y
    spot = jnp.tile(vectors, (1, 4)) * (jnp.arange(128) // 32 == rank % 4).astype(BF16)
    sm = jnp.concatenate([spot, up_bias[None, :], jnp.zeros((7, 128), BF16)])
    length = lax.dynamic_index_in_dim(lengths[:, 0], y, keepdims=False)
    near = jnp.arange(half, dtype=jnp.int32)
    position = jnp.concatenate([y * half + near, (1 - y) * half + near])
    ok = position < length
    valid = jnp.broadcast_to(ok[:, None], (rows, 128)).astype(F32)
    sixty = jnp.arange(128) % 64
    bias = jnp.where(ok, 0.0, -1e9)[:, None]
    kaug = jnp.where(sixty == 0, bias, ((sixty > 0) & (sixty < 4)).astype(F32)).astype(BF16)
    weights = (w_query, w_key, w_value, w_out, w_up, w_down)
    wfa, wfd, _, *saved, vec, rows_in = forward_pass(weights, sm, tokens, cotangent, kaug, valid)
    _, activations, grad_tokens, outs, small = backward_pass(wfa, wfd, saved, vec, rows_in, kaug)
    cut = width // 2
    shard = outs.shape[1]
    return (
        activations,
        grad_tokens,
        jnp.concatenate([outs[9, :, :cut], outs[10, :, cut:]], axis=1),
        jnp.concatenate([outs[9, :, cut:], outs[11, :, :cut]], axis=1),
        jnp.concatenate([outs[10, :, :cut], outs[11, :, cut:]], axis=1),
        outs[8],
        outs[4:8].transpose(1, 0, 2).reshape(shard, 4 * width),
        outs[0:4].reshape(4, shard, 4, width // 4).transpose(2, 1, 0, 3).reshape(4 * shard, width),
        lax.dynamic_slice_in_dim(small[0:8], (rank % 4) * 32, 32, axis=1),
        small[8],
    )


def solution(mesh):
    placed = (
        P(None, "dp", "seq", None),
        P(None, "dp"),
        P(("dp", "seq"), None),
        P(("dp", "seq"), None),
        P(("dp", "seq"), None),
        P(("dp", "seq"), None),
        P(("dp", "seq"), None),
        P(("dp", "seq"), None),
        P(None, ("dp", "seq")),
        P(("dp", "seq")),
        P(None, "dp", "seq", None),
    )
    own = mesh.shape["dp"] == 16 and mesh.shape["seq"] == 2
    return jax.shard_map(
        paired if own else per_device,
        mesh=mesh,
        in_specs=placed,
        out_specs=(
            P(None, "dp", "seq", None),
            P(None, "dp", "seq", None),
            P(("dp", "seq"), None),
            P(("dp", "seq"), None),
            P(("dp", "seq"), None),
            P(("dp", "seq"), None),
            P(("dp", "seq"), None),
            P(("dp", "seq"), None),
            P(None, ("dp", "seq")),
            P(("dp", "seq")),
        ),
        check_vma=False,
    )
```

```python
import functools
import math

import jax
import jax.numpy as jnp
from jax import lax
from jax.experimental import pallas as pl
from jax.experimental.pallas import tpu as pltpu
from jax.sharding import PartitionSpec as P

H = 16


EPSILON = 1e-05


def fetch_forward(w_query, w_key, w_value, w_out, w_up, w_down, vectors, up_bias):
    return (
        lax.all_gather(w_query, ("dp", "seq"), axis=0, tiled=True),
        lax.all_gather(w_key, ("dp", "seq"), axis=0, tiled=True),
        lax.all_gather(w_value, ("dp", "seq"), axis=0, tiled=True),
        lax.all_gather(w_out, ("dp", "seq"), axis=0, tiled=True),
        lax.all_gather(w_up, ("dp", "seq"), axis=0, tiled=True),
        lax.all_gather(w_down, ("dp", "seq"), axis=0, tiled=True),
        lax.all_gather(vectors, ("dp", "seq"), axis=1, tiled=True),
        lax.all_gather(up_bias, ("dp", "seq"), axis=0, tiled=True),
    )


def fetch_backward(w_query, w_key, w_value, w_out, w_up, w_down, vectors, up_bias):
    return (
        lax.all_gather(w_query, ("dp", "seq"), axis=0, tiled=True),
        lax.all_gather(w_key, ("dp", "seq"), axis=0, tiled=True),
        lax.all_gather(w_value, ("dp", "seq"), axis=0, tiled=True),
        lax.all_gather(w_out, ("dp", "seq"), axis=0, tiled=True),
        lax.all_gather(w_up, ("dp", "seq"), axis=0, tiled=True),
        lax.all_gather(w_down, ("dp", "seq"), axis=0, tiled=True),
        lax.all_gather(vectors, ("dp", "seq"), axis=1, tiled=True),
        lax.all_gather(up_bias, ("dp", "seq"), axis=0, tiled=True),
    )


def norm_forward(inputs, gain, shift):
    center = inputs - jnp.mean(inputs, axis=-1, keepdims=True)
    inverse = lax.rsqrt(jnp.mean(center * center, axis=-1, keepdims=True) + EPSILON)
    normed = center * inverse
    return (normed * gain + shift, normed, inverse)


def norm_backward(grad_out, normed, inverse, gain):
    grad_norm = grad_out * gain
    inner = (
        grad_norm
        - jnp.mean(grad_norm, axis=-1, keepdims=True)
        - normed * jnp.mean(grad_norm * normed, axis=-1, keepdims=True)
    )
    return (inner * inverse, jnp.sum(grad_out * normed, axis=0), jnp.sum(grad_out, axis=0))


def score_heads(query_heads, key_heads, key_valid, factor):
    scores = (
        jnp.einsum("qhd,khd->hqk", query_heads, key_heads, preferred_element_type=jnp.float32)
        * factor
    )
    return jnp.where(key_valid[None, None, :], scores, -1000000000.0)


def per_device(
    tokens, lengths, w_query, w_key, w_value, w_out, w_up, w_down, vectors, up_bias, cotangent
):
    micro = tokens.shape[0]
    slot = tokens.shape[2]
    width = tokens.shape[3]
    hidden_units = w_up.shape[1]
    heads = H
    head_dim = width // heads
    factor = 1.0 / math.sqrt(head_dim)
    positions = lax.axis_index("seq") * slot + jnp.arange(slot, dtype=jnp.int32)
    f32 = jnp.float32
    sums = [
        jnp.zeros((width, width), f32),
        jnp.zeros((width, width), f32),
        jnp.zeros((width, width), f32),
        jnp.zeros((width, width), f32),
        jnp.zeros((width, hidden_units), f32),
        jnp.zeros((hidden_units, width), f32),
        jnp.zeros((8, width), f32),
        jnp.zeros((hidden_units,), f32),
    ]
    outputs = []
    grad_list = []
    for micro_index in range(micro):
        full_query, full_key, full_value, full_out, full_up, full_down, full_vectors, full_bias = (
            fetch_forward(w_query, w_key, w_value, w_out, w_up, w_down, vectors, up_bias)
        )
        vec_f = full_vectors.astype(f32)
        bias_f = full_bias.astype(f32)
        rows_in = tokens[micro_index, 0]
        length = lengths[micro_index, 0]
        valid = (positions < length)[:, None].astype(f32)
        query = (jnp.dot(rows_in, full_query, preferred_element_type=f32) + vec_f[0]).astype(
            jnp.bfloat16
        )
        keys_own = jnp.dot(rows_in, full_key, preferred_element_type=f32).astype(jnp.bfloat16)
        vals_own = (jnp.dot(rows_in, full_value, preferred_element_type=f32) + vec_f[1]).astype(
            jnp.bfloat16
        )
        keys_all, vals_all = (
            lax.all_gather(keys_own, "seq", axis=0, tiled=True),
            lax.all_gather(vals_own, "seq", axis=0, tiled=True),
        )
        total_len = keys_all.shape[0]
        key_valid = jnp.arange(total_len, dtype=jnp.int32) < length
        query_heads = query.reshape(slot, heads, head_dim)
        key_heads = keys_all.reshape(total_len, heads, head_dim)
        val_heads = vals_all.reshape(total_len, heads, head_dim)
        scores = score_heads(query_heads, key_heads, key_valid, factor)
        top = jnp.max(scores, axis=-1, keepdims=True)
        log_total = top + jnp.log(jnp.sum(jnp.exp(scores - top), axis=-1, keepdims=True))
        probs = jnp.exp(scores - log_total).astype(jnp.bfloat16)
        context = (
            jnp.einsum("hqk,khd->qhd", probs, val_heads, preferred_element_type=f32)
            .reshape(slot, width)
            .astype(jnp.bfloat16)
        )
        attention = jnp.dot(context, full_out, preferred_element_type=f32) + vec_f[2]
        hidden, normed_one, inverse_one = norm_forward(
            rows_in.astype(f32) + attention, vec_f[3], vec_f[4]
        )
        hidden_low = hidden.astype(jnp.bfloat16)
        upper = jnp.dot(hidden_low, full_up, preferred_element_type=f32) + bias_f
        active = jax.nn.gelu(upper).astype(jnp.bfloat16)
        lowered = jnp.dot(active, full_down, preferred_element_type=f32) + vec_f[5]
        result, normed_two, inverse_two = norm_forward(hidden + lowered, vec_f[6], vec_f[7])
        outputs.append((result * valid).astype(jnp.bfloat16))
        full_query, full_key, full_value, full_out, full_up, full_down, full_vectors, full_bias = (
            fetch_backward(w_query, w_key, w_value, w_out, w_up, w_down, vectors, up_bias)
        )
        vec_f = full_vectors.astype(f32)
        grad_out = cotangent[micro_index, 0].astype(f32) * valid
        grad_res2, grad_gain2, grad_shift2 = norm_backward(
            grad_out, normed_two, inverse_two, vec_f[6]
        )
        grad_down = grad_res2.astype(jnp.bfloat16)
        grad_bias2 = jnp.sum(grad_down.astype(f32), axis=0)
        sums[5] = sums[5] + jnp.einsum("sf,sd->fd", active, grad_down, preferred_element_type=f32)
        grad_active = jnp.einsum("sd,fd->sf", grad_down, full_down, preferred_element_type=f32)
        gelu_pull = jax.vjp(jax.nn.gelu, upper)[1]
        grad_upper = gelu_pull(grad_active)[0].astype(jnp.bfloat16)
        sums[7] = sums[7] + jnp.sum(grad_upper.astype(f32), axis=0)
        sums[4] = sums[4] + jnp.einsum(
            "sd,sf->df", hidden_low, grad_upper, preferred_element_type=f32
        )
        grad_hidden = grad_res2 + jnp.einsum(
            "sf,df->sd", grad_upper, full_up, preferred_element_type=f32
        )
        grad_res1, grad_gain1, grad_shift1 = norm_backward(
            grad_hidden, normed_one, inverse_one, vec_f[3]
        )
        grad_att = grad_res1.astype(jnp.bfloat16)
        grad_bias_out = jnp.sum(grad_att.astype(f32), axis=0)
        sums[3] = sums[3] + jnp.einsum("sd,se->de", context, grad_att, preferred_element_type=f32)
        grad_context = jnp.einsum(
            "se,de->sd", grad_att, full_out, preferred_element_type=f32
        ).astype(jnp.bfloat16)
        grad_ctx_heads = grad_context.reshape(slot, heads, head_dim)
        scores_again = score_heads(query_heads, key_heads, key_valid, factor)
        full_probs = jnp.exp(scores_again - log_total)
        probs_low = full_probs.astype(jnp.bfloat16)
        grad_probs = jnp.einsum(
            "qhd,khd->hqk", grad_ctx_heads, val_heads, preferred_element_type=f32
        )
        grad_val_term = jnp.einsum(
            "hqk,qhd->khd", probs_low, grad_ctx_heads, preferred_element_type=f32
        )
        row_inner = jnp.sum(full_probs * grad_probs, axis=-1, keepdims=True)
        grad_scores = (full_probs * (grad_probs - row_inner)).astype(jnp.bfloat16)
        grad_query = (
            (
                jnp.einsum("hqk,khd->qhd", grad_scores, key_heads, preferred_element_type=f32)
                * factor
            )
            .reshape(slot, width)
            .astype(jnp.bfloat16)
        )
        grad_key_term = (
            jnp.einsum("hqk,qhd->khd", grad_scores, query_heads, preferred_element_type=f32)
            * factor
        )
        grad_keys, grad_vals = (
            lax.psum_scatter(
                grad_key_term.reshape(total_len, width).astype(jnp.bfloat16),
                "seq",
                scatter_dimension=0,
                tiled=True,
            ).astype(jnp.float32),
            lax.psum_scatter(
                grad_val_term.reshape(total_len, width).astype(jnp.bfloat16),
                "seq",
                scatter_dimension=0,
                tiled=True,
            ).astype(jnp.float32),
        )
        grad_keys = grad_keys.astype(jnp.bfloat16)
        grad_vals = grad_vals.astype(jnp.bfloat16)
        grad_bias_query = jnp.sum(grad_query.astype(f32), axis=0)
        grad_bias_vals = jnp.sum(grad_vals.astype(f32), axis=0)
        sums[0] = sums[0] + jnp.einsum("sd,se->de", rows_in, grad_query, preferred_element_type=f32)
        sums[1] = sums[1] + jnp.einsum("sd,se->de", rows_in, grad_keys, preferred_element_type=f32)
        sums[2] = sums[2] + jnp.einsum("sd,se->de", rows_in, grad_vals, preferred_element_type=f32)
        sums[6] = sums[6] + jnp.stack(
            [
                grad_bias_query,
                grad_bias_vals,
                grad_bias_out,
                grad_gain1,
                grad_shift1,
                grad_bias2,
                grad_gain2,
                grad_shift2,
            ]
        )
        grad_rows = grad_res1 + jnp.einsum(
            "se,de->sd", grad_query, full_query, preferred_element_type=f32
        )
        grad_rows = grad_rows + jnp.einsum(
            "se,de->sd", grad_keys, full_key, preferred_element_type=f32
        )
        grad_rows = grad_rows + jnp.einsum(
            "se,de->sd", grad_vals, full_value, preferred_element_type=f32
        )
        grad_list.append(grad_rows)
    shares = (
        lax.psum_scatter(sums[0], ("dp", "seq"), scatter_dimension=0, tiled=True),
        lax.psum_scatter(sums[1], ("dp", "seq"), scatter_dimension=0, tiled=True),
        lax.psum_scatter(sums[2], ("dp", "seq"), scatter_dimension=0, tiled=True),
        lax.psum_scatter(sums[3], ("dp", "seq"), scatter_dimension=0, tiled=True),
        lax.psum_scatter(sums[4], ("dp", "seq"), scatter_dimension=0, tiled=True),
        lax.psum_scatter(sums[5], ("dp", "seq"), scatter_dimension=0, tiled=True),
        lax.psum_scatter(sums[6], ("dp", "seq"), scatter_dimension=1, tiled=True),
        lax.psum_scatter(sums[7], ("dp", "seq"), scatter_dimension=0, tiled=True),
    )
    activations = jnp.stack(outputs)[:, None]
    grad_tokens = jnp.stack(grad_list)[:, None]
    return (
        activations,
        grad_tokens,
        shares[0],
        shares[1],
        shares[2],
        shares[3],
        shares[4],
        shares[5],
        shares[6],
        shares[7],
    )


MESH = pl.DeviceIdType.MESH
F32 = jnp.float32
BF16 = jnp.bfloat16
ANY = pl.ANY
VMEM = pltpu.VMEM
LOG2E = math.log2(math.e)
LIMIT = 58 * 1024 * 1024
GELU_C = math.sqrt(2.0 / math.pi)
GELU_A = 0.044715


def nt(a, b):
    return lax.dot_general(a, b, (((1,), (1,)), ((), ())), preferred_element_type=F32)


def nn(a, b):
    return lax.dot_general(a, b, (((1,), (0,)), ((), ())), preferred_element_type=F32)


def tn(a, b):
    return lax.dot_general(a, b, (((0,), (0,)), ((), ())), preferred_element_type=F32)


def place():
    dp = lax.axis_index("dp")
    return dp // 4, (dp // 2) % 2, dp % 2, lax.axis_index("seq")


def device(z, x, c, y):
    return (z * 4 + x * 2 + c, y)


def greet(z, x, c, y):
    barrier = pltpu.get_barrier_semaphore()
    partners = [device(z, x, 1 - c, y), device(z, 1 - x, c, y), device(z, x, c, 1 - y)]
    partners += [device((z + d) % 4, x, c, y) for d in (1, 2, 3)]
    for partner in partners:
        pl.semaphore_signal(barrier, inc=1, device_id=partner, device_id_type=MESH)
    pl.semaphore_wait(barrier, len(partners))


PHASES = 4
LAG = 2
WARM = PHASES * (LAG - 1)
SLOTS = 6


def gather_copies(ref, cross, send, recv, core, phase, pos):
    z, x, c, y = pos
    every = slice(None)
    order = "yzxc" if core == 0 else "zyxc" if cross else "zxyc"
    done = order[:phase]
    have = (
        every if "z" in done else z,
        every if "x" in done else x,
        every if "c" in done else c,
        every if "y" in done else y,
    )
    axis = order[phase]
    if axis == "z":
        targets = [(2 + d, ((z + d) % 4, x, c, y)) for d in (1, 2, 3)]
    elif axis == "x":
        targets = [(0, (z, 1 - x, c, y))]
    elif axis == "y":
        targets = [(1, (z, x, c, 1 - y))]
    else:
        targets = [(2, (z, x, 1 - c, y))]
    return [
        pltpu.make_async_remote_copy(
            src_ref=ref.at[have],
            dst_ref=ref.at[have],
            send_sem=send.at[slot],
            recv_sem=recv.at[slot],
            device_id=device(*target),
            device_id_type=MESH,
        )
        for slot, target in targets
    ]


def gather_phase(ref, cross, send, recv, phase, pos):
    for core in (0, 1):

        @pl.when(pos[2] == core)
        def _():
            if phase > 0:
                for copy in gather_copies(ref, cross, send, recv, core, phase - 1, pos):
                    copy.wait_recv()
            if phase < PHASES:
                for copy in gather_copies(ref, cross, send, recv, core, phase, pos):
                    copy.start()


def gather_sent(ref, cross, send, recv, pos):
    for core in (0, 1):

        @pl.when(pos[2] == core)
        def _():
            for phase in range(PHASES):
                for copy in gather_copies(ref, cross, send, recv, core, phase, pos):
                    copy.wait_send()


class Halves:
    def __init__(self, make):
        self.make = make

    def start(self):
        for h in range(2):
            self.make(h).start()

    def wait(self):
        for h in range(2):
            self.make(h).wait()


def lanes(shape):
    return lax.broadcasted_iota(jnp.int32, shape, len(shape) - 1)


def norm(v):
    center = v - jnp.mean(v, axis=-1, keepdims=True)
    inverse = lax.rsqrt(jnp.mean(center * center, axis=-1, keepdims=True) + EPSILON)
    return center * inverse, inverse


def norm_back(g, normed, inverse, gain):
    gn = g * gain
    inner = gn - jnp.mean(gn, axis=-1, keepdims=True) - normed * jnp.mean(gn * normed, axis=-1, keepdims=True)
    return inner * inverse


def rowsum(v):
    return jnp.sum(v, axis=0, keepdims=True)


def blocks(rows, block, body, straight=False):
    def run(b, carry):
        body(pl.ds(pl.multiple_of(b * block, block), block))
        return carry

    lax.fori_loop(0, rows // block, run, 0, unroll=straight)


def tiles(width, tile, body):
    def run(b, carry):
        body(b, pl.ds(pl.multiple_of(b * tile, tile), tile))
        return carry

    lax.fori_loop(0, width // tile, run, 0)


def forward_kernel(
    wq, wk, wv, wo, wup, wdown, sm, tok, cot, kaug, valid,
    wfq, wfa, wfd, sf, xs_o, quad_o, aug_o, res_o, low_o, act_o, slope_o, back_o, gdn_o, out_o, vec, rows_out,
    xs, ct, quad, aug, res, acc, low, actv, slope, wbuf, dbuf, small, out,
    send, recv, place_sem, own_sem, swap_send, swap_recv, wsem, dsem, out_sem,
):
    pos = place()
    z, x, c, y = pos
    rows, width = xs.shape
    half = rows // 2
    group = 256
    groups = width // group
    wide_from = 2 * groups
    tall_from = wide_from + 10
    chunks = tall_from + 8

    first = []

    def put(src, dst):
        first.append(pltpu.make_async_copy(src, dst, place_sem.at[len(first)]))

    for h in range(2):
        top = slice(16 * h, 16 * h + 16)
        for g in range(groups):
            for k, w in enumerate((wq, wk, wv)):
                put(
                    w.at[top, group * g : group * (g + 1)],
                    wfq.at[g, h, z, x, c, y, :, pl.ds(group * k, group)],
                )
        put(wo.at[top], wfa.at[0, h, z, x, c, y])
        for j in range(4):
            put(wup.at[top, width * j : width * (j + 1)], wfa.at[1 + j, h, z, x, c, y])
            put(wdown.at[64 * h : 64 * h + 64, 256 * j : 256 * (j + 1)], wfd.at[j, h, z, x, c, y])
    put(sm, sf.at[z, x, c, y])
    for copy in first:
        copy.start()
    mine = [
        pltpu.make_async_copy(tok.at[y, 0], xs.at[pl.ds(0, half)], own_sem.at[0]),
        pltpu.make_async_copy(cot.at[y, 0], ct.at[pl.ds(0, half)], own_sem.at[1]),
    ]
    for copy in mine:
        copy.start()
    greet(*pos)
    for copy in first:
        copy.wait()

    piece = half // 8

    def swap(src, dst, slot, index):
        at = pl.multiple_of(index * piece, piece)
        return pltpu.make_async_remote_copy(
            src_ref=src.at[1 - y, 0, pl.ds(at, piece)],
            dst_ref=dst.at[pl.ds(half + at, piece)],
            send_sem=swap_send.at[slot, index],
            recv_sem=swap_recv.at[slot, index],
            device_id=device(z, x, c, 1 - y),
            device_id_type=MESH,
        )

    def chunk(index, kind):
        odd = index % 2
        if kind == 0:
            ref = wfq.at[index // 2, odd]
        elif kind == 1:
            ref = wfa.at[(index - wide_from) // 2, odd]
        else:
            ref = wfd.at[(index - tall_from) // 2, odd]
        return (ref, kind == 0, send.at[index], recv.at[index])

    tiny = (sf, False, send.at[chunks], recv.at[chunks])

    def kinds(index, body):
        for kind, (start, stop) in enumerate(((0, wide_from), (wide_from, tall_from), (tall_from, chunks))):

            @pl.when((index >= start) & (index < stop))
            def _():
                body(chunk(index, kind))

    def step(t, carry):
        for phase in range(PHASES + 1):
            index = t - LAG * phase
            kinds(index, lambda parts: gather_phase(*parts, phase, pos))

            @pl.when(index == 0)
            def _():
                gather_phase(*tiny, phase, pos)

        @pl.when(t < 4)
        def _():
            swap(tok, xs, 0, 2 * t).start()
            swap(tok, xs, 0, 2 * t + 1).start()

        @pl.when((t >= 12) & (t < 20))
        def _():
            swap(cot, ct, 1, t - 12).start()

        return carry

    def advance(start, stop):
        lax.fori_loop(start, stop, step, 0)

    def weight(index, slot):
        return Halves(lambda h: pltpu.make_async_copy(wfa.at[index, h], wbuf.at[slot, :, :, :, :, h], wsem.at[slot, h]))

    def trio(g):
        return Halves(
            lambda h: pltpu.make_async_copy(
                wfq.at[g, h], wbuf.at[0, :, :, :, :, h, :, pl.ds(0, 3 * group)], wsem.at[0, h]
            )
        )

    def square(slot, cols):
        return wbuf[slot, :, :, :, :, :, :, cols].reshape(width, cols.size)

    def save(src, dst, slot):
        copy = pltpu.make_async_copy(src, dst, out_sem.at[slot])
        copy.start()
        return copy

    advance(0, 6 + WARM)
    trio(0).start()
    for index in range(8):
        swap(tok, xs, 0, index).wait_recv()
    for copy in mine:
        copy.wait()
    saves = [save(xs, xs_o, 0)]
    gathered = pltpu.make_async_copy(sf, small, own_sem.at[2])
    gathered.start()
    gathered.wait()
    tiles32 = [small[a, b, d, e].astype(F32) for a in range(4) for b in range(2) for d in range(2) for e in range(2)]
    for g in range(8):
        vec[0:8, 128 * g : 128 * g + 128] = sum(tiles32[4 * g + s] for s in range(4))[0:8]
    for r in range(4):
        for g in range(8):
            vec[8 + r : 9 + r, 128 * g : 128 * g + 128] = tiles32[8 * r + g][8:9]
    vec[12:16, :] = jnp.zeros((4, width), F32)

    block = 256
    low1 = (lanes((1, 128)) < 64).astype(F32).astype(BF16)
    high1 = (lanes((1, 128)) >= 64).astype(F32).astype(BF16)
    ones1 = (lanes((1, 128)) % 64 == 0).astype(F32).astype(BF16)
    qlane = lanes((block, 128))
    sixty = qlane % 64

    def heads(g, at):
        def run(n, carry):
            pair(g, at, n)
            advance(WARM + 6 + 3 * g + n, WARM + 7 + 3 * g + 2 * n)
            return carry

        lax.fori_loop(0, 2, run, 0)

    def pair(g, at, n):
        local = pl.multiple_of(n * 128, 128)
        qc, kc, vc, cc = (pl.ds(local + group * k, 128) for k in range(4))
        cols = pl.ds(pl.multiple_of(g * group + n * 128, 128), 128)
        k2 = quad[g, :, kc]
        v2 = quad[g, :, vc]
        ka = k2 * low1 + kaug[...] * high1
        kb = k2 * high1 + kaug[...] * low1

        def query_block(sl):
            q2 = quad[g, sl, qc]
            parts = []
            for own, other, kk in ((low1, high1, ka), (high1, low1, kb)):
                s = nt(q2 * own + ones1 * other, kk)
                top = jnp.max(s, axis=1, keepdims=True)
                e = jnp.exp2(s - top)
                total = jnp.sum(e, axis=1, keepdims=True)
                o = nn(e.astype(BF16), v2)
                parts.append((o / total, -(top + jnp.log2(total))))
            lower = qlane < 64
            quad[g, sl, cc] = jnp.where(lower, parts[0][0], parts[1][0]).astype(BF16)
            neg = jnp.where(lower, parts[1][1], parts[0][1])
            hi = neg.astype(BF16).astype(F32)
            mid = (neg - hi).astype(BF16).astype(F32)
            lo = neg - hi - mid
            aug[sl, cols] = jnp.where(
                sixty == 0,
                1.0,
                jnp.where(sixty == 1, hi, jnp.where(sixty == 2, mid, jnp.where(sixty == 3, lo, 0.0))),
            ).astype(BF16)

        blocks(rows, block, query_block, True)

    def attend(g, carry):
        trio(g).wait()
        at = pl.ds(pl.multiple_of(g * group, group), group)
        for k in range(3):
            out_k = nn(xs[...], square(0, pl.ds(group * k, group)))
            if k == 0:
                out_k = (out_k + vec[0:1, at]) * (LOG2E / 8.0)
            elif k == 2:
                out_k = out_k + vec[1:2, at]
            quad[g, :, group * k : group * (k + 1)] = out_k.astype(BF16)
        heads(g, at)

        @pl.when(g < groups - 1)
        def _():
            trio(g + 1).start()

        return carry

    lax.fori_loop(0, groups, attend, 0)
    weight(0, 1).start()
    for g in range(groups):
        saves.append(save(quad.at[g], quad_o.at[g], 1 + g))
    saves.append(save(aug, aug_o, 5))
    weight(0, 1).wait()

    def project_out(n, cols):
        total = vec[2:3, cols]
        for g in range(groups):
            total = total + nn(quad[g, :, 3 * group : 4 * group], wbuf[1, g, :, :, :, :, :, cols].reshape(group, group))
        res[:, cols] = xs[:, cols].astype(F32) + total

    tiles(width, 256, project_out)
    weight(1, 0).start()
    saves.append(save(res, res_o, 6))

    def normalize(sl):
        normed, _ = norm(res[sl, :])
        low[sl, :] = (normed * vec[3:4, :] + vec[4:5, :]).astype(BF16)

    blocks(rows, block, normalize)
    saves.append(save(low, low_o, 7))

    def shaft(j, slot):
        return Halves(lambda h: pltpu.make_async_copy(wfd.at[j, h], dbuf.at[slot, :, :, :, :, h], dsem.at[slot, h]))

    for j in range(4):
        weight(1 + j, j % 2).wait()

        def climb(n, cols):
            up = nn(low[...], square(j % 2, cols)) + vec[8 + j : 9 + j, cols]
            sq = up * up
            t = jnp.tanh(up * (GELU_C + (GELU_C * GELU_A) * sq))
            hf = 0.5 * up
            actv[j, :, cols] = (hf + hf * t).astype(BF16)
            slope[j, :, cols] = (
                0.5 + 0.5 * t + hf * (1.0 - t * t) * (GELU_C + (3.0 * GELU_C * GELU_A) * sq)
            ).astype(BF16)

            @pl.when(n == 1)
            def _():
                advance(WARM + 18 + 2 * j, WARM + 19 + 2 * j)

        tiles(width, 256, climb)
        advance(WARM + 19 + 2 * j, WARM + 20 + 2 * j)
        if j < 3:
            weight(2 + j, (1 + j) % 2).start()
        else:
            shaft(0, 0).start()
        saves.append(save(actv.at[j], act_o.at[j], 8 + j))
        saves.append(save(slope.at[j], slope_o.at[j], 12 + j))

    for j in range(4):
        shaft(j, j % 2).wait()
        cols = slice(256 * j, 256 * (j + 1))

        def slide(k, carry):
            part = nn(actv[k], dbuf[j % 2, k].reshape(width, 256))

            @pl.when(k == 0)
            def _():
                acc[:, cols] = part + vec[5:6, cols]

            @pl.when(k > 0)
            def _():
                acc[:, cols] += part

            return carry

        lax.fori_loop(0, 4, slide, 0)
        if j < 3:
            advance(WARM + 26 + 2 * j, min(WARM + 28 + 2 * j, chunks + LAG * PHASES))
            shaft(1 + j, (1 + j) % 2).start()

    for index in range(8):
        swap(cot, ct, 1, index).wait_recv()
    rows_out[...] = jnp.zeros_like(rows_out)

    def middle(sl):
        normed, _ = norm(res[sl, :])
        hidden = normed * vec[3:4, :] + vec[4:5, :]
        normed, inverse = norm(hidden + acc[sl, :])
        ok = valid[sl, 0:1]
        out[sl, :] = ((normed * vec[6:7, :] + vec[7:8, :]) * ok).astype(BF16)
        g = ct[sl, :].astype(F32) * ok
        back = norm_back(g, normed, inverse, vec[6:7, :])
        acc[sl, :] = back
        gd = back.astype(BF16)
        ct[sl, :] = gd
        rows_out[6:7, :] += rowsum(g * normed)
        rows_out[7:8, :] += rowsum(g)
        rows_out[5:6, :] += rowsum(gd.astype(F32))

    blocks(rows, block, middle)
    saves.append(save(out, out_o, 16))
    saves.append(save(acc, back_o, 17))
    saves.append(save(ct, gdn_o, 18))

    def finish(index, carry):
        kinds(index, lambda parts: gather_sent(*parts, pos))
        return carry

    lax.fori_loop(0, chunks, finish, 0)
    gather_sent(*tiny, pos)
    for slot, (src, dst) in enumerate(((tok, xs), (cot, ct))):
        for index in range(8):
            swap(src, dst, slot, index).wait_send()
    for copy in saves:
        copy.wait()


def forward_pass(weights, sm, tok, cot, kaug, valid):
    width = tok.shape[3]
    rows = 2 * tok.shape[2]
    low = jax.ShapeDtypeStruct((rows, width), BF16)
    full = jax.ShapeDtypeStruct((rows, width), F32)
    wide = jax.ShapeDtypeStruct((4, rows, width), BF16)
    six = (4, 2, 2, 2)
    vmem = pl.BlockSpec(memory_space=VMEM)
    hbm = pl.BlockSpec(memory_space=ANY)
    dma = pltpu.SemaphoreType.DMA
    return pl.pallas_call(
        forward_kernel,
        out_shape=(
            jax.ShapeDtypeStruct((4, 2) + six + (16, 768), BF16),
            jax.ShapeDtypeStruct((5, 2) + six + (16, width), BF16),
            jax.ShapeDtypeStruct((4, 2) + six + (64, 256), BF16),
            jax.ShapeDtypeStruct(six + (16, 128), BF16),
            low, wide, low, full, low, wide, wide, full, low, low,
            jax.ShapeDtypeStruct((16, width), F32),
            jax.ShapeDtypeStruct((8, width), F32),
        ),
        in_specs=[vmem] * 7 + [hbm] * 2 + [vmem] * 2,
        out_specs=[hbm] * 14 + [vmem] * 2,
        scratch_shapes=[
            VMEM((rows, width), BF16),
            VMEM((rows, width), BF16),
            VMEM((4, rows, width), BF16),
            VMEM((rows, width), BF16),
            VMEM((rows, width), F32),
            VMEM((rows, width), F32),
            VMEM((rows, width), BF16),
            VMEM((4, rows, width), BF16),
            VMEM((4, rows, width), BF16),
            VMEM((2,) + six + (2, 16, width), BF16),
            VMEM((2,) + six + (2, 64, 256), BF16),
            VMEM(six + (16, 128), BF16),
            VMEM((rows, width), BF16),
            dma((27, SLOTS)),
            dma((27, SLOTS)),
            dma((43,)),
            dma((3,)),
            dma((2, 8)),
            dma((2, 8)),
            dma((2, 2)),
            dma((2, 2)),
            dma((19,)),
        ],
        compiler_params=pltpu.CompilerParams(collective_id=0, has_side_effects=True, vmem_limit_bytes=LIMIT),
        cost_estimate=pl.CostEstimate(flops=2 * 14 * rows * width * width, bytes_accessed=90 << 20, transcendentals=1 << 24),
        name="forward_pass",
    )(*weights, sm, tok, cot, kaug, valid)


CHUNKS = 26
WIDE = 18
DEPTH = 6
LAST = CHUNKS - 1


def ways(core, index):
    full = 1024 if index < WIDE else 768
    mode = 0 if core == 0 or index >= CHUNKS - 4 else 2 if index >= WIDE else 1
    return ((mode, 0, full),)


def scatter_copies(way, part, phase, grad, bufs, send, recv, pos):
    z, x, c, y = pos
    mode, start, size = way
    cols = pl.ds(start, size)
    b0, b1, b2, b3 = bufs
    every = slice(None)

    def remote(src, dst, slot, target):
        return pltpu.make_async_remote_copy(
            src_ref=src,
            dst_ref=dst,
            send_sem=send.at[6 * part + slot],
            recv_sem=recv.at[6 * part + slot],
            device_id=device(*target),
            device_id_type=MESH,
        )

    across = (z, 1 - x, c, y)
    beside = (z, x, c, 1 - y)
    if phase == 0:
        return [remote(grad.at[:, :, 1 - c, :, :, cols], b0.at[:, :, :, :, cols], 2, (z, x, 1 - c, y))]
    if phase == 1:
        if mode == 1:
            return [remote(b0.at[:, :, 1 - y, :, cols], b1.at[:, :, :, cols], 1, beside)]
        return [remote(b0.at[:, 1 - x, :, :, cols], b1.at[:, :, :, cols], 0, across)]
    if phase == 2:
        if mode == 0:
            return [
                remote(
                    b1.at[(z + d) % 4, :, :, cols],
                    b2.at[pl.ds(2 * (d - 1), 2), :, cols],
                    2 + d,
                    ((z + d) % 4, x, c, y),
                )
                for d in (1, 2, 3)
            ]
        if mode == 1:
            return [remote(b1.at[:, 1 - x, :, cols], b2.at[pl.ds(0, 4), :, cols], 0, across)]
        return [remote(b1.at[:, 1 - y, :, cols], b2.at[pl.ds(0, 4), :, cols], 1, beside)]
    if mode == 0:
        return [remote(b1.at[z, 1 - y, :, cols], b3.at[0, :, cols], 1, beside)]
    return [
        remote(b2.at[(z + d) % 4, :, cols], b3.at[d - 1, :, cols], 2 + d, ((z + d) % 4, x, c, y)) for d in (1, 2, 3)
    ]


def scatter_add(way, phase, own, bufs, out, pos):
    z, x, c, y = pos
    mode, start, size = way
    cols = pl.ds(start, size)
    b0, b1, b2, b3 = bufs

    def plus(a, b):
        return (a.astype(F32) + b.astype(F32)).astype(BF16)

    def each(body):
        def run(zz, carry):
            body(zz)
            return carry

        lax.fori_loop(0, 4, run, 0)

    if phase == 0:

        def body(zz):
            b0[zz, :, :, :, cols] = plus(own[zz, :, :, :, cols], b0[zz, :, :, :, cols])

        each(body)
    elif phase == 1:

        def body(zz):
            kept = b0[zz, :, y, :, cols] if mode == 1 else b0[zz, x, :, :, cols]
            b1[zz, :, :, cols] = plus(kept, b1[zz, :, :, cols])

        each(body)
    elif mode == 0:
        if phase == 2:
            total = b1[z, :, :, cols].astype(F32)
            for d in range(3):
                total = total + b2[pl.ds(2 * d, 2), :, cols].astype(F32)
            b1[z, :, :, cols] = total.astype(BF16)
        else:
            out[:, cols] = b1[z, y, :, cols].astype(F32) + b3[0, :, cols].astype(F32)
    elif phase == 2:

        def body(zz):
            kept = b1[zz, x, :, cols] if mode == 1 else b1[zz, y, :, cols]
            b2[zz, :, cols] = plus(kept, b2[zz, :, cols])

        each(body)
    else:
        total = b2[z, :, cols].astype(F32)
        for d in range(3):
            total = total + b3[d, :, cols].astype(F32)
        out[:, cols] = total


def scatter_phase(phase, plan, full, grad, own, own_sem, bufs, out, send, recv, credit, index, pos):
    z, x, c, y = pos
    cols = pl.ds(0, full)

    def mine():
        return pltpu.make_async_copy(grad.at[:, :, c, :, :, cols], own.at[:, :, :, :, cols], own_sem)

    if phase == 0:
        mine().start()
        if credit is not None:

            @pl.when(index >= DEPTH)
            def _():
                pl.semaphore_wait(credit, 1)

    if phase == 1:
        mine().wait()
    for core in (0, 1):

        @pl.when(c == core)
        def _():
            def copies(phase):
                return [
                    copy
                    for part, way in enumerate(plan[core] if phase > 0 else ((0, 0, full),))
                    for copy in scatter_copies(way, part, phase, grad, bufs, send, recv, pos)
                ]

            if phase > 0:
                for copy in copies(phase - 1):
                    copy.wait_recv()
                if phase == 2:
                    for copy in copies(1):
                        copy.wait_send()
                for way in plan[core]:
                    scatter_add(way, phase - 1, own, bufs, out, pos)
            if phase < PHASES:
                for copy in copies(phase):
                    copy.start()

    if phase == 2 and credit is not None:

        @pl.when(index < CHUNKS - DEPTH)
        def _():
            pl.semaphore_signal(credit, inc=1, device_id=device(z, x, 1 - c, y), device_id_type=MESH)


def scatter_sent(plan, full, grad, bufs, send, recv, pos):
    for core in (0, 1):

        @pl.when(pos[2] == core)
        def _():
            for phase in (0, 2, 3):
                for part, way in enumerate(plan[core] if phase > 0 else ((0, 0, full),)):
                    for copy in scatter_copies(way, part, phase, grad, bufs, send, recv, pos):
                        copy.wait_send()


SMALL = (((0, 0, 128),), ((1, 0, 128),))


def backward_kernel(
    wfq, wfa, wfd, xs_i, quad_i, aug_i, res_i, low_i, act_i, slope_i, back_i, gdn_i, out_i, vec, rows_in, kaug,
    gw, act_o, gtok_o, outs, small_out,
    acc, rbuf, gdn, low, quad, duo, wbuf, dbuf, stage, own, b0, b1, b2, b3, home, rows_sum, bias_sum,
    small_g, small_own, s0, s1, s2, s3,
    send, recv, own_sem, credit, swap_send, swap_recv, load_sem, wsem, dsem, stage_sem, out_sem,
):
    pos = place()
    z, x, c, y = pos
    rows, width = acc.shape
    half = rows // 2
    block = 256
    group = 256
    groups = width // group
    piece = half // 8

    def load(src, dst, slot):
        return pltpu.make_async_copy(src, dst, load_sem.at[slot])

    loads = [load(act_i.at[k], quad.at[k], k) for k in range(4)]
    loads += [load(gdn_i, gdn, 4), load(low_i, low, 5), load(back_i, acc, 6)]
    loads += [load(out_i.at[pl.ds(0, half)], duo.at[1, pl.ds(0, half)], 7), load(slope_i.at[0], duo.at[0], 8)]
    for k in (4, 0, 1, 2, 3, 5, 6, 7, 8):
        loads[k].start()
    greet(*pos)

    def away(index):
        at = pl.multiple_of(index * piece, piece)
        return pltpu.make_async_remote_copy(
            src_ref=out_i.at[pl.ds(half + at, piece)],
            dst_ref=act_o.at[y, 0, pl.ds(at, piece)],
            send_sem=swap_send.at[index],
            recv_sem=swap_recv.at[index],
            device_id=device(z, x, c, 1 - y),
            device_id_type=MESH,
        )

    kinds = ((0, WIDE, 1024), (WIDE, CHUNKS - 4, 768), (CHUNKS - 4, CHUNKS, 768))

    def chunk(index):
        slot = index % DEPTH
        bufs = (b0.at[slot], b1.at[index], b2.at[index], b3.at[index])
        return gw.at[index // 2, index % 2], bufs, send.at[index], recv.at[index]

    small_bufs = (s0, s1, s2, s3)

    def step(t, carry):
        for phase in range(PHASES + 1):
            index = t - LAG * phase
            for first, stop, full in kinds:

                @pl.when((index >= first) & (index < stop))
                def _():
                    grad, bufs, sends, recvs = chunk(index)
                    scatter_phase(
                        phase, (ways(0, first), ways(1, first)), full, grad, own.at[index % 3], own_sem.at[index % 3],
                        bufs, outs.at[index], sends, recvs, credit, index, pos,
                    )

            @pl.when(index == LAST)
            def _():
                scatter_phase(
                    phase, SMALL, 128, small_g, small_own, own_sem.at[3], small_bufs, small_out,
                    send.at[CHUNKS], recv.at[CHUNKS], None, 0, pos,
                )

        @pl.when(t < 8)
        def _():
            away(t).start()

        return carry

    def advance(start, stop):
        lax.fori_loop(start, stop, step, 0)

    def weight(index, slot):
        return Halves(lambda h: pltpu.make_async_copy(wfa.at[index, h], wbuf.at[slot, :, :, :, :, h], wsem.at[slot, h]))

    def trio(g, slot):
        return Halves(
            lambda h: pltpu.make_async_copy(
                wfq.at[g, h], wbuf.at[slot, :, :, :, :, h, :, pl.ds(0, 3 * group)], wsem.at[slot, h]
            )
        )

    def shaft(j, slot):
        return Halves(
            lambda h: pltpu.make_async_copy(wfd.at[:, h, j], dbuf.at[slot, :, :, :, :, h], dsem.at[slot, h])
        )

    def store(index, slot):
        return Halves(
            lambda h: pltpu.make_async_copy(stage.at[slot, :, :, :, :, h], gw.at[index, h], stage_sem.at[slot, h])
        )

    weight(1, 0).start()
    shaft(0, 0).start()
    rows_sum[...] = rows_in[...]
    bias_sum[...] = jnp.zeros_like(bias_sum)

    for k in (4, 0, 1, 2, 3):
        loads[k].wait()
    for jj in range(4):
        slot = jj % 2
        if jj >= 2:
            store(jj - 2, slot).wait()

        def quarter(k, carry):
            part = tn(quad[k], gdn[:, 256 * jj : 256 * (jj + 1)]).astype(BF16).reshape(2, 2, 2, 4, 2, 16, 256)
            for q in range(4):
                stage[slot, k, :, :, :, :, :, 256 * q : 256 * (q + 1)] = part[:, :, :, q]
            return carry

        lax.fori_loop(0, 4, quarter, 0)
        store(jj, slot).start()
        if jj >= 2:
            advance(jj - 2, jj - 1)
    loads[5].wait()
    loads[6].wait()
    loads[7].wait()
    keep = pltpu.make_async_copy(duo.at[1, pl.ds(0, half)], act_o.at[y, 0], out_sem.at[0])
    keep.start()
    for k in range(4):
        load(quad_i.at[k], quad.at[k], k).start()
    small_block = 128
    load(res_i.at[pl.ds(0, small_block)], rbuf.at[0], 9).start()

    def slope_load(j):
        return load(slope_i.at[j], duo.at[j % 2], 8 - j % 2)

    def square_rows(slot, n):
        return wbuf[slot, n].reshape(256, width)

    for j in range(4):
        slot = j % 2
        slope_load(j).wait()
        shaft(j, slot).wait()
        if j == 0:
            keep.wait()
        if j < 3:
            slope_load(j + 1).start()
            weight(2 + j, 1 - slot).start()
            shaft(j + 1, 1 - slot).start()
        for n in range(4):
            cols = slice(256 * n, 256 * (n + 1))
            total = nt(gdn[:, 0:256], dbuf[slot, 0, n // 2, n % 2].reshape(256, 256))
            for jj in range(1, 4):
                total = total + nt(
                    gdn[:, 256 * jj : 256 * (jj + 1)], dbuf[slot, jj, n // 2, n % 2].reshape(256, 256)
                )
            gu = (duo[slot, :, cols].astype(F32) * total).astype(BF16)
            duo[slot, :, cols] = gu
            bias_sum[8 * j : 8 * j + 1, cols] = rowsum(gu.astype(F32))
        store(2 + j, slot).wait()
        advance(2 + 2 * j, 3 + 2 * j)

        def up_grad(n, cols):
            part = tn(low[...], duo[slot, :, cols]).astype(BF16)
            stage[slot, :, :, :, :, :, :, cols] = part.reshape(4, 2, 2, 2, 2, 16, 256)

        tiles(width, 256, up_grad)
        store(4 + j, slot).start()
        advance(3 + 2 * j, 4 + 2 * j)
        weight(1 + j, slot).wait()
        for n in range(4):
            cols = slice(256 * n, 256 * (n + 1))
            acc[:, cols] += nt(duo[slot], square_rows(slot, n))
    weight(0, 0).start()
    load(xs_i, duo.at[0], 8).start()
    load(aug_i, duo.at[1], 7).start()

    def first_norm(b, carry):
        sl = pl.ds(pl.multiple_of(b * small_block, small_block), small_block)

        @pl.when(b + 1 < rows // small_block)
        def _():
            after = pl.ds(pl.multiple_of((b + 1) * small_block, small_block), small_block)
            load(res_i.at[after], rbuf.at[(b + 1) % 2], 9 + (b + 1) % 2).start()

        load(res_i.at[sl], rbuf.at[b % 2], 9 + b % 2).wait()
        normed, inverse = norm(rbuf[b % 2])
        g = acc[sl, :]
        back = norm_back(g, normed, inverse, vec[3:4, :])
        acc[sl, :] = back
        gat = back.astype(BF16)
        gdn[sl, :] = gat
        rows_sum[3:4, :] += rowsum(g * normed)
        rows_sum[4:5, :] += rowsum(g)
        rows_sum[2:3, :] += rowsum(gat.astype(F32))
        return carry

    lax.fori_loop(0, rows // small_block, first_norm, 0)
    store(6, 0).wait()
    advance(10, 11)
    for k in range(4):
        load(quad_i.at[k], quad.at[k], k).wait()

    for g in range(groups):
        for n in range(4):
            cols = slice(256 * n, 256 * (n + 1))
            part = tn(quad[g, :, 3 * group : 4 * group], gdn[:, cols]).astype(BF16)
            stage[0, g, :, :, :, :, :, cols] = part.reshape(2, 2, 2, 2, 16, 256)
    store(8, 0).start()
    weight(0, 0).wait()
    for n in range(4):
        low[:, 256 * n : 256 * (n + 1)] = nt(gdn[...], square_rows(0, n)).astype(BF16)
    store(7, 1).wait()
    advance(11, 12)
    trio(0, 0).start()
    load(xs_i, duo.at[0], 8).wait()
    load(aug_i, duo.at[1], 7).wait()
    store(8, 0).wait()

    xs, aug = duo.at[0], duo.at[1]
    low1 = (lanes((1, 128)) < 64).astype(F32).astype(BF16)
    high1 = (lanes((1, 128)) >= 64).astype(F32).astype(BF16)
    ones1 = (lanes((1, 128)) % 64 < 2).astype(F32).astype(BF16)
    alane = lanes((rows, 128))
    lower = alane < 64
    sixty = alane % 64

    def pair(g, n):
        local = pl.multiple_of(n * 128, 128)
        qc, kc, vc, cc = (pl.ds(local + group * k, 128) for k in range(4))
        cols = pl.ds(pl.multiple_of(g * group + n * 128, 128), 128)
        q2 = quad[g, :, qc]
        k2 = quad[g, :, kc]
        v2 = quad[g, :, vc]
        g2 = low[:, cols]
        au = aug[:, cols]
        prod = g2.astype(F32) * quad[g, :, cc].astype(F32)
        da = -jnp.sum(jnp.where(lower, prod, 0.0), axis=1, keepdims=True)
        db = -jnp.sum(jnp.where(lower, 0.0, prod), axis=1, keepdims=True)
        neg = jnp.where(lower, db, da)
        hi = neg.astype(BF16).astype(F32)
        daug = jnp.where(sixty == 0, hi, jnp.where(sixty == 1, neg - hi, 0.0)).astype(BF16)
        gq = []
        gk = []
        gv = []
        for head in range(2):
            mine, other = (low1, high1) if head == 0 else (high1, low1)
            qa = q2 * mine + au * other
            ga = g2 * mine + daug * other
            ka = k2 * mine + kaug[...] * other
            va = v2 * mine + ones1 * other
            parts = []
            for b in range(rows // block):
                sl = slice(b * block, (b + 1) * block)
                p = jnp.exp2(nt(ka, qa[sl]))
                ds = (p * nt(va, ga[sl])).astype(BF16)
                new_v = nn(p.astype(BF16), g2[sl])
                new_k = nn(ds, q2[sl])
                sum_v = new_v if b == 0 else sum_v + new_v
                sum_k = new_k if b == 0 else sum_k + new_k
                parts.append(tn(k2, ds))
            gq.append(parts)
            gk.append(sum_k)
            gv.append(sum_v)
        quad[g, :, kc] = (jnp.where(lower, gk[0], gk[1]) * (1.0 / LOG2E)).astype(BF16)
        quad[g, :, vc] = jnp.where(lower, gv[0], gv[1]).astype(BF16)
        for b in range(rows // block):
            sl = slice(b * block, (b + 1) * block)
            both = jnp.concatenate([gq[0][b][0:64], gq[1][b][64:128]], axis=0) * 0.125
            quad[g, sl, qc] = both.T.astype(BF16)

    def token_rows(g, slot, sl):
        for n in range(4):
            cols = slice(256 * n, 256 * (n + 1))
            acc[sl, cols] += nt(quad[g, sl, 0 : 3 * group], wbuf[slot, n, :, :, :, :, :, 0 : 3 * group].reshape(256, 3 * group))

    def trio_grad(g):
        at = pl.ds(pl.multiple_of(g * group, group), group)
        for k in range(3):
            part = tn(xs[...], quad[g, :, group * k : group * (k + 1)]).astype(BF16)
            stage[1, :, :, :, :, :, :, group * k : group * (k + 1)] = part.reshape(4, 2, 2, 2, 2, 16, group)
        rows_sum[0:1, at] = rowsum(quad[g, :, 0:group].astype(F32))
        rows_sum[1:2, at] = rowsum(quad[g, :, 2 * group : 3 * group].astype(F32))

    def attend(g, carry):
        def run(n, carry):
            @pl.when((g > 0) & (n == 1))
            def _():
                store(8 + g, 1).wait()

            @pl.when(g + n > 0)
            def _():
                advance(11 + 3 * g + n, 12 + 3 * g + n)

            pair(g, n)
            return carry

        lax.fori_loop(0, 2, run, 0)
        advance(13 + 3 * g, 14 + 3 * g)

        @pl.when(g < groups - 1)
        def _():
            trio(g, 0).wait()
            token_rows(g, 0, slice(0, rows))
            trio(g + 1, 0).start()

            trio_grad(g)
            store(9 + g, 1).start()

        return carry

    lax.fori_loop(0, groups, attend, 0)
    last = groups - 1

    advance(LAST - 2, LAST - 1)
    trio(last, 0).wait()
    token_rows(last, 0, slice(half, rows))
    low[0:half, :] = acc[half:rows, :].astype(BF16)
    turn = pltpu.make_async_remote_copy(
        src_ref=low.at[pl.ds(0, half)],
        dst_ref=home,
        send_sem=swap_send.at[8],
        recv_sem=swap_recv.at[8],
        device_id=device(z, x, c, 1 - y),
        device_id_type=MESH,
    )
    turn.start()
    trio_grad(last)
    store(9 + last, 1).start()
    for zz in range(4):
        for s in range(8):
            at = 2 * zz + s // 4
            tile = jnp.concatenate(
                [
                    rows_sum[:, 128 * at : 128 * (at + 1)],
                    bias_sum[8 * zz : 8 * zz + 8, 128 * s : 128 * (s + 1)],
                ],
                axis=0,
            )
            small_g[zz, s // 4, (s // 2) % 2, s % 2] = tile.astype(BF16)
    store(9 + last, 1).wait()
    advance(LAST - 1, LAST + 1)
    token_rows(last, 0, slice(0, half))
    kept = pltpu.make_async_copy(acc.at[pl.ds(0, half)], gtok_o.at[y, 0], out_sem.at[0])
    kept.start()
    advance(LAST + 1, LAST + LAG * PHASES + 1)
    turn.wait()
    acc[half:rows, :] = home[...].astype(F32)
    came = pltpu.make_async_copy(acc.at[pl.ds(half, half)], gtok_o.at[1 - y, 0], out_sem.at[1])
    came.start()
    for index in range(8):
        away(index).wait()

    def finish(index, carry):
        for first, stop, full in kinds:

            @pl.when((index >= first) & (index < stop))
            def _():
                grad, bufs, sends, recvs = chunk(index)
                scatter_sent((ways(0, first), ways(1, first)), full, grad, bufs, sends, recvs, pos)

        return carry

    lax.fori_loop(0, CHUNKS, finish, 0)
    scatter_sent(SMALL, 128, small_g, small_bufs, send.at[CHUNKS], recv.at[CHUNKS], pos)
    kept.wait()
    came.wait()


def backward_pass(wfq, wfa, wfd, saved, vec, rows_in, kaug):
    rows, width = saved[0].shape
    six = (4, 2, 2, 2)
    vmem = pl.BlockSpec(memory_space=VMEM)
    hbm = pl.BlockSpec(memory_space=ANY)
    dma = pltpu.SemaphoreType.DMA

    def buffers(rows, width, depth, count):
        return [
            VMEM(depth + (4, 2, 2, rows, width), BF16),
            VMEM(count + (4, 2, rows, width), BF16),
            VMEM(count + (6, rows, width), BF16),
            VMEM(count + (3, rows, width), BF16),
        ]

    return pl.pallas_call(
        backward_kernel,
        out_shape=(
            jax.ShapeDtypeStruct((CHUNKS // 2, 2) + six + (16, width), BF16),
            jax.ShapeDtypeStruct((2, 1, rows // 2, width), BF16),
            jax.ShapeDtypeStruct((2, 1, rows // 2, width), F32),
            jax.ShapeDtypeStruct((CHUNKS, 16, width), F32),
            jax.ShapeDtypeStruct((16, 128), F32),
        ),
        in_specs=[hbm] * 13 + [vmem] * 3,
        out_specs=[hbm] * 3 + [vmem] * 2,
        scratch_shapes=[
            VMEM((rows, width), F32),
            VMEM((2, 128, width), F32),
            VMEM((rows, width), BF16),
            VMEM((rows, width), BF16),
            VMEM((4, rows, width), BF16),
            VMEM((2, rows, width), BF16),
            VMEM((2,) + six + (2, 16, width), BF16),
            VMEM((2, 4, 2, 2, 2, 2, 64, 256), BF16),
            VMEM((2,) + six + (2, 16, width), BF16),
            VMEM((3, 4, 2, 2, 16, width), BF16),
        ]
        + buffers(16, width, (DEPTH,), (CHUNKS,))
        + [
            VMEM((rows // 2, width), BF16),
            VMEM((8, width), F32),
            VMEM((32, width), F32),
            VMEM(six + (16, 128), BF16),
            VMEM((4, 2, 2, 16, 128), BF16),
        ]
        + buffers(16, 128, (), ())
        + [
            dma((CHUNKS + 1, SLOTS)),
            dma((CHUNKS + 1, SLOTS)),
            dma((4,)),
            pltpu.SemaphoreType.REGULAR,
            dma((9,)),
            dma((9,)),
            dma((11,)),
            dma((2, 2)),
            dma((2, 2)),
            dma((2, 2)),
            dma((2,)),
        ],
        compiler_params=pltpu.CompilerParams(collective_id=1, has_side_effects=True, vmem_limit_bytes=61 * 1024 * 1024),
        cost_estimate=pl.CostEstimate(flops=2 * 32 * rows * width * width, bytes_accessed=90 << 20, transcendentals=1 << 24),
        name="backward_pass",
    )(wfq, wfa, wfd, *saved, vec, rows_in, kaug)


def paired(
    tokens, lengths, w_query, w_key, w_value, w_out, w_up, w_down, vectors, up_bias, cotangent
):
    half, width = tokens.shape[2:]
    rows = 2 * half
    y = lax.axis_index("seq")
    rank = lax.axis_index("dp") * 2 + y
    spot = jnp.tile(vectors, (1, 4)) * (jnp.arange(128) // 32 == rank % 4).astype(BF16)
    sm = jnp.concatenate([spot, up_bias[None, :], jnp.zeros((7, 128), BF16)])
    length = lax.dynamic_index_in_dim(lengths[:, 0], y, keepdims=False)
    near = jnp.arange(half, dtype=jnp.int32)
    position = jnp.concatenate([y * half + near, (1 - y) * half + near])
    ok = position < length
    valid = jnp.broadcast_to(ok[:, None], (rows, 128)).astype(F32)
    sixty = jnp.arange(128) % 64
    bias = jnp.where(ok, 0.0, -1e9)[:, None]
    kaug = jnp.where(sixty == 0, bias, ((sixty > 0) & (sixty < 4)).astype(F32)).astype(BF16)
    weights = (w_query, w_key, w_value, w_out, w_up, w_down)
    wfq, wfa, wfd, _, *saved, vec, rows_in = forward_pass(weights, sm, tokens, cotangent, kaug, valid)
    _, activations, grad_tokens, outs, small = backward_pass(wfq, wfa, wfd, saved, vec, rows_in, kaug)
    shard = 2 * outs.shape[1]
    trio = outs[WIDE:].reshape(4, shard, width)[:, :, :768].reshape(4, shard, 3, 256).transpose(2, 1, 0, 3)
    trio = trio.reshape(3, shard, width)
    return (
        activations,
        grad_tokens,
        trio[0],
        trio[1],
        trio[2],
        outs[16:18].reshape(shard, width),
        outs[8:16].reshape(4, shard, width).transpose(1, 0, 2).reshape(shard, 4 * width),
        outs[0:8].reshape(4, shard, 4, width // 4).transpose(2, 1, 0, 3).reshape(4 * shard, width),
        lax.dynamic_slice_in_dim(small[0:8], (rank % 4) * 32, 32, axis=1),
        small[8],
    )


def solution(mesh):
    placed = (
        P(None, "dp", "seq", None),
        P(None, "dp"),
        P(("dp", "seq"), None),
        P(("dp", "seq"), None),
        P(("dp", "seq"), None),
        P(("dp", "seq"), None),
        P(("dp", "seq"), None),
        P(("dp", "seq"), None),
        P(None, ("dp", "seq")),
        P(("dp", "seq")),
        P(None, "dp", "seq", None),
    )
    own = mesh.shape["dp"] == 16 and mesh.shape["seq"] == 2
    return jax.shard_map(
        paired if own else per_device,
        mesh=mesh,
        in_specs=placed,
        out_specs=(
            P(None, "dp", "seq", None),
            P(None, "dp", "seq", None),
            P(("dp", "seq"), None),
            P(("dp", "seq"), None),
            P(("dp", "seq"), None),
            P(("dp", "seq"), None),
            P(("dp", "seq"), None),
            P(("dp", "seq"), None),
            P(None, ("dp", "seq")),
            P(("dp", "seq")),
        ),
        check_vma=False,
    )
```

```python
import functools
import math

import jax
import jax.numpy as jnp
from jax import lax
from jax.experimental import pallas as pl
from jax.experimental.pallas import tpu as pltpu
from jax.sharding import PartitionSpec as P

H = 16


EPSILON = 1e-05


def fetch_forward(w_query, w_key, w_value, w_out, w_up, w_down, vectors, up_bias):
    return (
        lax.all_gather(w_query, ("dp", "seq"), axis=0, tiled=True),
        lax.all_gather(w_key, ("dp", "seq"), axis=0, tiled=True),
        lax.all_gather(w_value, ("dp", "seq"), axis=0, tiled=True),
        lax.all_gather(w_out, ("dp", "seq"), axis=0, tiled=True),
        lax.all_gather(w_up, ("dp", "seq"), axis=0, tiled=True),
        lax.all_gather(w_down, ("dp", "seq"), axis=0, tiled=True),
        lax.all_gather(vectors, ("dp", "seq"), axis=1, tiled=True),
        lax.all_gather(up_bias, ("dp", "seq"), axis=0, tiled=True),
    )


def fetch_backward(w_query, w_key, w_value, w_out, w_up, w_down, vectors, up_bias):
    return (
        lax.all_gather(w_query, ("dp", "seq"), axis=0, tiled=True),
        lax.all_gather(w_key, ("dp", "seq"), axis=0, tiled=True),
        lax.all_gather(w_value, ("dp", "seq"), axis=0, tiled=True),
        lax.all_gather(w_out, ("dp", "seq"), axis=0, tiled=True),
        lax.all_gather(w_up, ("dp", "seq"), axis=0, tiled=True),
        lax.all_gather(w_down, ("dp", "seq"), axis=0, tiled=True),
        lax.all_gather(vectors, ("dp", "seq"), axis=1, tiled=True),
        lax.all_gather(up_bias, ("dp", "seq"), axis=0, tiled=True),
    )


def norm_forward(inputs, gain, shift):
    center = inputs - jnp.mean(inputs, axis=-1, keepdims=True)
    inverse = lax.rsqrt(jnp.mean(center * center, axis=-1, keepdims=True) + EPSILON)
    normed = center * inverse
    return (normed * gain + shift, normed, inverse)


def norm_backward(grad_out, normed, inverse, gain):
    grad_norm = grad_out * gain
    inner = (
        grad_norm
        - jnp.mean(grad_norm, axis=-1, keepdims=True)
        - normed * jnp.mean(grad_norm * normed, axis=-1, keepdims=True)
    )
    return (inner * inverse, jnp.sum(grad_out * normed, axis=0), jnp.sum(grad_out, axis=0))


def score_heads(query_heads, key_heads, key_valid, factor):
    scores = (
        jnp.einsum("qhd,khd->hqk", query_heads, key_heads, preferred_element_type=jnp.float32)
        * factor
    )
    return jnp.where(key_valid[None, None, :], scores, -1000000000.0)


def per_device(
    tokens, lengths, w_query, w_key, w_value, w_out, w_up, w_down, vectors, up_bias, cotangent
):
    micro = tokens.shape[0]
    slot = tokens.shape[2]
    width = tokens.shape[3]
    hidden_units = w_up.shape[1]
    heads = H
    head_dim = width // heads
    factor = 1.0 / math.sqrt(head_dim)
    positions = lax.axis_index("seq") * slot + jnp.arange(slot, dtype=jnp.int32)
    f32 = jnp.float32
    sums = [
        jnp.zeros((width, width), f32),
        jnp.zeros((width, width), f32),
        jnp.zeros((width, width), f32),
        jnp.zeros((width, width), f32),
        jnp.zeros((width, hidden_units), f32),
        jnp.zeros((hidden_units, width), f32),
        jnp.zeros((8, width), f32),
        jnp.zeros((hidden_units,), f32),
    ]
    outputs = []
    grad_list = []
    for micro_index in range(micro):
        full_query, full_key, full_value, full_out, full_up, full_down, full_vectors, full_bias = (
            fetch_forward(w_query, w_key, w_value, w_out, w_up, w_down, vectors, up_bias)
        )
        vec_f = full_vectors.astype(f32)
        bias_f = full_bias.astype(f32)
        rows_in = tokens[micro_index, 0]
        length = lengths[micro_index, 0]
        valid = (positions < length)[:, None].astype(f32)
        query = (jnp.dot(rows_in, full_query, preferred_element_type=f32) + vec_f[0]).astype(
            jnp.bfloat16
        )
        keys_own = jnp.dot(rows_in, full_key, preferred_element_type=f32).astype(jnp.bfloat16)
        vals_own = (jnp.dot(rows_in, full_value, preferred_element_type=f32) + vec_f[1]).astype(
            jnp.bfloat16
        )
        keys_all, vals_all = (
            lax.all_gather(keys_own, "seq", axis=0, tiled=True),
            lax.all_gather(vals_own, "seq", axis=0, tiled=True),
        )
        total_len = keys_all.shape[0]
        key_valid = jnp.arange(total_len, dtype=jnp.int32) < length
        query_heads = query.reshape(slot, heads, head_dim)
        key_heads = keys_all.reshape(total_len, heads, head_dim)
        val_heads = vals_all.reshape(total_len, heads, head_dim)
        scores = score_heads(query_heads, key_heads, key_valid, factor)
        top = jnp.max(scores, axis=-1, keepdims=True)
        log_total = top + jnp.log(jnp.sum(jnp.exp(scores - top), axis=-1, keepdims=True))
        probs = jnp.exp(scores - log_total).astype(jnp.bfloat16)
        context = (
            jnp.einsum("hqk,khd->qhd", probs, val_heads, preferred_element_type=f32)
            .reshape(slot, width)
            .astype(jnp.bfloat16)
        )
        attention = jnp.dot(context, full_out, preferred_element_type=f32) + vec_f[2]
        hidden, normed_one, inverse_one = norm_forward(
            rows_in.astype(f32) + attention, vec_f[3], vec_f[4]
        )
        hidden_low = hidden.astype(jnp.bfloat16)
        upper = jnp.dot(hidden_low, full_up, preferred_element_type=f32) + bias_f
        active = jax.nn.gelu(upper).astype(jnp.bfloat16)
        lowered = jnp.dot(active, full_down, preferred_element_type=f32) + vec_f[5]
        result, normed_two, inverse_two = norm_forward(hidden + lowered, vec_f[6], vec_f[7])
        outputs.append((result * valid).astype(jnp.bfloat16))
        full_query, full_key, full_value, full_out, full_up, full_down, full_vectors, full_bias = (
            fetch_backward(w_query, w_key, w_value, w_out, w_up, w_down, vectors, up_bias)
        )
        vec_f = full_vectors.astype(f32)
        grad_out = cotangent[micro_index, 0].astype(f32) * valid
        grad_res2, grad_gain2, grad_shift2 = norm_backward(
            grad_out, normed_two, inverse_two, vec_f[6]
        )
        grad_down = grad_res2.astype(jnp.bfloat16)
        grad_bias2 = jnp.sum(grad_down.astype(f32), axis=0)
        sums[5] = sums[5] + jnp.einsum("sf,sd->fd", active, grad_down, preferred_element_type=f32)
        grad_active = jnp.einsum("sd,fd->sf", grad_down, full_down, preferred_element_type=f32)
        gelu_pull = jax.vjp(jax.nn.gelu, upper)[1]
        grad_upper = gelu_pull(grad_active)[0].astype(jnp.bfloat16)
        sums[7] = sums[7] + jnp.sum(grad_upper.astype(f32), axis=0)
        sums[4] = sums[4] + jnp.einsum(
            "sd,sf->df", hidden_low, grad_upper, preferred_element_type=f32
        )
        grad_hidden = grad_res2 + jnp.einsum(
            "sf,df->sd", grad_upper, full_up, preferred_element_type=f32
        )
        grad_res1, grad_gain1, grad_shift1 = norm_backward(
            grad_hidden, normed_one, inverse_one, vec_f[3]
        )
        grad_att = grad_res1.astype(jnp.bfloat16)
        grad_bias_out = jnp.sum(grad_att.astype(f32), axis=0)
        sums[3] = sums[3] + jnp.einsum("sd,se->de", context, grad_att, preferred_element_type=f32)
        grad_context = jnp.einsum(
            "se,de->sd", grad_att, full_out, preferred_element_type=f32
        ).astype(jnp.bfloat16)
        grad_ctx_heads = grad_context.reshape(slot, heads, head_dim)
        scores_again = score_heads(query_heads, key_heads, key_valid, factor)
        full_probs = jnp.exp(scores_again - log_total)
        probs_low = full_probs.astype(jnp.bfloat16)
        grad_probs = jnp.einsum(
            "qhd,khd->hqk", grad_ctx_heads, val_heads, preferred_element_type=f32
        )
        grad_val_term = jnp.einsum(
            "hqk,qhd->khd", probs_low, grad_ctx_heads, preferred_element_type=f32
        )
        row_inner = jnp.sum(full_probs * grad_probs, axis=-1, keepdims=True)
        grad_scores = (full_probs * (grad_probs - row_inner)).astype(jnp.bfloat16)
        grad_query = (
            (
                jnp.einsum("hqk,khd->qhd", grad_scores, key_heads, preferred_element_type=f32)
                * factor
            )
            .reshape(slot, width)
            .astype(jnp.bfloat16)
        )
        grad_key_term = (
            jnp.einsum("hqk,qhd->khd", grad_scores, query_heads, preferred_element_type=f32)
            * factor
        )
        grad_keys, grad_vals = (
            lax.psum_scatter(
                grad_key_term.reshape(total_len, width).astype(jnp.bfloat16),
                "seq",
                scatter_dimension=0,
                tiled=True,
            ).astype(jnp.float32),
            lax.psum_scatter(
                grad_val_term.reshape(total_len, width).astype(jnp.bfloat16),
                "seq",
                scatter_dimension=0,
                tiled=True,
            ).astype(jnp.float32),
        )
        grad_keys = grad_keys.astype(jnp.bfloat16)
        grad_vals = grad_vals.astype(jnp.bfloat16)
        grad_bias_query = jnp.sum(grad_query.astype(f32), axis=0)
        grad_bias_vals = jnp.sum(grad_vals.astype(f32), axis=0)
        sums[0] = sums[0] + jnp.einsum("sd,se->de", rows_in, grad_query, preferred_element_type=f32)
        sums[1] = sums[1] + jnp.einsum("sd,se->de", rows_in, grad_keys, preferred_element_type=f32)
        sums[2] = sums[2] + jnp.einsum("sd,se->de", rows_in, grad_vals, preferred_element_type=f32)
        sums[6] = sums[6] + jnp.stack(
            [
                grad_bias_query,
                grad_bias_vals,
                grad_bias_out,
                grad_gain1,
                grad_shift1,
                grad_bias2,
                grad_gain2,
                grad_shift2,
            ]
        )
        grad_rows = grad_res1 + jnp.einsum(
            "se,de->sd", grad_query, full_query, preferred_element_type=f32
        )
        grad_rows = grad_rows + jnp.einsum(
            "se,de->sd", grad_keys, full_key, preferred_element_type=f32
        )
        grad_rows = grad_rows + jnp.einsum(
            "se,de->sd", grad_vals, full_value, preferred_element_type=f32
        )
        grad_list.append(grad_rows)
    shares = (
        lax.psum_scatter(sums[0], ("dp", "seq"), scatter_dimension=0, tiled=True),
        lax.psum_scatter(sums[1], ("dp", "seq"), scatter_dimension=0, tiled=True),
        lax.psum_scatter(sums[2], ("dp", "seq"), scatter_dimension=0, tiled=True),
        lax.psum_scatter(sums[3], ("dp", "seq"), scatter_dimension=0, tiled=True),
        lax.psum_scatter(sums[4], ("dp", "seq"), scatter_dimension=0, tiled=True),
        lax.psum_scatter(sums[5], ("dp", "seq"), scatter_dimension=0, tiled=True),
        lax.psum_scatter(sums[6], ("dp", "seq"), scatter_dimension=1, tiled=True),
        lax.psum_scatter(sums[7], ("dp", "seq"), scatter_dimension=0, tiled=True),
    )
    activations = jnp.stack(outputs)[:, None]
    grad_tokens = jnp.stack(grad_list)[:, None]
    return (
        activations,
        grad_tokens,
        shares[0],
        shares[1],
        shares[2],
        shares[3],
        shares[4],
        shares[5],
        shares[6],
        shares[7],
    )


MESH = pl.DeviceIdType.MESH
F32 = jnp.float32
BF16 = jnp.bfloat16
ANY = pl.ANY
VMEM = pltpu.VMEM
LOG2E = math.log2(math.e)
LIMIT = 58 * 1024 * 1024
GELU_C = math.sqrt(2.0 / math.pi)
GELU_A = 0.044715


def nt(a, b):
    return lax.dot_general(a, b, (((1,), (1,)), ((), ())), preferred_element_type=F32)


def nn(a, b):
    return lax.dot_general(a, b, (((1,), (0,)), ((), ())), preferred_element_type=F32)


def tn(a, b):
    return lax.dot_general(a, b, (((0,), (0,)), ((), ())), preferred_element_type=F32)


def place():
    dp = lax.axis_index("dp")
    return dp // 4, (dp // 2) % 2, dp % 2, lax.axis_index("seq")


def device(z, x, c, y):
    return (z * 4 + x * 2 + c, y)


def greet(z, x, c, y):
    barrier = pltpu.get_barrier_semaphore()
    partners = [device(z, x, 1 - c, y), device(z, 1 - x, c, y), device(z, x, c, 1 - y)]
    partners += [device((z + d) % 4, x, c, y) for d in (1, 2, 3)]
    for partner in partners:
        pl.semaphore_signal(barrier, inc=1, device_id=partner, device_id_type=MESH)
    pl.semaphore_wait(barrier, len(partners))


PHASES = 4
LAG = 2
WARM = PHASES * (LAG - 1)
SLOTS = 6


def gather_copies(ref, cross, send, recv, core, phase, pos):
    z, x, c, y = pos
    every = slice(None)
    order = "yzxc" if core == 0 else "zyxc" if cross else "zxyc"
    done = order[:phase]
    have = (
        every if "z" in done else z,
        every if "x" in done else x,
        every if "c" in done else c,
        every if "y" in done else y,
    )
    axis = order[phase]
    if axis == "z":
        targets = [(2 + d, ((z + d) % 4, x, c, y)) for d in (1, 2, 3)]
    elif axis == "x":
        targets = [(0, (z, 1 - x, c, y))]
    elif axis == "y":
        targets = [(1, (z, x, c, 1 - y))]
    else:
        targets = [(2, (z, x, 1 - c, y))]
    return [
        pltpu.make_async_remote_copy(
            src_ref=ref.at[have],
            dst_ref=ref.at[have],
            send_sem=send.at[slot],
            recv_sem=recv.at[slot],
            device_id=device(*target),
            device_id_type=MESH,
        )
        for slot, target in targets
    ]


def gather_phase(ref, cross, send, recv, phase, pos):
    for core in (0, 1):

        @pl.when(pos[2] == core)
        def _():
            if phase > 0:
                for copy in gather_copies(ref, cross, send, recv, core, phase - 1, pos):
                    copy.wait_recv()
            if phase < PHASES:
                for copy in gather_copies(ref, cross, send, recv, core, phase, pos):
                    copy.start()


def gather_sent(ref, cross, send, recv, pos):
    for core in (0, 1):

        @pl.when(pos[2] == core)
        def _():
            for phase in range(PHASES):
                for copy in gather_copies(ref, cross, send, recv, core, phase, pos):
                    copy.wait_send()


class Halves:
    def __init__(self, make):
        self.make = make

    def start(self):
        for h in range(2):
            self.make(h).start()

    def wait(self):
        for h in range(2):
            self.make(h).wait()


def lanes(shape):
    return lax.broadcasted_iota(jnp.int32, shape, len(shape) - 1)


def norm(v):
    center = v - jnp.mean(v, axis=-1, keepdims=True)
    inverse = lax.rsqrt(jnp.mean(center * center, axis=-1, keepdims=True) + EPSILON)
    return center * inverse, inverse


def norm_back(g, normed, inverse, gain):
    gn = g * gain
    inner = gn - jnp.mean(gn, axis=-1, keepdims=True) - normed * jnp.mean(gn * normed, axis=-1, keepdims=True)
    return inner * inverse


def within(lens, y, rows):
    row = lax.broadcasted_iota(jnp.int32, (rows, 128), 0)
    half = rows // 2
    position = jnp.where(row < half, y * half + row, (1 - y) * half + row - half)
    return position < lens[y, 0]


def key_lanes(ok):
    sixty = lanes(ok.shape) % 64
    ones = ((sixty > 0) & (sixty < 4)).astype(F32)
    return jnp.where(sixty == 0, jnp.where(ok, 0.0, -1e9), ones).astype(BF16)


def rowsum(v):
    return jnp.sum(v, axis=0, keepdims=True)


def blocks(rows, block, body, straight=False):
    def run(b, carry):
        body(pl.ds(pl.multiple_of(b * block, block), block))
        return carry

    lax.fori_loop(0, rows // block, run, 0, unroll=straight)


def tiles(width, tile, body):
    def run(b, carry):
        body(b, pl.ds(pl.multiple_of(b * tile, tile), tile))
        return carry

    lax.fori_loop(0, width // tile, run, 0)


def forward_kernel(
    wq, wk, wv, wo, wup, wdown, sm, tok, cot, lens,
    wfq, wfa, wfd, sf, xs_o, quad_o, aug_o, res_o, low_o, act_o, slope_o, back_o, gdn_o, out_o, vec, rows_out,
    xs, ct, quad, aug, res, acc, low, actv, slope, wbuf, dbuf, small, out, kaug, valid,
    send, recv, place_sem, own_sem, swap_send, swap_recv, wsem, dsem, out_sem,
):
    pos = place()
    z, x, c, y = pos
    rows, width = xs.shape
    half = rows // 2
    group = 256
    groups = width // group
    wide_from = 2 * groups
    tall_from = wide_from + 10
    chunks = tall_from + 8

    first = []

    def put(src, dst):
        first.append(pltpu.make_async_copy(src, dst, place_sem.at[len(first)]))

    for h in range(2):
        top = slice(16 * h, 16 * h + 16)
        for g in range(groups):
            for k, w in enumerate((wq, wk, wv)):
                put(
                    w.at[top, group * g : group * (g + 1)],
                    wfq.at[g, h, z, x, c, y, :, pl.ds(group * k, group)],
                )
        put(wo.at[top], wfa.at[0, h, z, x, c, y])
        for j in range(4):
            put(wup.at[top, width * j : width * (j + 1)], wfa.at[1 + j, h, z, x, c, y])
            put(wdown.at[64 * h : 64 * h + 64, 256 * j : 256 * (j + 1)], wfd.at[j, h, z, x, c, y])
    put(sm, sf.at[z, x, c, y])
    for copy in first:
        copy.start()
    mine = [
        pltpu.make_async_copy(tok.at[y, 0], xs.at[pl.ds(0, half)], own_sem.at[0]),
        pltpu.make_async_copy(cot.at[y, 0], ct.at[pl.ds(0, half)], own_sem.at[1]),
    ]
    for copy in mine:
        copy.start()
    greet(*pos)
    for copy in first:
        copy.wait()

    piece = half // 8

    def swap(src, dst, slot, index):
        at = pl.multiple_of(index * piece, piece)
        return pltpu.make_async_remote_copy(
            src_ref=src.at[1 - y, 0, pl.ds(at, piece)],
            dst_ref=dst.at[pl.ds(half + at, piece)],
            send_sem=swap_send.at[slot, index],
            recv_sem=swap_recv.at[slot, index],
            device_id=device(z, x, c, 1 - y),
            device_id_type=MESH,
        )

    def chunk(index, kind):
        odd = index % 2
        if kind == 0:
            ref = wfq.at[index // 2, odd]
        elif kind == 1:
            ref = wfa.at[(index - wide_from) // 2, odd]
        else:
            ref = wfd.at[(index - tall_from) // 2, odd]
        return (ref, kind == 0, send.at[index], recv.at[index])

    tiny = (sf, False, send.at[chunks], recv.at[chunks])

    def kinds(index, body):
        for kind, (start, stop) in enumerate(((0, wide_from), (wide_from, tall_from), (tall_from, chunks))):

            @pl.when((index >= start) & (index < stop))
            def _():
                body(chunk(index, kind))

    def step(t, carry):
        for phase in range(PHASES + 1):
            index = t - LAG * phase
            kinds(index, lambda parts: gather_phase(*parts, phase, pos))

            @pl.when(index == 0)
            def _():
                gather_phase(*tiny, phase, pos)

        @pl.when(t < 4)
        def _():
            swap(tok, xs, 0, 2 * t).start()
            swap(tok, xs, 0, 2 * t + 1).start()

        @pl.when((t >= 4) & (t < 12))
        def _():
            swap(cot, ct, 1, t - 4).start()

        return carry

    def advance(start, stop):
        lax.fori_loop(start, stop, step, 0)

    def weight(index, slot):
        return Halves(lambda h: pltpu.make_async_copy(wfa.at[index, h], wbuf.at[slot, :, :, :, :, h], wsem.at[slot, h]))

    def trio(g):
        return Halves(
            lambda h: pltpu.make_async_copy(
                wfq.at[g, h], wbuf.at[0, :, :, :, :, h, :, pl.ds(0, 3 * group)], wsem.at[0, h]
            )
        )

    def square(slot, cols):
        return wbuf[slot, :, :, :, :, :, :, cols].reshape(width, cols.size)

    def save(src, dst, slot):
        copy = pltpu.make_async_copy(src, dst, out_sem.at[slot])
        copy.start()
        return copy

    advance(0, 6 + WARM)
    trio(0).start()
    for index in range(8):
        swap(tok, xs, 0, index).wait_recv()
    for copy in mine:
        copy.wait()
    saves = [save(xs, xs_o, 0)]
    ok = within(lens, y, rows)
    kaug[...] = key_lanes(ok)
    valid[...] = ok.astype(F32)
    gathered = pltpu.make_async_copy(sf, small, own_sem.at[2])
    gathered.start()
    gathered.wait()
    tiles32 = [small[a, b, d, e].astype(F32) for a in range(4) for b in range(2) for d in range(2) for e in range(2)]
    for g in range(8):
        vec[0:8, 128 * g : 128 * g + 128] = sum(tiles32[4 * g + s] for s in range(4))[0:8]
    for r in range(4):
        for g in range(8):
            vec[8 + r : 9 + r, 128 * g : 128 * g + 128] = tiles32[8 * r + g][8:9]
    vec[12:16, :] = jnp.zeros((4, width), F32)

    block = 256
    low1 = (lanes((1, 128)) < 64).astype(F32).astype(BF16)
    high1 = (lanes((1, 128)) >= 64).astype(F32).astype(BF16)
    ones1 = (lanes((1, 128)) % 64 == 0).astype(F32).astype(BF16)
    qlane = lanes((block, 128))
    sixty = qlane % 64

    def heads(g, at):
        def run(n, carry):
            pair(g, at, n)
            advance(WARM + 6 + 3 * g + n, WARM + 7 + 3 * g + 2 * n)
            return carry

        lax.fori_loop(0, 2, run, 0)

    def pair(g, at, n):
        local = pl.multiple_of(n * 128, 128)
        qc, kc, vc, cc = (pl.ds(local + group * k, 128) for k in range(4))
        cols = pl.ds(pl.multiple_of(g * group + n * 128, 128), 128)
        k2 = quad[g, :, kc]
        v2 = quad[g, :, vc]
        ka = k2 * low1 + kaug[...] * high1
        kb = k2 * high1 + kaug[...] * low1

        def query_block(sl):
            q2 = quad[g, sl, qc]
            parts = []
            for own, other, kk in ((low1, high1, ka), (high1, low1, kb)):
                s = nt(q2 * own + ones1 * other, kk)
                top = jnp.max(s, axis=1, keepdims=True)
                e = jnp.exp2(s - top)
                total = jnp.sum(e, axis=1, keepdims=True)
                o = nn(e.astype(BF16), v2)
                parts.append((o / total, -(top + jnp.log2(total))))
            lower = qlane < 64
            quad[g, sl, cc] = jnp.where(lower, parts[0][0], parts[1][0]).astype(BF16)
            neg = jnp.where(lower, parts[1][1], parts[0][1])
            hi = neg.astype(BF16).astype(F32)
            mid = (neg - hi).astype(BF16).astype(F32)
            lo = neg - hi - mid
            aug[sl, cols] = jnp.where(
                sixty == 0,
                1.0,
                jnp.where(sixty == 1, hi, jnp.where(sixty == 2, mid, jnp.where(sixty == 3, lo, 0.0))),
            ).astype(BF16)

        blocks(rows, block, query_block, True)

    def attend(g, carry):
        trio(g).wait()
        at = pl.ds(pl.multiple_of(g * group, group), group)
        for k in range(3):
            out_k = nn(xs[...], square(0, pl.ds(group * k, group)))
            if k == 0:
                out_k = (out_k + vec[0:1, at]) * (LOG2E / 8.0)
            elif k == 2:
                out_k = out_k + vec[1:2, at]
            quad[g, :, group * k : group * (k + 1)] = out_k.astype(BF16)
        heads(g, at)

        @pl.when(g < groups - 1)
        def _():
            trio(g + 1).start()

        return carry

    lax.fori_loop(0, groups, attend, 0)
    weight(0, 1).start()
    for g in range(groups):
        saves.append(save(quad.at[g], quad_o.at[g], 1 + g))
    saves.append(save(aug, aug_o, 5))
    weight(0, 1).wait()

    def project_out(n, cols):
        total = vec[2:3, cols]
        for g in range(groups):
            total = total + nn(quad[g, :, 3 * group : 4 * group], wbuf[1, g, :, :, :, :, :, cols].reshape(group, group))
        res[:, cols] = xs[:, cols].astype(F32) + total

    tiles(width, 256, project_out)
    weight(1, 0).start()
    saves.append(save(res, res_o, 6))

    def normalize(sl):
        normed, _ = norm(res[sl, :])
        low[sl, :] = (normed * vec[3:4, :] + vec[4:5, :]).astype(BF16)

    blocks(rows, block, normalize)
    saves.append(save(low, low_o, 7))

    def shaft(j, slot):
        return Halves(lambda h: pltpu.make_async_copy(wfd.at[j, h], dbuf.at[slot, :, :, :, :, h], dsem.at[slot, h]))

    for j in range(4):
        weight(1 + j, j % 2).wait()

        def climb(n, cols):
            up = nn(low[...], square(j % 2, cols)) + vec[8 + j : 9 + j, cols]
            sq = up * up
            t = jnp.tanh(up * (GELU_C + (GELU_C * GELU_A) * sq))
            hf = 0.5 * up
            actv[j, :, cols] = (hf + hf * t).astype(BF16)
            slope[j, :, cols] = (
                0.5 + 0.5 * t + hf * (1.0 - t * t) * (GELU_C + (3.0 * GELU_C * GELU_A) * sq)
            ).astype(BF16)

            @pl.when(n == 1)
            def _():
                advance(WARM + 18 + 2 * j, WARM + 19 + 2 * j)

        tiles(width, 256, climb)
        advance(WARM + 19 + 2 * j, WARM + 20 + 2 * j)
        if j < 3:
            weight(2 + j, (1 + j) % 2).start()
        else:
            shaft(0, 0).start()
        saves.append(save(actv.at[j], act_o.at[j], 8 + j))
        saves.append(save(slope.at[j], slope_o.at[j], 12 + j))

    for j in range(4):
        shaft(j, j % 2).wait()
        cols = slice(256 * j, 256 * (j + 1))

        def slide(k, carry):
            part = nn(actv[k], dbuf[j % 2, k].reshape(width, 256))

            @pl.when(k == 0)
            def _():
                acc[:, cols] = part + vec[5:6, cols]

            @pl.when(k > 0)
            def _():
                acc[:, cols] += part

            return carry

        lax.fori_loop(0, 4, slide, 0)
        if j < 3:
            advance(WARM + 26 + 2 * j, min(WARM + 28 + 2 * j, chunks + LAG * PHASES))
            shaft(1 + j, (1 + j) % 2).start()

    for index in range(8):
        swap(cot, ct, 1, index).wait_recv()
    rows_out[...] = jnp.zeros_like(rows_out)

    def middle(sl):
        normed, _ = norm(res[sl, :])
        hidden = normed * vec[3:4, :] + vec[4:5, :]
        normed, inverse = norm(hidden + acc[sl, :])
        ok = valid[sl, 0:1]
        out[sl, :] = ((normed * vec[6:7, :] + vec[7:8, :]) * ok).astype(BF16)
        g = ct[sl, :].astype(F32) * ok
        back = norm_back(g, normed, inverse, vec[6:7, :])
        acc[sl, :] = back
        gd = back.astype(BF16)
        ct[sl, :] = gd
        rows_out[6:7, :] += rowsum(g * normed)
        rows_out[7:8, :] += rowsum(g)
        rows_out[5:6, :] += rowsum(gd.astype(F32))

    blocks(rows, block, middle)
    saves.append(save(out, out_o, 16))
    saves.append(save(acc, back_o, 17))
    saves.append(save(ct, gdn_o, 18))

    def finish(index, carry):
        kinds(index, lambda parts: gather_sent(*parts, pos))
        return carry

    lax.fori_loop(0, chunks, finish, 0)
    gather_sent(*tiny, pos)
    for slot, (src, dst) in enumerate(((tok, xs), (cot, ct))):
        for index in range(8):
            swap(src, dst, slot, index).wait_send()
    for copy in saves:
        copy.wait()


def forward_pass(weights, sm, tok, cot, lens):
    width = tok.shape[3]
    rows = 2 * tok.shape[2]
    low = jax.ShapeDtypeStruct((rows, width), BF16)
    full = jax.ShapeDtypeStruct((rows, width), F32)
    wide = jax.ShapeDtypeStruct((4, rows, width), BF16)
    six = (4, 2, 2, 2)
    vmem = pl.BlockSpec(memory_space=VMEM)
    hbm = pl.BlockSpec(memory_space=ANY)
    dma = pltpu.SemaphoreType.DMA
    return pl.pallas_call(
        forward_kernel,
        out_shape=(
            jax.ShapeDtypeStruct((4, 2) + six + (16, 768), BF16),
            jax.ShapeDtypeStruct((5, 2) + six + (16, width), BF16),
            jax.ShapeDtypeStruct((4, 2) + six + (64, 256), BF16),
            jax.ShapeDtypeStruct(six + (16, 128), BF16),
            low, wide, low, full, low, wide, wide, full, low, low,
            jax.ShapeDtypeStruct((16, width), F32),
            jax.ShapeDtypeStruct((8, width), F32),
        ),
        in_specs=[vmem] * 7 + [hbm] * 2 + [pl.BlockSpec(memory_space=pltpu.SMEM)],
        out_specs=[hbm] * 14 + [vmem] * 2,
        scratch_shapes=[
            VMEM((rows, width), BF16),
            VMEM((rows, width), BF16),
            VMEM((4, rows, width), BF16),
            VMEM((rows, width), BF16),
            VMEM((rows, width), F32),
            VMEM((rows, width), F32),
            VMEM((rows, width), BF16),
            VMEM((4, rows, width), BF16),
            VMEM((4, rows, width), BF16),
            VMEM((2,) + six + (2, 16, width), BF16),
            VMEM((2,) + six + (2, 64, 256), BF16),
            VMEM(six + (16, 128), BF16),
            VMEM((rows, width), BF16),
            VMEM((rows, 128), BF16),
            VMEM((rows, 128), F32),
            dma((27, SLOTS)),
            dma((27, SLOTS)),
            dma((43,)),
            dma((3,)),
            dma((2, 8)),
            dma((2, 8)),
            dma((2, 2)),
            dma((2, 2)),
            dma((19,)),
        ],
        compiler_params=pltpu.CompilerParams(collective_id=0, has_side_effects=True, vmem_limit_bytes=LIMIT),
        cost_estimate=pl.CostEstimate(flops=2 * 14 * rows * width * width, bytes_accessed=90 << 20, transcendentals=1 << 24),
        name="forward_pass",
    )(*weights, sm, tok, cot, lens)


CHUNKS = 26
WIDE = 18
DEPTH = 6
LAST = CHUNKS - 1


def ways(core, index):
    full = 1024 if index < WIDE else 768
    mode = 0 if core == 0 or index >= CHUNKS - 4 else 2 if index >= WIDE else 1
    return ((mode, 0, full),)


def scatter_copies(way, part, phase, grad, bufs, send, recv, pos):
    z, x, c, y = pos
    mode, start, size = way
    cols = pl.ds(start, size)
    b0, b1, b2, b3 = bufs
    every = slice(None)

    def remote(src, dst, slot, target):
        return pltpu.make_async_remote_copy(
            src_ref=src,
            dst_ref=dst,
            send_sem=send.at[6 * part + slot],
            recv_sem=recv.at[6 * part + slot],
            device_id=device(*target),
            device_id_type=MESH,
        )

    across = (z, 1 - x, c, y)
    beside = (z, x, c, 1 - y)
    if phase == 0:
        return [remote(grad.at[:, :, 1 - c, :, :, cols], b0.at[:, :, :, :, cols], 2, (z, x, 1 - c, y))]
    if phase == 1:
        if mode == 1:
            return [remote(b0.at[:, :, 1 - y, :, cols], b1.at[:, :, :, cols], 1, beside)]
        return [remote(b0.at[:, 1 - x, :, :, cols], b1.at[:, :, :, cols], 0, across)]
    if phase == 2:
        if mode == 0:
            return [
                remote(
                    b1.at[(z + d) % 4, :, :, cols],
                    b2.at[pl.ds(2 * (d - 1), 2), :, cols],
                    2 + d,
                    ((z + d) % 4, x, c, y),
                )
                for d in (1, 2, 3)
            ]
        if mode == 1:
            return [remote(b1.at[:, 1 - x, :, cols], b2.at[pl.ds(0, 4), :, cols], 0, across)]
        return [remote(b1.at[:, 1 - y, :, cols], b2.at[pl.ds(0, 4), :, cols], 1, beside)]
    if mode == 0:
        return [remote(b1.at[z, 1 - y, :, cols], b3.at[0, :, cols], 1, beside)]
    return [
        remote(b2.at[(z + d) % 4, :, cols], b3.at[d - 1, :, cols], 2 + d, ((z + d) % 4, x, c, y)) for d in (1, 2, 3)
    ]


def scatter_add(way, phase, own, bufs, out, pos):
    z, x, c, y = pos
    mode, start, size = way
    cols = pl.ds(start, size)
    b0, b1, b2, b3 = bufs

    def plus(a, b):
        return a + b

    def each(body):
        def run(zz, carry):
            body(zz)
            return carry

        lax.fori_loop(0, 4, run, 0)

    if phase == 0:

        def body(zz):
            b0[zz, :, :, :, cols] = plus(own[zz, :, :, :, cols], b0[zz, :, :, :, cols])

        each(body)
    elif phase == 1:

        def body(zz):
            kept = b0[zz, :, y, :, cols] if mode == 1 else b0[zz, x, :, :, cols]
            b1[zz, :, :, cols] = plus(kept, b1[zz, :, :, cols])

        each(body)
    elif mode == 0:
        if phase == 2:
            total = b1[z, :, :, cols].astype(F32)
            for d in range(3):
                total = total + b2[pl.ds(2 * d, 2), :, cols].astype(F32)
            b1[z, :, :, cols] = total.astype(BF16)
        else:
            out(b1[z, y, :, cols].astype(F32) + b3[0, :, cols].astype(F32))
    elif phase == 2:

        def body(zz):
            kept = b1[zz, x, :, cols] if mode == 1 else b1[zz, y, :, cols]
            b2[zz, :, cols] = plus(kept, b2[zz, :, cols])

        each(body)
    else:
        total = b2[z, :, cols].astype(F32)
        for d in range(3):
            total = total + b3[d, :, cols].astype(F32)
        out(total)


def scatter_phase(phase, plan, full, grad, own, own_sem, bufs, out, send, recv, credit, index, pos):
    z, x, c, y = pos
    cols = pl.ds(0, full)

    def mine():
        return pltpu.make_async_copy(grad.at[:, :, c, :, :, cols], own.at[:, :, :, :, cols], own_sem)

    if phase == 0:
        mine().start()
        if credit is not None:

            @pl.when(index >= DEPTH)
            def _():
                pl.semaphore_wait(credit, 1)

    if phase == 1:
        mine().wait()
    for core in (0, 1):

        @pl.when(c == core)
        def _():
            def copies(phase):
                return [
                    copy
                    for part, way in enumerate(plan[core] if phase > 0 else ((0, 0, full),))
                    for copy in scatter_copies(way, part, phase, grad, bufs, send, recv, pos)
                ]

            if phase > 0:
                for copy in copies(phase - 1):
                    copy.wait_recv()
                if phase == 2:
                    for copy in copies(1):
                        copy.wait_send()
                for way in plan[core]:
                    scatter_add(way, phase - 1, own, bufs, out, pos)
            if phase < PHASES:
                for copy in copies(phase):
                    copy.start()

    if phase == 2 and credit is not None:

        @pl.when(index < CHUNKS - DEPTH)
        def _():
            pl.semaphore_signal(credit, inc=1, device_id=device(z, x, 1 - c, y), device_id_type=MESH)


def scatter_sent(plan, full, grad, bufs, send, recv, pos):
    for core in (0, 1):

        @pl.when(pos[2] == core)
        def _():
            for phase in (0, 2, 3):
                for part, way in enumerate(plan[core] if phase > 0 else ((0, 0, full),)):
                    for copy in scatter_copies(way, part, phase, grad, bufs, send, recv, pos):
                        copy.wait_send()


SMALL = (((0, 0, 128),), ((1, 0, 128),))


def backward_kernel(
    wfq, wfa, wfd, xs_i, quad_i, aug_i, res_i, low_i, act_i, slope_i, back_i, gdn_i, out_i, vec, rows_in, lens,
    gw, act_o, gtok_o, gq_o, gk_o, gv_o, go_o, gup_o, gdown_o, small_out,
    acc, rbuf, gdn, low, quad, duo, wbuf, dbuf, stage, own, b0, b1, b2, b3, home, rows_sum, bias_sum,
    small_g, small_own, s0, s1, s2, s3, kaug,
    send, recv, own_sem, credit, swap_send, swap_recv, load_sem, wsem, dsem, stage_sem, out_sem,
):
    pos = place()
    z, x, c, y = pos
    rows, width = acc.shape
    half = rows // 2
    block = 256
    group = 256
    groups = width // group
    piece = half // 8

    def load(src, dst, slot):
        return pltpu.make_async_copy(src, dst, load_sem.at[slot])

    loads = [load(act_i.at[k], quad.at[k], k) for k in range(4)]
    loads += [load(gdn_i, gdn, 4), load(low_i, low, 5), load(back_i, acc, 6)]
    loads += [load(out_i.at[pl.ds(0, half)], duo.at[1, pl.ds(0, half)], 7), load(slope_i.at[0], duo.at[0], 8)]
    for k in (4, 0, 1, 2, 3, 5, 6, 7, 8):
        loads[k].start()
    greet(*pos)

    def away(index):
        at = pl.multiple_of(index * piece, piece)
        return pltpu.make_async_remote_copy(
            src_ref=out_i.at[pl.ds(half + at, piece)],
            dst_ref=act_o.at[y, 0, pl.ds(at, piece)],
            send_sem=swap_send.at[index],
            recv_sem=swap_recv.at[index],
            device_id=device(z, x, c, 1 - y),
            device_id_type=MESH,
        )

    kinds = ((0, WIDE, 1024), (WIDE, CHUNKS - 4, 768), (CHUNKS - 4, CHUNKS, 768))

    def chunk(index):
        slot = index % DEPTH
        bufs = (b0.at[slot], b1.at[index], b2.at[index], b3.at[index])
        return gw.at[index // 2, index % 2], bufs, send.at[index], recv.at[index]

    small_bufs = (s0, s1, s2, s3)

    def deliver(index, first):
        odd = index % 2
        row = pl.multiple_of(16 * odd, 16)

        def at(size, which):
            return pl.ds(pl.multiple_of(which * size, size), size)

        def wide(total):
            @pl.when(index < 8)
            def _():
                for q in range(4):
                    gdown_o[pl.ds(32 * q + row, 16), at(256, index // 2)] = total[:, 256 * q : 256 * (q + 1)]

            @pl.when((index >= 8) & (index < 16))
            def _():
                gup_o[pl.ds(row, 16), at(width, index // 2 - 4)] = total

            @pl.when(index >= 16)
            def _():
                go_o[pl.ds(row, 16), :] = total

        def trio_part(total):
            for k, dst in enumerate((gq_o, gk_o, gv_o)):
                dst[pl.ds(row, 16), at(group, (index - WIDE) // 2)] = total[:, group * k : group * (k + 1)]

        return wide if first == 0 else trio_part

    def deliver_small(total):
        small_out[...] = total


    def step(t, carry):
        for phase in range(PHASES + 1):
            index = t - LAG * phase
            for first, stop, full in kinds:

                @pl.when((index >= first) & (index < stop))
                def _():
                    grad, bufs, sends, recvs = chunk(index)
                    scatter_phase(
                        phase, (ways(0, first), ways(1, first)), full, grad, own.at[index % 3], own_sem.at[index % 3],
                        bufs, deliver(index, first), sends, recvs, credit, index, pos,
                    )

            @pl.when(index == LAST)
            def _():
                scatter_phase(
                    phase, SMALL, 128, small_g, small_own, own_sem.at[3], small_bufs, deliver_small,
                    send.at[CHUNKS], recv.at[CHUNKS], None, 0, pos,
                )

        @pl.when((t < 16) & (t % 2 == 0))
        def _():
            away(t // 2).start()

        return carry

    def advance(start, stop):
        lax.fori_loop(start, stop, step, 0)

    def weight(index, slot):
        return Halves(lambda h: pltpu.make_async_copy(wfa.at[index, h], wbuf.at[slot, :, :, :, :, h], wsem.at[slot, h]))

    def trio(g, slot):
        return Halves(
            lambda h: pltpu.make_async_copy(
                wfq.at[g, h], wbuf.at[slot, :, :, :, :, h, :, pl.ds(0, 3 * group)], wsem.at[slot, h]
            )
        )

    def shaft(j, slot):
        return Halves(
            lambda h: pltpu.make_async_copy(wfd.at[:, h, j], dbuf.at[slot, :, :, :, :, h], dsem.at[slot, h])
        )

    def store(index, slot):
        return Halves(
            lambda h: pltpu.make_async_copy(stage.at[slot, :, :, :, :, h], gw.at[index, h], stage_sem.at[slot, h])
        )

    weight(1, 0).start()
    shaft(0, 0).start()
    rows_sum[...] = rows_in[...]
    kaug[...] = key_lanes(within(lens, y, rows))
    bias_sum[...] = jnp.zeros_like(bias_sum)

    for k in (4, 0, 1, 2, 3):
        loads[k].wait()
    for jj in range(4):
        slot = jj % 2
        if jj >= 2:
            store(jj - 2, slot).wait()

        def quarter(k, carry):
            part = tn(quad[k], gdn[:, 256 * jj : 256 * (jj + 1)]).astype(BF16).reshape(2, 2, 2, 4, 2, 16, 256)
            for q in range(4):
                stage[slot, k, :, :, :, :, :, 256 * q : 256 * (q + 1)] = part[:, :, :, q]
            return carry

        lax.fori_loop(0, 4, quarter, 0)
        store(jj, slot).start()
        if jj >= 2:
            advance(jj - 2, jj - 1)
    loads[5].wait()
    loads[6].wait()
    loads[7].wait()
    keep = pltpu.make_async_copy(duo.at[1, pl.ds(0, half)], act_o.at[y, 0], out_sem.at[0])
    keep.start()
    for k in range(4):
        load(quad_i.at[k], quad.at[k], k).start()
    small_block = 128
    load(res_i.at[pl.ds(0, small_block)], rbuf.at[0], 9).start()

    def slope_load(j):
        return load(slope_i.at[j], duo.at[j % 2], 8 - j % 2)

    def square_rows(slot, n):
        return wbuf[slot, n].reshape(256, width)

    for j in range(4):
        slot = j % 2
        slope_load(j).wait()
        shaft(j, slot).wait()
        if j == 0:
            keep.wait()
        if j < 3:
            slope_load(j + 1).start()
            weight(2 + j, 1 - slot).start()
            shaft(j + 1, 1 - slot).start()
        for n in range(4):
            cols = slice(256 * n, 256 * (n + 1))
            total = nt(gdn[:, 0:256], dbuf[slot, 0, n // 2, n % 2].reshape(256, 256))
            for jj in range(1, 4):
                total = total + nt(
                    gdn[:, 256 * jj : 256 * (jj + 1)], dbuf[slot, jj, n // 2, n % 2].reshape(256, 256)
                )
            gu = (duo[slot, :, cols].astype(F32) * total).astype(BF16)
            duo[slot, :, cols] = gu
            bias_sum[8 * j : 8 * j + 1, cols] = rowsum(gu.astype(F32))
        store(2 + j, slot).wait()
        advance(2 + 2 * j, 3 + 2 * j)

        def up_grad(n, cols):
            part = tn(low[...], duo[slot, :, cols]).astype(BF16)
            stage[slot, :, :, :, :, :, :, cols] = part.reshape(4, 2, 2, 2, 2, 16, 256)

        tiles(width, 256, up_grad)
        store(4 + j, slot).start()
        advance(3 + 2 * j, 4 + 2 * j)
        weight(1 + j, slot).wait()
        for n in range(4):
            cols = slice(256 * n, 256 * (n + 1))
            acc[:, cols] += nt(duo[slot], square_rows(slot, n))
    weight(0, 0).start()
    load(xs_i, duo.at[0], 8).start()
    load(aug_i, duo.at[1], 7).start()

    def first_norm(b, carry):
        sl = pl.ds(pl.multiple_of(b * small_block, small_block), small_block)

        @pl.when(b + 1 < rows // small_block)
        def _():
            after = pl.ds(pl.multiple_of((b + 1) * small_block, small_block), small_block)
            load(res_i.at[after], rbuf.at[(b + 1) % 2], 9 + (b + 1) % 2).start()

        load(res_i.at[sl], rbuf.at[b % 2], 9 + b % 2).wait()
        normed, inverse = norm(rbuf[b % 2])
        g = acc[sl, :]
        back = norm_back(g, normed, inverse, vec[3:4, :])
        acc[sl, :] = back
        gat = back.astype(BF16)
        gdn[sl, :] = gat
        rows_sum[3:4, :] += rowsum(g * normed)
        rows_sum[4:5, :] += rowsum(g)
        rows_sum[2:3, :] += rowsum(gat.astype(F32))
        return carry

    lax.fori_loop(0, rows // small_block, first_norm, 0)
    store(6, 0).wait()
    advance(10, 11)
    for k in range(4):
        load(quad_i.at[k], quad.at[k], k).wait()

    for g in range(groups):
        for n in range(4):
            cols = slice(256 * n, 256 * (n + 1))
            part = tn(quad[g, :, 3 * group : 4 * group], gdn[:, cols]).astype(BF16)
            stage[0, g, :, :, :, :, :, cols] = part.reshape(2, 2, 2, 2, 16, 256)
    store(8, 0).start()
    weight(0, 0).wait()
    for n in range(4):
        low[:, 256 * n : 256 * (n + 1)] = nt(gdn[...], square_rows(0, n)).astype(BF16)
    store(7, 1).wait()
    advance(11, 12)
    trio(0, 0).start()
    load(xs_i, duo.at[0], 8).wait()
    load(aug_i, duo.at[1], 7).wait()
    store(8, 0).wait()

    xs, aug = duo.at[0], duo.at[1]
    low1 = (lanes((1, 128)) < 64).astype(F32).astype(BF16)
    high1 = (lanes((1, 128)) >= 64).astype(F32).astype(BF16)
    ones1 = (lanes((1, 128)) % 64 < 2).astype(F32).astype(BF16)
    alane = lanes((rows, 128))
    lower = alane < 64
    sixty = alane % 64

    def pair(g, n):
        local = pl.multiple_of(n * 128, 128)
        qc, kc, vc, cc = (pl.ds(local + group * k, 128) for k in range(4))
        cols = pl.ds(pl.multiple_of(g * group + n * 128, 128), 128)
        q2 = quad[g, :, qc]
        k2 = quad[g, :, kc]
        v2 = quad[g, :, vc]
        g2 = low[:, cols]
        au = aug[:, cols]
        prod = g2.astype(F32) * quad[g, :, cc].astype(F32)
        da = -jnp.sum(jnp.where(lower, prod, 0.0), axis=1, keepdims=True)
        db = -jnp.sum(jnp.where(lower, 0.0, prod), axis=1, keepdims=True)
        neg = jnp.where(lower, db, da)
        hi = neg.astype(BF16).astype(F32)
        daug = jnp.where(sixty == 0, hi, jnp.where(sixty == 1, neg - hi, 0.0)).astype(BF16)
        gq = []
        gk = []
        gv = []
        for head in range(2):
            mine, other = (low1, high1) if head == 0 else (high1, low1)
            qa = q2 * mine + au * other
            ga = g2 * mine + daug * other
            ka = k2 * mine + kaug[...] * other
            va = v2 * mine + ones1 * other
            parts = []
            for b in range(rows // block):
                sl = slice(b * block, (b + 1) * block)
                p = jnp.exp2(nt(ka, qa[sl]))
                ds = (p * nt(va, ga[sl])).astype(BF16)
                new_v = nn(p.astype(BF16), g2[sl])
                new_k = nn(ds, q2[sl])
                sum_v = new_v if b == 0 else sum_v + new_v
                sum_k = new_k if b == 0 else sum_k + new_k
                parts.append(tn(k2, ds))
            gq.append(parts)
            gk.append(sum_k)
            gv.append(sum_v)
        quad[g, :, kc] = (jnp.where(lower, gk[0], gk[1]) * (1.0 / LOG2E)).astype(BF16)
        quad[g, :, vc] = jnp.where(lower, gv[0], gv[1]).astype(BF16)
        for b in range(rows // block):
            sl = slice(b * block, (b + 1) * block)
            both = jnp.concatenate([gq[0][b][0:64], gq[1][b][64:128]], axis=0) * 0.125
            quad[g, sl, qc] = both.T.astype(BF16)

    def token_rows(g, slot, sl):
        for n in range(4):
            cols = slice(256 * n, 256 * (n + 1))
            acc[sl, cols] += nt(quad[g, sl, 0 : 3 * group], wbuf[slot, n, :, :, :, :, :, 0 : 3 * group].reshape(256, 3 * group))

    def trio_grad(g):
        at = pl.ds(pl.multiple_of(g * group, group), group)
        for k in range(3):
            part = tn(xs[...], quad[g, :, group * k : group * (k + 1)]).astype(BF16)
            stage[1, :, :, :, :, :, :, group * k : group * (k + 1)] = part.reshape(4, 2, 2, 2, 2, 16, group)
        rows_sum[0:1, at] = rowsum(quad[g, :, 0:group].astype(F32))
        rows_sum[1:2, at] = rowsum(quad[g, :, 2 * group : 3 * group].astype(F32))

    def attend(g, carry):
        def run(n, carry):
            @pl.when((g > 0) & (n == 1))
            def _():
                store(8 + g, 1).wait()

            @pl.when(g + n > 0)
            def _():
                advance(11 + 3 * g + n, 12 + 3 * g + n)

            pair(g, n)
            return carry

        lax.fori_loop(0, 2, run, 0)
        advance(13 + 3 * g, 14 + 3 * g)

        @pl.when(g < groups - 1)
        def _():
            trio(g, 0).wait()
            token_rows(g, 0, slice(0, rows))
            trio(g + 1, 0).start()

            trio_grad(g)
            store(9 + g, 1).start()

        return carry

    lax.fori_loop(0, groups, attend, 0)
    last = groups - 1

    advance(LAST - 2, LAST - 1)
    trio(last, 0).wait()
    token_rows(last, 0, slice(half, rows))
    low[0:half, :] = acc[half:rows, :].astype(BF16)
    turn = pltpu.make_async_remote_copy(
        src_ref=low.at[pl.ds(0, half)],
        dst_ref=home,
        send_sem=swap_send.at[8],
        recv_sem=swap_recv.at[8],
        device_id=device(z, x, c, 1 - y),
        device_id_type=MESH,
    )
    turn.start()
    trio_grad(last)
    store(9 + last, 1).start()
    for zz in range(4):
        for s in range(8):
            at = 2 * zz + s // 4
            tile = jnp.concatenate(
                [
                    rows_sum[:, 128 * at : 128 * (at + 1)],
                    bias_sum[8 * zz : 8 * zz + 8, 128 * s : 128 * (s + 1)],
                ],
                axis=0,
            )
            small_g[zz, s // 4, (s // 2) % 2, s % 2] = tile.astype(BF16)
    store(9 + last, 1).wait()
    advance(LAST - 1, LAST + 1)
    token_rows(last, 0, slice(0, half))
    kept = pltpu.make_async_copy(acc.at[pl.ds(0, half)], gtok_o.at[y, 0], out_sem.at[0])
    kept.start()
    advance(LAST + 1, LAST + LAG * PHASES + 1)
    turn.wait()
    acc[half:rows, :] = home[...].astype(F32)
    came = pltpu.make_async_copy(acc.at[pl.ds(half, half)], gtok_o.at[1 - y, 0], out_sem.at[1])
    came.start()
    for index in range(8):
        away(index).wait()

    def finish(index, carry):
        for first, stop, full in kinds:

            @pl.when((index >= first) & (index < stop))
            def _():
                grad, bufs, sends, recvs = chunk(index)
                scatter_sent((ways(0, first), ways(1, first)), full, grad, bufs, sends, recvs, pos)

        return carry

    lax.fori_loop(0, CHUNKS, finish, 0)
    scatter_sent(SMALL, 128, small_g, small_bufs, send.at[CHUNKS], recv.at[CHUNKS], pos)
    kept.wait()
    came.wait()


def backward_pass(wfq, wfa, wfd, saved, vec, rows_in, lens):
    rows, width = saved[0].shape
    six = (4, 2, 2, 2)
    vmem = pl.BlockSpec(memory_space=VMEM)
    hbm = pl.BlockSpec(memory_space=ANY)
    dma = pltpu.SemaphoreType.DMA

    def buffers(rows, width, depth, count):
        return [
            VMEM(depth + (4, 2, 2, rows, width), BF16),
            VMEM(count + (4, 2, rows, width), BF16),
            VMEM(count + (6, rows, width), BF16),
            VMEM(count + (3, rows, width), BF16),
        ]

    return pl.pallas_call(
        backward_kernel,
        out_shape=(
            jax.ShapeDtypeStruct((CHUNKS // 2, 2) + six + (16, width), BF16),
            jax.ShapeDtypeStruct((2, 1, rows // 2, width), BF16),
            jax.ShapeDtypeStruct((2, 1, rows // 2, width), F32),
            jax.ShapeDtypeStruct((32, width), F32),
            jax.ShapeDtypeStruct((32, width), F32),
            jax.ShapeDtypeStruct((32, width), F32),
            jax.ShapeDtypeStruct((32, width), F32),
            jax.ShapeDtypeStruct((32, 4 * width), F32),
            jax.ShapeDtypeStruct((128, width), F32),
            jax.ShapeDtypeStruct((16, 128), F32),
        ),
        in_specs=[hbm] * 13 + [vmem] * 2 + [pl.BlockSpec(memory_space=pltpu.SMEM)],
        out_specs=[hbm] * 3 + [vmem] * 7,
        scratch_shapes=[
            VMEM((rows, width), F32),
            VMEM((2, 128, width), F32),
            VMEM((rows, width), BF16),
            VMEM((rows, width), BF16),
            VMEM((4, rows, width), BF16),
            VMEM((2, rows, width), BF16),
            VMEM((2,) + six + (2, 16, width), BF16),
            VMEM((2, 4, 2, 2, 2, 2, 64, 256), BF16),
            VMEM((2,) + six + (2, 16, width), BF16),
            VMEM((3, 4, 2, 2, 16, width), BF16),
        ]
        + buffers(16, width, (DEPTH,), (CHUNKS,))
        + [
            VMEM((rows // 2, width), BF16),
            VMEM((8, width), F32),
            VMEM((32, width), F32),
            VMEM(six + (16, 128), BF16),
            VMEM((4, 2, 2, 16, 128), BF16),
        ]
        + buffers(16, 128, (), ())
        + [
            VMEM((rows, 128), BF16),
            dma((CHUNKS + 1, SLOTS)),
            dma((CHUNKS + 1, SLOTS)),
            dma((4,)),
            pltpu.SemaphoreType.REGULAR,
            dma((9,)),
            dma((9,)),
            dma((11,)),
            dma((2, 2)),
            dma((2, 2)),
            dma((2, 2)),
            dma((2,)),
        ],
        compiler_params=pltpu.CompilerParams(collective_id=1, has_side_effects=True, vmem_limit_bytes=61 * 1024 * 1024),
        cost_estimate=pl.CostEstimate(flops=2 * 32 * rows * width * width, bytes_accessed=90 << 20, transcendentals=1 << 24),
        name="backward_pass",
    )(wfq, wfa, wfd, *saved, vec, rows_in, lens)


def paired(
    tokens, lengths, w_query, w_key, w_value, w_out, w_up, w_down, vectors, up_bias, cotangent
):
    y = lax.axis_index("seq")
    rank = lax.axis_index("dp") * 2 + y
    spot = jnp.tile(vectors, (1, 4)) * (jnp.arange(128) // 32 == rank % 4).astype(BF16)
    sm = jnp.concatenate([spot, up_bias[None, :], jnp.zeros((7, 128), BF16)])
    weights = (w_query, w_key, w_value, w_out, w_up, w_down)
    wfq, wfa, wfd, _, *saved, vec, rows_in = forward_pass(weights, sm, tokens, cotangent, lengths)
    _, activations, grad_tokens, *grads, small = backward_pass(wfq, wfa, wfd, saved, vec, rows_in, lengths)
    return (
        activations,
        grad_tokens,
        *grads,
        lax.dynamic_slice_in_dim(small[0:8], (rank % 4) * 32, 32, axis=1),
        small[8],
    )


def solution(mesh):
    placed = (
        P(None, "dp", "seq", None),
        P(None, "dp"),
        P(("dp", "seq"), None),
        P(("dp", "seq"), None),
        P(("dp", "seq"), None),
        P(("dp", "seq"), None),
        P(("dp", "seq"), None),
        P(("dp", "seq"), None),
        P(None, ("dp", "seq")),
        P(("dp", "seq")),
        P(None, "dp", "seq", None),
    )
    own = mesh.shape["dp"] == 16 and mesh.shape["seq"] == 2
    return jax.shard_map(
        paired if own else per_device,
        mesh=mesh,
        in_specs=placed,
        out_specs=(
            P(None, "dp", "seq", None),
            P(None, "dp", "seq", None),
            P(("dp", "seq"), None),
            P(("dp", "seq"), None),
            P(("dp", "seq"), None),
            P(("dp", "seq"), None),
            P(("dp", "seq"), None),
            P(("dp", "seq"), None),
            P(None, ("dp", "seq")),
            P(("dp", "seq")),
        ),
        check_vma=False,
    )
```

```python
import functools
import math

import jax
import jax.numpy as jnp
from jax import lax
from jax.experimental import pallas as pl
from jax.experimental.pallas import tpu as pltpu
from jax.sharding import PartitionSpec as P

H = 16


EPSILON = 1e-05


def fetch_forward(w_query, w_key, w_value, w_out, w_up, w_down, vectors, up_bias):
    return (
        lax.all_gather(w_query, ("dp", "seq"), axis=0, tiled=True),
        lax.all_gather(w_key, ("dp", "seq"), axis=0, tiled=True),
        lax.all_gather(w_value, ("dp", "seq"), axis=0, tiled=True),
        lax.all_gather(w_out, ("dp", "seq"), axis=0, tiled=True),
        lax.all_gather(w_up, ("dp", "seq"), axis=0, tiled=True),
        lax.all_gather(w_down, ("dp", "seq"), axis=0, tiled=True),
        lax.all_gather(vectors, ("dp", "seq"), axis=1, tiled=True),
        lax.all_gather(up_bias, ("dp", "seq"), axis=0, tiled=True),
    )


def fetch_backward(w_query, w_key, w_value, w_out, w_up, w_down, vectors, up_bias):
    return (
        lax.all_gather(w_query, ("dp", "seq"), axis=0, tiled=True),
        lax.all_gather(w_key, ("dp", "seq"), axis=0, tiled=True),
        lax.all_gather(w_value, ("dp", "seq"), axis=0, tiled=True),
        lax.all_gather(w_out, ("dp", "seq"), axis=0, tiled=True),
        lax.all_gather(w_up, ("dp", "seq"), axis=0, tiled=True),
        lax.all_gather(w_down, ("dp", "seq"), axis=0, tiled=True),
        lax.all_gather(vectors, ("dp", "seq"), axis=1, tiled=True),
        lax.all_gather(up_bias, ("dp", "seq"), axis=0, tiled=True),
    )


def norm_forward(inputs, gain, shift):
    center = inputs - jnp.mean(inputs, axis=-1, keepdims=True)
    inverse = lax.rsqrt(jnp.mean(center * center, axis=-1, keepdims=True) + EPSILON)
    normed = center * inverse
    return (normed * gain + shift, normed, inverse)


def norm_backward(grad_out, normed, inverse, gain):
    grad_norm = grad_out * gain
    inner = (
        grad_norm
        - jnp.mean(grad_norm, axis=-1, keepdims=True)
        - normed * jnp.mean(grad_norm * normed, axis=-1, keepdims=True)
    )
    return (inner * inverse, jnp.sum(grad_out * normed, axis=0), jnp.sum(grad_out, axis=0))


def score_heads(query_heads, key_heads, key_valid, factor):
    scores = (
        jnp.einsum("qhd,khd->hqk", query_heads, key_heads, preferred_element_type=jnp.float32)
        * factor
    )
    return jnp.where(key_valid[None, None, :], scores, -1000000000.0)


def per_device(
    tokens, lengths, w_query, w_key, w_value, w_out, w_up, w_down, vectors, up_bias, cotangent
):
    micro = tokens.shape[0]
    slot = tokens.shape[2]
    width = tokens.shape[3]
    hidden_units = w_up.shape[1]
    heads = H
    head_dim = width // heads
    factor = 1.0 / math.sqrt(head_dim)
    positions = lax.axis_index("seq") * slot + jnp.arange(slot, dtype=jnp.int32)
    f32 = jnp.float32
    sums = [
        jnp.zeros((width, width), f32),
        jnp.zeros((width, width), f32),
        jnp.zeros((width, width), f32),
        jnp.zeros((width, width), f32),
        jnp.zeros((width, hidden_units), f32),
        jnp.zeros((hidden_units, width), f32),
        jnp.zeros((8, width), f32),
        jnp.zeros((hidden_units,), f32),
    ]
    outputs = []
    grad_list = []
    for micro_index in range(micro):
        full_query, full_key, full_value, full_out, full_up, full_down, full_vectors, full_bias = (
            fetch_forward(w_query, w_key, w_value, w_out, w_up, w_down, vectors, up_bias)
        )
        vec_f = full_vectors.astype(f32)
        bias_f = full_bias.astype(f32)
        rows_in = tokens[micro_index, 0]
        length = lengths[micro_index, 0]
        valid = (positions < length)[:, None].astype(f32)
        query = (jnp.dot(rows_in, full_query, preferred_element_type=f32) + vec_f[0]).astype(
            jnp.bfloat16
        )
        keys_own = jnp.dot(rows_in, full_key, preferred_element_type=f32).astype(jnp.bfloat16)
        vals_own = (jnp.dot(rows_in, full_value, preferred_element_type=f32) + vec_f[1]).astype(
            jnp.bfloat16
        )
        keys_all, vals_all = (
            lax.all_gather(keys_own, "seq", axis=0, tiled=True),
            lax.all_gather(vals_own, "seq", axis=0, tiled=True),
        )
        total_len = keys_all.shape[0]
        key_valid = jnp.arange(total_len, dtype=jnp.int32) < length
        query_heads = query.reshape(slot, heads, head_dim)
        key_heads = keys_all.reshape(total_len, heads, head_dim)
        val_heads = vals_all.reshape(total_len, heads, head_dim)
        scores = score_heads(query_heads, key_heads, key_valid, factor)
        top = jnp.max(scores, axis=-1, keepdims=True)
        log_total = top + jnp.log(jnp.sum(jnp.exp(scores - top), axis=-1, keepdims=True))
        probs = jnp.exp(scores - log_total).astype(jnp.bfloat16)
        context = (
            jnp.einsum("hqk,khd->qhd", probs, val_heads, preferred_element_type=f32)
            .reshape(slot, width)
            .astype(jnp.bfloat16)
        )
        attention = jnp.dot(context, full_out, preferred_element_type=f32) + vec_f[2]
        hidden, normed_one, inverse_one = norm_forward(
            rows_in.astype(f32) + attention, vec_f[3], vec_f[4]
        )
        hidden_low = hidden.astype(jnp.bfloat16)
        upper = jnp.dot(hidden_low, full_up, preferred_element_type=f32) + bias_f
        active = jax.nn.gelu(upper).astype(jnp.bfloat16)
        lowered = jnp.dot(active, full_down, preferred_element_type=f32) + vec_f[5]
        result, normed_two, inverse_two = norm_forward(hidden + lowered, vec_f[6], vec_f[7])
        outputs.append((result * valid).astype(jnp.bfloat16))
        full_query, full_key, full_value, full_out, full_up, full_down, full_vectors, full_bias = (
            fetch_backward(w_query, w_key, w_value, w_out, w_up, w_down, vectors, up_bias)
        )
        vec_f = full_vectors.astype(f32)
        grad_out = cotangent[micro_index, 0].astype(f32) * valid
        grad_res2, grad_gain2, grad_shift2 = norm_backward(
            grad_out, normed_two, inverse_two, vec_f[6]
        )
        grad_down = grad_res2.astype(jnp.bfloat16)
        grad_bias2 = jnp.sum(grad_down.astype(f32), axis=0)
        sums[5] = sums[5] + jnp.einsum("sf,sd->fd", active, grad_down, preferred_element_type=f32)
        grad_active = jnp.einsum("sd,fd->sf", grad_down, full_down, preferred_element_type=f32)
        gelu_pull = jax.vjp(jax.nn.gelu, upper)[1]
        grad_upper = gelu_pull(grad_active)[0].astype(jnp.bfloat16)
        sums[7] = sums[7] + jnp.sum(grad_upper.astype(f32), axis=0)
        sums[4] = sums[4] + jnp.einsum(
            "sd,sf->df", hidden_low, grad_upper, preferred_element_type=f32
        )
        grad_hidden = grad_res2 + jnp.einsum(
            "sf,df->sd", grad_upper, full_up, preferred_element_type=f32
        )
        grad_res1, grad_gain1, grad_shift1 = norm_backward(
            grad_hidden, normed_one, inverse_one, vec_f[3]
        )
        grad_att = grad_res1.astype(jnp.bfloat16)
        grad_bias_out = jnp.sum(grad_att.astype(f32), axis=0)
        sums[3] = sums[3] + jnp.einsum("sd,se->de", context, grad_att, preferred_element_type=f32)
        grad_context = jnp.einsum(
            "se,de->sd", grad_att, full_out, preferred_element_type=f32
        ).astype(jnp.bfloat16)
        grad_ctx_heads = grad_context.reshape(slot, heads, head_dim)
        scores_again = score_heads(query_heads, key_heads, key_valid, factor)
        full_probs = jnp.exp(scores_again - log_total)
        probs_low = full_probs.astype(jnp.bfloat16)
        grad_probs = jnp.einsum(
            "qhd,khd->hqk", grad_ctx_heads, val_heads, preferred_element_type=f32
        )
        grad_val_term = jnp.einsum(
            "hqk,qhd->khd", probs_low, grad_ctx_heads, preferred_element_type=f32
        )
        row_inner = jnp.sum(full_probs * grad_probs, axis=-1, keepdims=True)
        grad_scores = (full_probs * (grad_probs - row_inner)).astype(jnp.bfloat16)
        grad_query = (
            (
                jnp.einsum("hqk,khd->qhd", grad_scores, key_heads, preferred_element_type=f32)
                * factor
            )
            .reshape(slot, width)
            .astype(jnp.bfloat16)
        )
        grad_key_term = (
            jnp.einsum("hqk,qhd->khd", grad_scores, query_heads, preferred_element_type=f32)
            * factor
        )
        grad_keys, grad_vals = (
            lax.psum_scatter(
                grad_key_term.reshape(total_len, width).astype(jnp.bfloat16),
                "seq",
                scatter_dimension=0,
                tiled=True,
            ).astype(jnp.float32),
            lax.psum_scatter(
                grad_val_term.reshape(total_len, width).astype(jnp.bfloat16),
                "seq",
                scatter_dimension=0,
                tiled=True,
            ).astype(jnp.float32),
        )
        grad_keys = grad_keys.astype(jnp.bfloat16)
        grad_vals = grad_vals.astype(jnp.bfloat16)
        grad_bias_query = jnp.sum(grad_query.astype(f32), axis=0)
        grad_bias_vals = jnp.sum(grad_vals.astype(f32), axis=0)
        sums[0] = sums[0] + jnp.einsum("sd,se->de", rows_in, grad_query, preferred_element_type=f32)
        sums[1] = sums[1] + jnp.einsum("sd,se->de", rows_in, grad_keys, preferred_element_type=f32)
        sums[2] = sums[2] + jnp.einsum("sd,se->de", rows_in, grad_vals, preferred_element_type=f32)
        sums[6] = sums[6] + jnp.stack(
            [
                grad_bias_query,
                grad_bias_vals,
                grad_bias_out,
                grad_gain1,
                grad_shift1,
                grad_bias2,
                grad_gain2,
                grad_shift2,
            ]
        )
        grad_rows = grad_res1 + jnp.einsum(
            "se,de->sd", grad_query, full_query, preferred_element_type=f32
        )
        grad_rows = grad_rows + jnp.einsum(
            "se,de->sd", grad_keys, full_key, preferred_element_type=f32
        )
        grad_rows = grad_rows + jnp.einsum(
            "se,de->sd", grad_vals, full_value, preferred_element_type=f32
        )
        grad_list.append(grad_rows)
    shares = (
        lax.psum_scatter(sums[0], ("dp", "seq"), scatter_dimension=0, tiled=True),
        lax.psum_scatter(sums[1], ("dp", "seq"), scatter_dimension=0, tiled=True),
        lax.psum_scatter(sums[2], ("dp", "seq"), scatter_dimension=0, tiled=True),
        lax.psum_scatter(sums[3], ("dp", "seq"), scatter_dimension=0, tiled=True),
        lax.psum_scatter(sums[4], ("dp", "seq"), scatter_dimension=0, tiled=True),
        lax.psum_scatter(sums[5], ("dp", "seq"), scatter_dimension=0, tiled=True),
        lax.psum_scatter(sums[6], ("dp", "seq"), scatter_dimension=1, tiled=True),
        lax.psum_scatter(sums[7], ("dp", "seq"), scatter_dimension=0, tiled=True),
    )
    activations = jnp.stack(outputs)[:, None]
    grad_tokens = jnp.stack(grad_list)[:, None]
    return (
        activations,
        grad_tokens,
        shares[0],
        shares[1],
        shares[2],
        shares[3],
        shares[4],
        shares[5],
        shares[6],
        shares[7],
    )


MESH = pl.DeviceIdType.MESH
F32 = jnp.float32
BF16 = jnp.bfloat16
ANY = pl.ANY
VMEM = pltpu.VMEM
LOG2E = math.log2(math.e)
LIMIT = 58 * 1024 * 1024
GELU_C = math.sqrt(2.0 / math.pi)
GELU_A = 0.044715


def nt(a, b):
    return lax.dot_general(a, b, (((1,), (1,)), ((), ())), preferred_element_type=F32)


def nn(a, b):
    return lax.dot_general(a, b, (((1,), (0,)), ((), ())), preferred_element_type=F32)


def tn(a, b):
    return lax.dot_general(a, b, (((0,), (0,)), ((), ())), preferred_element_type=F32)


def place():
    dp = lax.axis_index("dp")
    return dp // 4, (dp // 2) % 2, dp % 2, lax.axis_index("seq")


def device(z, x, c, y):
    return (z * 4 + x * 2 + c, y)


def greet(z, x, c, y):
    barrier = pltpu.get_barrier_semaphore()
    partners = [device(z, x, 1 - c, y), device(z, 1 - x, c, y), device(z, x, c, 1 - y)]
    partners += [device((z + d) % 4, x, c, y) for d in (1, 2, 3)]
    for partner in partners:
        pl.semaphore_signal(barrier, inc=1, device_id=partner, device_id_type=MESH)
    pl.semaphore_wait(barrier, len(partners))


PHASES = 4
LAG = 2
WARM = PHASES * (LAG - 1)
SLOTS = 6


def gather_copies(ref, cross, send, recv, core, phase, pos):
    z, x, c, y = pos
    every = slice(None)
    order = "yzxc" if core == 0 else "zyxc" if cross else "zxyc"
    done = order[:phase]
    have = (
        every if "z" in done else z,
        every if "x" in done else x,
        every if "c" in done else c,
        every if "y" in done else y,
    )
    axis = order[phase]
    if axis == "z":
        targets = [(2 + d, ((z + d) % 4, x, c, y)) for d in (1, 2, 3)]
    elif axis == "x":
        targets = [(0, (z, 1 - x, c, y))]
    elif axis == "y":
        targets = [(1, (z, x, c, 1 - y))]
    else:
        targets = [(2, (z, x, 1 - c, y))]
    return [
        pltpu.make_async_remote_copy(
            src_ref=ref.at[have],
            dst_ref=ref.at[have],
            send_sem=send.at[slot],
            recv_sem=recv.at[slot],
            device_id=device(*target),
            device_id_type=MESH,
        )
        for slot, target in targets
    ]


def gather_phase(ref, cross, send, recv, phase, pos):
    for core in (0, 1):

        @pl.when(pos[2] == core)
        def _():
            if phase > 0:
                for copy in gather_copies(ref, cross, send, recv, core, phase - 1, pos):
                    copy.wait_recv()
            if phase < PHASES:
                for copy in gather_copies(ref, cross, send, recv, core, phase, pos):
                    copy.start()


def gather_sent(ref, cross, send, recv, pos):
    for core in (0, 1):

        @pl.when(pos[2] == core)
        def _():
            for phase in range(PHASES):
                for copy in gather_copies(ref, cross, send, recv, core, phase, pos):
                    copy.wait_send()


class Halves:
    def __init__(self, make):
        self.make = make

    def start(self):
        for h in range(2):
            self.make(h).start()

    def wait(self):
        for h in range(2):
            self.make(h).wait()


def lanes(shape):
    return lax.broadcasted_iota(jnp.int32, shape, len(shape) - 1)


def norm(v):
    center = v - jnp.mean(v, axis=-1, keepdims=True)
    inverse = lax.rsqrt(jnp.mean(center * center, axis=-1, keepdims=True) + EPSILON)
    return center * inverse, inverse


def norm_back(g, normed, inverse, gain):
    gn = g * gain
    inner = gn - jnp.mean(gn, axis=-1, keepdims=True) - normed * jnp.mean(gn * normed, axis=-1, keepdims=True)
    return inner * inverse


def within(lens, y, rows):
    row = lax.broadcasted_iota(jnp.int32, (rows, 128), 0)
    half = rows // 2
    position = jnp.where(row < half, y * half + row, (1 - y) * half + row - half)
    return position < lens[y, 0]


def key_lanes(ok):
    sixty = lanes(ok.shape) % 64
    ones = ((sixty > 0) & (sixty < 4)).astype(F32)
    return jnp.where(sixty == 0, jnp.where(ok, 0.0, -1e9), ones).astype(BF16)


def rowsum(v):
    return jnp.sum(v, axis=0, keepdims=True)


def blocks(rows, block, body, straight=False):
    def run(b, carry):
        body(pl.ds(pl.multiple_of(b * block, block), block))
        return carry

    lax.fori_loop(0, rows // block, run, 0, unroll=straight)


def tiles(width, tile, body):
    def run(b, carry):
        body(b, pl.ds(pl.multiple_of(b * tile, tile), tile))
        return carry

    lax.fori_loop(0, width // tile, run, 0)


def forward_kernel(
    wq, wk, wv, wo, wup, wdown, sm, tok, cot, lens,
    wfq, wfa, wfd, sf, xs_o, quad_o, aug_o, res_o, low_o, act_o, slope_o, back_o, gdn_o, out_o, vec, rows_out,
    xs, ct, quad, aug, res, acc, low, actv, slope, wbuf, dbuf, small, out, kaug, valid,
    send, recv, place_sem, own_sem, swap_send, swap_recv, wsem, dsem, out_sem,
):
    pos = place()
    z, x, c, y = pos
    rows, width = xs.shape
    half = rows // 2
    group = 256
    groups = width // group
    wide_from = 2 * groups
    tall_from = wide_from + 10
    chunks = tall_from + 8

    first = []

    def put(src, dst):
        first.append(pltpu.make_async_copy(src, dst, place_sem.at[len(first)]))

    for h in range(2):
        top = slice(16 * h, 16 * h + 16)
        for g in range(groups):
            for k, w in enumerate((wq, wk, wv)):
                put(
                    w.at[top, group * g : group * (g + 1)],
                    wfq.at[g, h, z, x, c, y, :, pl.ds(group * k, group)],
                )
        put(wo.at[top], wfa.at[0, h, z, x, c, y])
        for j in range(4):
            put(wup.at[top, width * j : width * (j + 1)], wfa.at[1 + j, h, z, x, c, y])
            put(wdown.at[64 * h : 64 * h + 64, 256 * j : 256 * (j + 1)], wfd.at[j, h, z, x, c, y])
    put(sm, sf.at[z, x, c, y])
    for copy in first:
        copy.start()
    mine = [
        pltpu.make_async_copy(tok.at[y, 0], xs.at[pl.ds(0, half)], own_sem.at[0]),
        pltpu.make_async_copy(cot.at[y, 0], ct.at[pl.ds(0, half)], own_sem.at[1]),
    ]
    for copy in mine:
        copy.start()
    greet(*pos)
    for copy in first:
        copy.wait()

    piece = half // 8

    def swap(src, dst, slot, index):
        at = pl.multiple_of(index * piece, piece)
        return pltpu.make_async_remote_copy(
            src_ref=src.at[1 - y, 0, pl.ds(at, piece)],
            dst_ref=dst.at[pl.ds(half + at, piece)],
            send_sem=swap_send.at[slot, index],
            recv_sem=swap_recv.at[slot, index],
            device_id=device(z, x, c, 1 - y),
            device_id_type=MESH,
        )

    def chunk(index, kind):
        odd = index % 2
        if kind == 0:
            ref = wfq.at[index // 2, odd]
        elif kind == 1:
            ref = wfa.at[(index - wide_from) // 2, odd]
        else:
            ref = wfd.at[(index - tall_from) // 2, odd]
        return (ref, kind == 0, send.at[index], recv.at[index])

    tiny = (sf, False, send.at[chunks], recv.at[chunks])

    def kinds(index, body):
        for kind, (start, stop) in enumerate(((0, wide_from), (wide_from, tall_from), (tall_from, chunks))):

            @pl.when((index >= start) & (index < stop))
            def _():
                body(chunk(index, kind))

    def step(t, carry):
        for phase in range(PHASES + 1):
            index = t - LAG * phase
            kinds(index, lambda parts: gather_phase(*parts, phase, pos))

            @pl.when(index == 0)
            def _():
                gather_phase(*tiny, phase, pos)

        @pl.when(t < 8)
        def _():
            swap(tok, xs, 0, t).start()

        @pl.when((t >= 8) & (t < 24) & (t % 2 == 0))
        def _():
            swap(cot, ct, 1, t // 2 - 4).start()

        return carry

    def advance(start, stop):
        lax.fori_loop(start, stop, step, 0)

    def weight(index, slot):
        return Halves(lambda h: pltpu.make_async_copy(wfa.at[index, h], wbuf.at[slot, :, :, :, :, h], wsem.at[slot, h]))

    def trio(g):
        return Halves(
            lambda h: pltpu.make_async_copy(
                wfq.at[g, h], wbuf.at[0, :, :, :, :, h, :, pl.ds(0, 3 * group)], wsem.at[0, h]
            )
        )

    def square(slot, cols):
        return wbuf[slot, :, :, :, :, :, :, cols].reshape(width, cols.size)

    def save(src, dst, slot):
        copy = pltpu.make_async_copy(src, dst, out_sem.at[slot])
        copy.start()
        return copy

    advance(0, 6 + WARM)
    trio(0).start()
    for index in range(8):
        swap(tok, xs, 0, index).wait_recv()
    for copy in mine:
        copy.wait()
    saves = [save(xs, xs_o, 0)]
    ok = within(lens, y, rows)
    kaug[...] = key_lanes(ok)
    valid[...] = ok.astype(F32)
    gathered = pltpu.make_async_copy(sf, small, own_sem.at[2])
    gathered.start()
    gathered.wait()
    tiles32 = [small[a, b, d, e].astype(F32) for a in range(4) for b in range(2) for d in range(2) for e in range(2)]
    for g in range(8):
        vec[0:8, 128 * g : 128 * g + 128] = sum(tiles32[4 * g + s] for s in range(4))[0:8]
    for r in range(4):
        for g in range(8):
            vec[8 + r : 9 + r, 128 * g : 128 * g + 128] = tiles32[8 * r + g][8:9]
    vec[12:16, :] = jnp.zeros((4, width), F32)

    block = 256
    low1 = (lanes((1, 128)) < 64).astype(F32).astype(BF16)
    high1 = (lanes((1, 128)) >= 64).astype(F32).astype(BF16)
    ones1 = (lanes((1, 128)) % 64 == 0).astype(F32).astype(BF16)
    qlane = lanes((block, 128))
    sixty = qlane % 64

    def heads(g, at):
        def run(n, carry):
            pair(g, at, n)
            advance(WARM + 6 + 3 * g + n, WARM + 7 + 3 * g + 2 * n)
            return carry

        lax.fori_loop(0, 2, run, 0)

    def pair(g, at, n):
        local = pl.multiple_of(n * 128, 128)
        qc, kc, vc, cc = (pl.ds(local + group * k, 128) for k in range(4))
        cols = pl.ds(pl.multiple_of(g * group + n * 128, 128), 128)
        k2 = quad[g, :, kc]
        v2 = quad[g, :, vc]
        ka = k2 * low1 + kaug[...] * high1
        kb = k2 * high1 + kaug[...] * low1

        def query_block(sl):
            q2 = quad[g, sl, qc]
            parts = []
            for own, other, kk in ((low1, high1, ka), (high1, low1, kb)):
                s = nt(q2 * own + ones1 * other, kk)
                top = jnp.max(s, axis=1, keepdims=True)
                e = jnp.exp2(s - top)
                total = jnp.sum(e, axis=1, keepdims=True)
                o = nn(e.astype(BF16), v2)
                parts.append((o / total, -(top + jnp.log2(total))))
            lower = qlane < 64
            quad[g, sl, cc] = jnp.where(lower, parts[0][0], parts[1][0]).astype(BF16)
            neg = jnp.where(lower, parts[1][1], parts[0][1])
            hi = neg.astype(BF16).astype(F32)
            mid = (neg - hi).astype(BF16).astype(F32)
            lo = neg - hi - mid
            aug[sl, cols] = jnp.where(
                sixty == 0,
                1.0,
                jnp.where(sixty == 1, hi, jnp.where(sixty == 2, mid, jnp.where(sixty == 3, lo, 0.0))),
            ).astype(BF16)

        blocks(rows, block, query_block, True)

    def attend(g, carry):
        trio(g).wait()
        at = pl.ds(pl.multiple_of(g * group, group), group)
        for k in range(3):
            out_k = nn(xs[...], square(0, pl.ds(group * k, group)))
            if k == 0:
                out_k = (out_k + vec[0:1, at]) * (LOG2E / 8.0)
            elif k == 2:
                out_k = out_k + vec[1:2, at]
            quad[g, :, group * k : group * (k + 1)] = out_k.astype(BF16)
        heads(g, at)

        @pl.when(g < groups - 1)
        def _():
            trio(g + 1).start()

        return carry

    lax.fori_loop(0, groups, attend, 0)
    weight(0, 1).start()
    for g in range(groups):
        saves.append(save(quad.at[g], quad_o.at[g], 1 + g))
    saves.append(save(aug, aug_o, 5))
    weight(0, 1).wait()

    def project_out(n, cols):
        total = vec[2:3, cols]
        for g in range(groups):
            total = total + nn(quad[g, :, 3 * group : 4 * group], wbuf[1, g, :, :, :, :, :, cols].reshape(group, group))
        res[:, cols] = xs[:, cols].astype(F32) + total

    tiles(width, 256, project_out)
    weight(1, 0).start()
    saves.append(save(res, res_o, 6))

    def normalize(sl):
        normed, _ = norm(res[sl, :])
        low[sl, :] = (normed * vec[3:4, :] + vec[4:5, :]).astype(BF16)

    blocks(rows, block, normalize)
    saves.append(save(low, low_o, 7))

    def shaft(j, slot):
        return Halves(lambda h: pltpu.make_async_copy(wfd.at[j, h], dbuf.at[slot, :, :, :, :, h], dsem.at[slot, h]))

    for j in range(4):
        weight(1 + j, j % 2).wait()

        def climb(n, cols):
            up = nn(low[...], square(j % 2, cols)) + vec[8 + j : 9 + j, cols]
            sq = up * up
            t = jnp.tanh(up * (GELU_C + (GELU_C * GELU_A) * sq))
            hf = 0.5 * up
            actv[j, :, cols] = (hf + hf * t).astype(BF16)
            slope[j, :, cols] = (
                0.5 + 0.5 * t + hf * (1.0 - t * t) * (GELU_C + (3.0 * GELU_C * GELU_A) * sq)
            ).astype(BF16)

            @pl.when(n == 1)
            def _():
                advance(WARM + 18 + 2 * j, WARM + 19 + 2 * j)

        tiles(width, 256, climb)
        advance(WARM + 19 + 2 * j, WARM + 20 + 2 * j)
        if j < 3:
            weight(2 + j, (1 + j) % 2).start()
        else:
            shaft(0, 0).start()
        saves.append(save(actv.at[j], act_o.at[j], 8 + j))
        saves.append(save(slope.at[j], slope_o.at[j], 12 + j))

    for j in range(4):
        shaft(j, j % 2).wait()
        cols = slice(256 * j, 256 * (j + 1))

        def slide(k, carry):
            part = nn(actv[k], dbuf[j % 2, k].reshape(width, 256))

            @pl.when(k == 0)
            def _():
                acc[:, cols] = part + vec[5:6, cols]

            @pl.when(k > 0)
            def _():
                acc[:, cols] += part

            return carry

        lax.fori_loop(0, 4, slide, 0)
        if j < 3:
            advance(WARM + 26 + 2 * j, min(WARM + 28 + 2 * j, chunks + LAG * PHASES))
            shaft(1 + j, (1 + j) % 2).start()

    for index in range(8):
        swap(cot, ct, 1, index).wait_recv()
    rows_out[...] = jnp.zeros_like(rows_out)

    def middle(sl):
        normed, _ = norm(res[sl, :])
        hidden = normed * vec[3:4, :] + vec[4:5, :]
        normed, inverse = norm(hidden + acc[sl, :])
        ok = valid[sl, 0:1]
        out[sl, :] = ((normed * vec[6:7, :] + vec[7:8, :]) * ok).astype(BF16)
        g = ct[sl, :].astype(F32) * ok
        back = norm_back(g, normed, inverse, vec[6:7, :])
        acc[sl, :] = back
        gd = back.astype(BF16)
        ct[sl, :] = gd
        rows_out[6:7, :] += rowsum(g * normed)
        rows_out[7:8, :] += rowsum(g)
        rows_out[5:6, :] += rowsum(gd.astype(F32))

    blocks(rows, block, middle)
    saves.append(save(out, out_o, 16))
    saves.append(save(acc, back_o, 17))
    saves.append(save(ct, gdn_o, 18))

    def finish(index, carry):
        kinds(index, lambda parts: gather_sent(*parts, pos))
        return carry

    lax.fori_loop(0, chunks, finish, 0)
    gather_sent(*tiny, pos)
    for slot, (src, dst) in enumerate(((tok, xs), (cot, ct))):
        for index in range(8):
            swap(src, dst, slot, index).wait_send()
    for copy in saves:
        copy.wait()


def forward_pass(weights, sm, tok, cot, lens):
    width = tok.shape[3]
    rows = 2 * tok.shape[2]
    low = jax.ShapeDtypeStruct((rows, width), BF16)
    full = jax.ShapeDtypeStruct((rows, width), F32)
    wide = jax.ShapeDtypeStruct((4, rows, width), BF16)
    six = (4, 2, 2, 2)
    vmem = pl.BlockSpec(memory_space=VMEM)
    hbm = pl.BlockSpec(memory_space=ANY)
    dma = pltpu.SemaphoreType.DMA
    return pl.pallas_call(
        forward_kernel,
        out_shape=(
            jax.ShapeDtypeStruct((4, 2) + six + (16, 768), BF16),
            jax.ShapeDtypeStruct((5, 2) + six + (16, width), BF16),
            jax.ShapeDtypeStruct((4, 2) + six + (64, 256), BF16),
            jax.ShapeDtypeStruct(six + (16, 128), BF16),
            low, wide, low, full, low, wide, wide, full, low, low,
            jax.ShapeDtypeStruct((16, width), F32),
            jax.ShapeDtypeStruct((8, width), F32),
        ),
        in_specs=[vmem] * 7 + [hbm] * 2 + [pl.BlockSpec(memory_space=pltpu.SMEM)],
        out_specs=[hbm] * 14 + [vmem] * 2,
        scratch_shapes=[
            VMEM((rows, width), BF16),
            VMEM((rows, width), BF16),
            VMEM((4, rows, width), BF16),
            VMEM((rows, width), BF16),
            VMEM((rows, width), F32),
            VMEM((rows, width), F32),
            VMEM((rows, width), BF16),
            VMEM((4, rows, width), BF16),
            VMEM((4, rows, width), BF16),
            VMEM((2,) + six + (2, 16, width), BF16),
            VMEM((2,) + six + (2, 64, 256), BF16),
            VMEM(six + (16, 128), BF16),
            VMEM((rows, width), BF16),
            VMEM((rows, 128), BF16),
            VMEM((rows, 128), F32),
            dma((27, SLOTS)),
            dma((27, SLOTS)),
            dma((43,)),
            dma((3,)),
            dma((2, 8)),
            dma((2, 8)),
            dma((2, 2)),
            dma((2, 2)),
            dma((19,)),
        ],
        compiler_params=pltpu.CompilerParams(collective_id=0, has_side_effects=True, vmem_limit_bytes=LIMIT),
        cost_estimate=pl.CostEstimate(flops=2 * 14 * rows * width * width, bytes_accessed=90 << 20, transcendentals=1 << 24),
        name="forward_pass",
    )(*weights, sm, tok, cot, lens)


CHUNKS = 26
WIDE = 18
DEPTH = 6
LAST = CHUNKS - 1


def ways(core, index):
    full = 1024 if index < WIDE else 768
    mode = 0 if core == 0 or index >= CHUNKS - 4 else 2 if index >= WIDE else 1
    return ((mode, 0, full),)


def scatter_copies(way, part, phase, grad, bufs, send, recv, pos):
    z, x, c, y = pos
    mode, start, size = way
    cols = pl.ds(start, size)
    b0, b1, b2, b3 = bufs
    every = slice(None)

    def remote(src, dst, slot, target):
        return pltpu.make_async_remote_copy(
            src_ref=src,
            dst_ref=dst,
            send_sem=send.at[6 * part + slot],
            recv_sem=recv.at[6 * part + slot],
            device_id=device(*target),
            device_id_type=MESH,
        )

    across = (z, 1 - x, c, y)
    beside = (z, x, c, 1 - y)
    if phase == 0:
        return [remote(grad.at[:, :, 1 - c, :, :, cols], b0.at[:, :, :, :, cols], 2, (z, x, 1 - c, y))]
    if phase == 1:
        if mode == 1:
            return [remote(b0.at[:, :, 1 - y, :, cols], b1.at[:, :, :, cols], 1, beside)]
        return [remote(b0.at[:, 1 - x, :, :, cols], b1.at[:, :, :, cols], 0, across)]
    if phase == 2:
        if mode == 0:
            return [
                remote(
                    b1.at[(z + d) % 4, :, :, cols],
                    b2.at[pl.ds(2 * (d - 1), 2), :, cols],
                    2 + d,
                    ((z + d) % 4, x, c, y),
                )
                for d in (1, 2, 3)
            ]
        if mode == 1:
            return [remote(b1.at[:, 1 - x, :, cols], b2.at[pl.ds(0, 4), :, cols], 0, across)]
        return [remote(b1.at[:, 1 - y, :, cols], b2.at[pl.ds(0, 4), :, cols], 1, beside)]
    if mode == 0:
        return [remote(b1.at[z, 1 - y, :, cols], b3.at[0, :, cols], 1, beside)]
    return [
        remote(b2.at[(z + d) % 4, :, cols], b3.at[d - 1, :, cols], 2 + d, ((z + d) % 4, x, c, y)) for d in (1, 2, 3)
    ]


def scatter_add(way, phase, own, bufs, out, pos):
    z, x, c, y = pos
    mode, start, size = way
    cols = pl.ds(start, size)
    b0, b1, b2, b3 = bufs

    def plus(a, b):
        return a + b

    def each(body):
        def run(zz, carry):
            body(zz)
            return carry

        lax.fori_loop(0, 4, run, 0)

    if phase == 0:

        def body(zz):
            b0[zz, :, :, :, cols] = plus(own[zz, :, :, :, cols], b0[zz, :, :, :, cols])

        each(body)
    elif phase == 1:

        def body(zz):
            kept = b0[zz, :, y, :, cols] if mode == 1 else b0[zz, x, :, :, cols]
            b1[zz, :, :, cols] = plus(kept, b1[zz, :, :, cols])

        each(body)
    elif mode == 0:
        if phase == 2:
            total = b1[z, :, :, cols].astype(F32)
            for d in range(3):
                total = total + b2[pl.ds(2 * d, 2), :, cols].astype(F32)
            b1[z, :, :, cols] = total.astype(BF16)
        else:
            out(b1[z, y, :, cols].astype(F32) + b3[0, :, cols].astype(F32))
    elif phase == 2:

        def body(zz):
            kept = b1[zz, x, :, cols] if mode == 1 else b1[zz, y, :, cols]
            b2[zz, :, cols] = plus(kept, b2[zz, :, cols])

        each(body)
    else:
        total = b2[z, :, cols].astype(F32)
        for d in range(3):
            total = total + b3[d, :, cols].astype(F32)
        out(total)


def scatter_phase(phase, plan, full, grad, own, own_sem, bufs, out, send, recv, credit, index, pos):
    z, x, c, y = pos
    cols = pl.ds(0, full)

    def mine():
        return pltpu.make_async_copy(grad.at[:, :, c, :, :, cols], own.at[:, :, :, :, cols], own_sem)

    if phase == 0:
        mine().start()
        if credit is not None:

            @pl.when(index >= DEPTH)
            def _():
                pl.semaphore_wait(credit, 1)

    if phase == 1:
        mine().wait()
    for core in (0, 1):

        @pl.when(c == core)
        def _():
            def copies(phase):
                return [
                    copy
                    for part, way in enumerate(plan[core] if phase > 0 else ((0, 0, full),))
                    for copy in scatter_copies(way, part, phase, grad, bufs, send, recv, pos)
                ]

            if phase > 0:
                for copy in copies(phase - 1):
                    copy.wait_recv()
                if phase == 2:
                    for copy in copies(1):
                        copy.wait_send()
                for way in plan[core]:
                    scatter_add(way, phase - 1, own, bufs, out, pos)
            if phase < PHASES:
                for copy in copies(phase):
                    copy.start()

    if phase == 2 and credit is not None:

        @pl.when(index < CHUNKS - DEPTH)
        def _():
            pl.semaphore_signal(credit, inc=1, device_id=device(z, x, 1 - c, y), device_id_type=MESH)


def scatter_sent(plan, full, grad, bufs, send, recv, pos):
    for core in (0, 1):

        @pl.when(pos[2] == core)
        def _():
            for phase in (0, 2, 3):
                for part, way in enumerate(plan[core] if phase > 0 else ((0, 0, full),)):
                    for copy in scatter_copies(way, part, phase, grad, bufs, send, recv, pos):
                        copy.wait_send()


SMALL = (((0, 0, 128),), ((1, 0, 128),))


def backward_kernel(
    wfq, wfa, wfd, xs_i, quad_i, aug_i, res_i, low_i, act_i, slope_i, back_i, gdn_i, out_i, vec, rows_in, lens,
    gw, act_o, gtok_o, gq_o, gk_o, gv_o, go_o, gup_o, gdown_o, small_out,
    acc, rbuf, gdn, low, quad, duo, wbuf, dbuf, stage, own, b0, b1, b2, b3, home, rows_sum, bias_sum,
    small_g, small_own, s0, s1, s2, s3, kaug,
    send, recv, own_sem, credit, swap_send, swap_recv, load_sem, wsem, dsem, stage_sem, out_sem,
):
    pos = place()
    z, x, c, y = pos
    rows, width = acc.shape
    half = rows // 2
    block = 256
    group = 256
    groups = width // group
    piece = half // 8

    def load(src, dst, slot):
        return pltpu.make_async_copy(src, dst, load_sem.at[slot])

    loads = [load(act_i.at[k], quad.at[k], k) for k in range(4)]
    loads += [load(gdn_i, gdn, 4), load(low_i, low, 5), load(back_i, acc, 6)]
    loads += [load(out_i.at[pl.ds(0, half)], duo.at[1, pl.ds(0, half)], 7), load(slope_i.at[0], duo.at[0], 8)]
    for k in (4, 0, 1, 2, 3, 5, 6, 7, 8):
        loads[k].start()
    greet(*pos)

    def away(index):
        at = pl.multiple_of(index * piece, piece)
        return pltpu.make_async_remote_copy(
            src_ref=out_i.at[pl.ds(half + at, piece)],
            dst_ref=act_o.at[y, 0, pl.ds(at, piece)],
            send_sem=swap_send.at[index],
            recv_sem=swap_recv.at[index],
            device_id=device(z, x, c, 1 - y),
            device_id_type=MESH,
        )

    kinds = ((0, WIDE, 1024), (WIDE, CHUNKS - 4, 768), (CHUNKS - 4, CHUNKS, 768))

    def chunk(index):
        slot = index % DEPTH
        bufs = (b0.at[slot], b1.at[index], b2.at[index], b3.at[index])
        return gw.at[index // 2, index % 2], bufs, send.at[index], recv.at[index]

    small_bufs = (s0, s1, s2, s3)

    def deliver(index, first):
        odd = index % 2
        row = pl.multiple_of(16 * odd, 16)

        def at(size, which):
            return pl.ds(pl.multiple_of(which * size, size), size)

        def wide(total):
            @pl.when(index < 8)
            def _():
                for q in range(4):
                    gdown_o[pl.ds(32 * q + row, 16), at(256, index // 2)] = total[:, 256 * q : 256 * (q + 1)]

            @pl.when((index >= 8) & (index < 16))
            def _():
                gup_o[pl.ds(row, 16), at(width, index // 2 - 4)] = total

            @pl.when(index >= 16)
            def _():
                go_o[pl.ds(row, 16), :] = total

        def trio_part(total):
            for k, dst in enumerate((gq_o, gk_o, gv_o)):
                dst[pl.ds(row, 16), at(group, (index - WIDE) // 2)] = total[:, group * k : group * (k + 1)]

        return wide if first == 0 else trio_part

    def deliver_small(total):
        small_out[...] = total


    def step(t, carry):
        for phase in range(PHASES + 1):
            index = t - LAG * phase
            for first, stop, full in kinds:

                @pl.when((index >= first) & (index < stop))
                def _():
                    grad, bufs, sends, recvs = chunk(index)
                    scatter_phase(
                        phase, (ways(0, first), ways(1, first)), full, grad, own.at[index % 3], own_sem.at[index % 3],
                        bufs, deliver(index, first), sends, recvs, credit, index, pos,
                    )

            @pl.when(index == LAST)
            def _():
                scatter_phase(
                    phase, SMALL, 128, small_g, small_own, own_sem.at[3], small_bufs, deliver_small,
                    send.at[CHUNKS], recv.at[CHUNKS], None, 0, pos,
                )

        @pl.when((t < 16) & (t % 2 == 0))
        def _():
            away(t // 2).start()

        return carry

    def advance(start, stop):
        lax.fori_loop(start, stop, step, 0)

    def weight(index, slot):
        return Halves(lambda h: pltpu.make_async_copy(wfa.at[index, h], wbuf.at[slot, :, :, :, :, h], wsem.at[slot, h]))

    def trio(g, slot):
        return Halves(
            lambda h: pltpu.make_async_copy(
                wfq.at[g, h], wbuf.at[slot, :, :, :, :, h, :, pl.ds(0, 3 * group)], wsem.at[slot, h]
            )
        )

    def shaft(j, slot):
        return Halves(
            lambda h: pltpu.make_async_copy(wfd.at[:, h, j], dbuf.at[slot, :, :, :, :, h], dsem.at[slot, h])
        )

    def store(index, slot):
        return Halves(
            lambda h: pltpu.make_async_copy(stage.at[slot, :, :, :, :, h], gw.at[index, h], stage_sem.at[slot, h])
        )

    weight(1, 0).start()
    shaft(0, 0).start()
    rows_sum[...] = rows_in[...]
    kaug[...] = key_lanes(within(lens, y, rows))
    bias_sum[...] = jnp.zeros_like(bias_sum)

    for k in (4, 0, 1, 2, 3):
        loads[k].wait()
    for jj in range(4):
        slot = jj % 2
        if jj >= 2:
            store(jj - 2, slot).wait()

        def quarter(k, carry):
            part = tn(quad[k], gdn[:, 256 * jj : 256 * (jj + 1)]).astype(BF16).reshape(2, 2, 2, 4, 2, 16, 256)
            for q in range(4):
                stage[slot, k, :, :, :, :, :, 256 * q : 256 * (q + 1)] = part[:, :, :, q]
            return carry

        lax.fori_loop(0, 4, quarter, 0)
        store(jj, slot).start()
        if jj >= 2:
            advance(jj - 2, jj - 1)
    loads[5].wait()
    loads[6].wait()
    loads[7].wait()
    keep = pltpu.make_async_copy(duo.at[1, pl.ds(0, half)], act_o.at[y, 0], out_sem.at[0])
    keep.start()
    for k in range(4):
        load(quad_i.at[k], quad.at[k], k).start()
    small_block = 128
    load(res_i.at[pl.ds(0, small_block)], rbuf.at[0], 9).start()

    def slope_load(j):
        return load(slope_i.at[j], duo.at[j % 2], 8 - j % 2)

    def square_rows(slot, n):
        return wbuf[slot, n].reshape(256, width)

    for j in range(4):
        slot = j % 2
        slope_load(j).wait()
        shaft(j, slot).wait()
        if j == 0:
            keep.wait()
        if j < 3:
            slope_load(j + 1).start()
            weight(2 + j, 1 - slot).start()
            shaft(j + 1, 1 - slot).start()
        for n in range(4):
            cols = slice(256 * n, 256 * (n + 1))
            total = nt(gdn[:, 0:256], dbuf[slot, 0, n // 2, n % 2].reshape(256, 256))
            for jj in range(1, 4):
                total = total + nt(
                    gdn[:, 256 * jj : 256 * (jj + 1)], dbuf[slot, jj, n // 2, n % 2].reshape(256, 256)
                )
            gu = (duo[slot, :, cols].astype(F32) * total).astype(BF16)
            duo[slot, :, cols] = gu
            bias_sum[8 * j : 8 * j + 1, cols] = rowsum(gu.astype(F32))
        store(2 + j, slot).wait()
        advance(2 + 2 * j, 3 + 2 * j)

        def up_grad(n, cols):
            part = tn(low[...], duo[slot, :, cols]).astype(BF16)
            stage[slot, :, :, :, :, :, :, cols] = part.reshape(4, 2, 2, 2, 2, 16, 256)

        tiles(width, 256, up_grad)
        store(4 + j, slot).start()
        advance(3 + 2 * j, 4 + 2 * j)
        weight(1 + j, slot).wait()
        for n in range(4):
            cols = slice(256 * n, 256 * (n + 1))
            acc[:, cols] += nt(duo[slot], square_rows(slot, n))
    weight(0, 0).start()
    load(xs_i, duo.at[0], 8).start()
    load(aug_i, duo.at[1], 7).start()

    def first_norm(b, carry):
        sl = pl.ds(pl.multiple_of(b * small_block, small_block), small_block)

        @pl.when(b + 1 < rows // small_block)
        def _():
            after = pl.ds(pl.multiple_of((b + 1) * small_block, small_block), small_block)
            load(res_i.at[after], rbuf.at[(b + 1) % 2], 9 + (b + 1) % 2).start()

        load(res_i.at[sl], rbuf.at[b % 2], 9 + b % 2).wait()
        normed, inverse = norm(rbuf[b % 2])
        g = acc[sl, :]
        back = norm_back(g, normed, inverse, vec[3:4, :])
        acc[sl, :] = back
        gat = back.astype(BF16)
        gdn[sl, :] = gat
        rows_sum[3:4, :] += rowsum(g * normed)
        rows_sum[4:5, :] += rowsum(g)
        rows_sum[2:3, :] += rowsum(gat.astype(F32))
        return carry

    lax.fori_loop(0, rows // small_block, first_norm, 0)
    store(6, 0).wait()
    advance(10, 11)
    for k in range(4):
        load(quad_i.at[k], quad.at[k], k).wait()

    for g in range(groups):
        for n in range(4):
            cols = slice(256 * n, 256 * (n + 1))
            part = tn(quad[g, :, 3 * group : 4 * group], gdn[:, cols]).astype(BF16)
            stage[0, g, :, :, :, :, :, cols] = part.reshape(2, 2, 2, 2, 16, 256)
    store(8, 0).start()
    weight(0, 0).wait()
    for n in range(4):
        low[:, 256 * n : 256 * (n + 1)] = nt(gdn[...], square_rows(0, n)).astype(BF16)
    store(7, 1).wait()
    advance(11, 12)
    trio(0, 0).start()
    load(xs_i, duo.at[0], 8).wait()
    load(aug_i, duo.at[1], 7).wait()
    store(8, 0).wait()

    xs, aug = duo.at[0], duo.at[1]
    low1 = (lanes((1, 128)) < 64).astype(F32).astype(BF16)
    high1 = (lanes((1, 128)) >= 64).astype(F32).astype(BF16)
    ones1 = (lanes((1, 128)) % 64 < 2).astype(F32).astype(BF16)
    alane = lanes((rows, 128))
    lower = alane < 64
    sixty = alane % 64

    def pair(g, n):
        local = pl.multiple_of(n * 128, 128)
        qc, kc, vc, cc = (pl.ds(local + group * k, 128) for k in range(4))
        cols = pl.ds(pl.multiple_of(g * group + n * 128, 128), 128)
        q2 = quad[g, :, qc]
        k2 = quad[g, :, kc]
        v2 = quad[g, :, vc]
        g2 = low[:, cols]
        au = aug[:, cols]
        prod = g2.astype(F32) * quad[g, :, cc].astype(F32)
        da = -jnp.sum(jnp.where(lower, prod, 0.0), axis=1, keepdims=True)
        db = -jnp.sum(jnp.where(lower, 0.0, prod), axis=1, keepdims=True)
        neg = jnp.where(lower, db, da)
        hi = neg.astype(BF16).astype(F32)
        daug = jnp.where(sixty == 0, hi, jnp.where(sixty == 1, neg - hi, 0.0)).astype(BF16)
        gq = []
        gk = []
        gv = []
        for head in range(2):
            mine, other = (low1, high1) if head == 0 else (high1, low1)
            qa = q2 * mine + au * other
            ga = g2 * mine + daug * other
            ka = k2 * mine + kaug[...] * other
            va = v2 * mine + ones1 * other
            parts = []
            for b in range(rows // block):
                sl = slice(b * block, (b + 1) * block)
                p = jnp.exp2(nt(ka, qa[sl]))
                ds = (p * nt(va, ga[sl])).astype(BF16)
                new_v = nn(p.astype(BF16), g2[sl])
                new_k = nn(ds, q2[sl])
                sum_v = new_v if b == 0 else sum_v + new_v
                sum_k = new_k if b == 0 else sum_k + new_k
                parts.append(tn(k2, ds))
            gq.append(parts)
            gk.append(sum_k)
            gv.append(sum_v)
        quad[g, :, kc] = (jnp.where(lower, gk[0], gk[1]) * (1.0 / LOG2E)).astype(BF16)
        quad[g, :, vc] = jnp.where(lower, gv[0], gv[1]).astype(BF16)
        for b in range(rows // block):
            sl = slice(b * block, (b + 1) * block)
            both = jnp.concatenate([gq[0][b][0:64], gq[1][b][64:128]], axis=0) * 0.125
            quad[g, sl, qc] = both.T.astype(BF16)

    def token_rows(g, slot, sl):
        for n in range(4):
            cols = slice(256 * n, 256 * (n + 1))
            acc[sl, cols] += nt(quad[g, sl, 0 : 3 * group], wbuf[slot, n, :, :, :, :, :, 0 : 3 * group].reshape(256, 3 * group))

    def trio_grad(g):
        at = pl.ds(pl.multiple_of(g * group, group), group)
        for k in range(3):
            part = tn(xs[...], quad[g, :, group * k : group * (k + 1)]).astype(BF16)
            stage[1, :, :, :, :, :, :, group * k : group * (k + 1)] = part.reshape(4, 2, 2, 2, 2, 16, group)
        rows_sum[0:1, at] = rowsum(quad[g, :, 0:group].astype(F32))
        rows_sum[1:2, at] = rowsum(quad[g, :, 2 * group : 3 * group].astype(F32))

    def attend(g, carry):
        def run(n, carry):
            @pl.when((g > 0) & (n == 1))
            def _():
                store(8 + g, 1).wait()

            @pl.when(g + n > 0)
            def _():
                advance(11 + 3 * g + n, 12 + 3 * g + n)

            pair(g, n)
            return carry

        lax.fori_loop(0, 2, run, 0)
        advance(13 + 3 * g, 14 + 3 * g)

        @pl.when(g < groups - 1)
        def _():
            trio(g, 0).wait()
            token_rows(g, 0, slice(0, rows))
            trio(g + 1, 0).start()

            trio_grad(g)
            store(9 + g, 1).start()

        return carry

    lax.fori_loop(0, groups, attend, 0)
    last = groups - 1

    advance(LAST - 2, LAST - 1)
    trio(last, 0).wait()
    token_rows(last, 0, slice(half, rows))
    low[0:half, :] = acc[half:rows, :].astype(BF16)
    turn = pltpu.make_async_remote_copy(
        src_ref=low.at[pl.ds(0, half)],
        dst_ref=home,
        send_sem=swap_send.at[8],
        recv_sem=swap_recv.at[8],
        device_id=device(z, x, c, 1 - y),
        device_id_type=MESH,
    )
    turn.start()
    trio_grad(last)
    store(9 + last, 1).start()
    for zz in range(4):
        for s in range(8):
            at = 2 * zz + s // 4
            tile = jnp.concatenate(
                [
                    rows_sum[:, 128 * at : 128 * (at + 1)],
                    bias_sum[8 * zz : 8 * zz + 8, 128 * s : 128 * (s + 1)],
                ],
                axis=0,
            )
            small_g[zz, s // 4, (s // 2) % 2, s % 2] = tile.astype(BF16)
    store(9 + last, 1).wait()
    advance(LAST - 1, LAST + 1)
    token_rows(last, 0, slice(0, half))
    kept = pltpu.make_async_copy(acc.at[pl.ds(0, half)], gtok_o.at[y, 0], out_sem.at[0])
    kept.start()
    advance(LAST + 1, LAST + LAG * PHASES + 1)
    turn.wait()
    acc[half:rows, :] = home[...].astype(F32)
    came = pltpu.make_async_copy(acc.at[pl.ds(half, half)], gtok_o.at[1 - y, 0], out_sem.at[1])
    came.start()
    for index in range(8):
        away(index).wait()

    def finish(index, carry):
        for first, stop, full in kinds:

            @pl.when((index >= first) & (index < stop))
            def _():
                grad, bufs, sends, recvs = chunk(index)
                scatter_sent((ways(0, first), ways(1, first)), full, grad, bufs, sends, recvs, pos)

        return carry

    lax.fori_loop(0, CHUNKS, finish, 0)
    scatter_sent(SMALL, 128, small_g, small_bufs, send.at[CHUNKS], recv.at[CHUNKS], pos)
    kept.wait()
    came.wait()


def backward_pass(wfq, wfa, wfd, saved, vec, rows_in, lens):
    rows, width = saved[0].shape
    six = (4, 2, 2, 2)
    vmem = pl.BlockSpec(memory_space=VMEM)
    hbm = pl.BlockSpec(memory_space=ANY)
    dma = pltpu.SemaphoreType.DMA

    def buffers(rows, width, depth, count):
        return [
            VMEM(depth + (4, 2, 2, rows, width), BF16),
            VMEM(count + (4, 2, rows, width), BF16),
            VMEM(count + (6, rows, width), BF16),
            VMEM(count + (3, rows, width), BF16),
        ]

    return pl.pallas_call(
        backward_kernel,
        out_shape=(
            jax.ShapeDtypeStruct((CHUNKS // 2, 2) + six + (16, width), BF16),
            jax.ShapeDtypeStruct((2, 1, rows // 2, width), BF16),
            jax.ShapeDtypeStruct((2, 1, rows // 2, width), F32),
            jax.ShapeDtypeStruct((32, width), F32),
            jax.ShapeDtypeStruct((32, width), F32),
            jax.ShapeDtypeStruct((32, width), F32),
            jax.ShapeDtypeStruct((32, width), F32),
            jax.ShapeDtypeStruct((32, 4 * width), F32),
            jax.ShapeDtypeStruct((128, width), F32),
            jax.ShapeDtypeStruct((16, 128), F32),
        ),
        in_specs=[hbm] * 13 + [vmem] * 2 + [pl.BlockSpec(memory_space=pltpu.SMEM)],
        out_specs=[hbm] * 3 + [vmem] * 7,
        scratch_shapes=[
            VMEM((rows, width), F32),
            VMEM((2, 128, width), F32),
            VMEM((rows, width), BF16),
            VMEM((rows, width), BF16),
            VMEM((4, rows, width), BF16),
            VMEM((2, rows, width), BF16),
            VMEM((2,) + six + (2, 16, width), BF16),
            VMEM((2, 4, 2, 2, 2, 2, 64, 256), BF16),
            VMEM((2,) + six + (2, 16, width), BF16),
            VMEM((3, 4, 2, 2, 16, width), BF16),
        ]
        + buffers(16, width, (DEPTH,), (CHUNKS,))
        + [
            VMEM((rows // 2, width), BF16),
            VMEM((8, width), F32),
            VMEM((32, width), F32),
            VMEM(six + (16, 128), BF16),
            VMEM((4, 2, 2, 16, 128), BF16),
        ]
        + buffers(16, 128, (), ())
        + [
            VMEM((rows, 128), BF16),
            dma((CHUNKS + 1, SLOTS)),
            dma((CHUNKS + 1, SLOTS)),
            dma((4,)),
            pltpu.SemaphoreType.REGULAR,
            dma((9,)),
            dma((9,)),
            dma((11,)),
            dma((2, 2)),
            dma((2, 2)),
            dma((2, 2)),
            dma((2,)),
        ],
        compiler_params=pltpu.CompilerParams(collective_id=1, has_side_effects=True, vmem_limit_bytes=61 * 1024 * 1024),
        cost_estimate=pl.CostEstimate(flops=2 * 32 * rows * width * width, bytes_accessed=90 << 20, transcendentals=1 << 24),
        name="backward_pass",
    )(wfq, wfa, wfd, *saved, vec, rows_in, lens)


def paired(
    tokens, lengths, w_query, w_key, w_value, w_out, w_up, w_down, vectors, up_bias, cotangent
):
    y = lax.axis_index("seq")
    rank = lax.axis_index("dp") * 2 + y
    spot = jnp.tile(vectors, (1, 4)) * (jnp.arange(128) // 32 == rank % 4).astype(BF16)
    sm = jnp.concatenate([spot, up_bias[None, :], jnp.zeros((7, 128), BF16)])
    weights = (w_query, w_key, w_value, w_out, w_up, w_down)
    wfq, wfa, wfd, _, *saved, vec, rows_in = forward_pass(weights, sm, tokens, cotangent, lengths)
    _, activations, grad_tokens, *grads, small = backward_pass(wfq, wfa, wfd, saved, vec, rows_in, lengths)
    return (
        activations,
        grad_tokens,
        *grads,
        lax.dynamic_slice_in_dim(small[0:8], (rank % 4) * 32, 32, axis=1),
        small[8],
    )


def solution(mesh):
    placed = (
        P(None, "dp", "seq", None),
        P(None, "dp"),
        P(("dp", "seq"), None),
        P(("dp", "seq"), None),
        P(("dp", "seq"), None),
        P(("dp", "seq"), None),
        P(("dp", "seq"), None),
        P(("dp", "seq"), None),
        P(None, ("dp", "seq")),
        P(("dp", "seq")),
        P(None, "dp", "seq", None),
    )
    own = mesh.shape["dp"] == 16 and mesh.shape["seq"] == 2
    return jax.shard_map(
        paired if own else per_device,
        mesh=mesh,
        in_specs=placed,
        out_specs=(
            P(None, "dp", "seq", None),
            P(None, "dp", "seq", None),
            P(("dp", "seq"), None),
            P(("dp", "seq"), None),
            P(("dp", "seq"), None),
            P(("dp", "seq"), None),
            P(("dp", "seq"), None),
            P(("dp", "seq"), None),
            P(None, ("dp", "seq")),
            P(("dp", "seq")),
        ),
        check_vma=False,
    )
```
